128 devices in a mesh: dp: 4 (over y), seq: 32 (over x, z, core).
Axes of the slice: x: 4, y: 4, z: 4, core: 2. Of those that a mesh axis runs over, the one named last changes fastest.
Arguments:
- tokens: bfloat16 [4, 8192, 576], P('dp', 'seq'), may hold values from -6 to 6
- segments: int32 [4, 8192], P('dp', 'seq'), may hold values from 0 to 2, as said below
- positions: int32 [4, 8192], P('dp', 'seq'), may hold values from 0 to 8189, as said below
- norm_gain: float32 [576], replicated, may hold values from 0.5 to 1.5
- query_weight: bfloat16 [576, 576], replicated, may hold values from -0.25 to 0.25
- key_weight: bfloat16 [576, 192], replicated, may hold values from -0.25 to 0.25
- value_weight: bfloat16 [576, 192], replicated, may hold values from -0.25 to 0.25
- output_weight: bfloat16 [576, 576], replicated, may hold values from -4 to 4
- mlp_gain: float32 [576], replicated, may hold values from 0.5 to 1.5
- gate_weight: bfloat16 [576, 1536], replicated, may hold values from -0.25 to 0.25
- up_weight: bfloat16 [576, 1536], replicated, may hold values from -0.25 to 0.25
- down_weight: bfloat16 [1536, 576], replicated, may hold values from -0.15625 to 0.15625
- cotangent: bfloat16 [4, 8192, 576], P('dp', 'seq'), may hold values from -6 to 6
Outputs:
- layer_output: bfloat16 [4, 8192, 576], P('dp', 'seq')
- input_grad: bfloat16 [4, 8192, 576], P('dp', 'seq')
- grad_norm_gain: float32 [576], replicated
- grad_query_weight: float32 [576, 576], replicated
- grad_key_weight: float32 [576, 192], replicated
- grad_value_weight: float32 [576, 192], replicated
- grad_output_weight: float32 [576, 576], replicated
- grad_mlp_gain: float32 [576], replicated
- grad_gate_weight: float32 [576, 1536], replicated
- grad_up_weight: float32 [576, 1536], replicated
- grad_down_weight: float32 [1536, 576], replicated
The draws below stay inside these ranges and needn't reach their ends.
Inputs may be any that keep to these rules, and one draw needn't show every extreme that they name: `segments`: in each row segment 0 is a fragment within the first 256 tokens, segment 1 a document from there to within the last 256 tokens, segment 2 the rest; ids never fall. Within a segment positions rise by one from token to token; in every row segment 1 ends at position 8189, the other segments start at an offset below 1024.
All inputs are finite; a program needn't handle non-finite values.
Results may differ from the reference program's by a relative error of at most 0.019.
Values may be sent and summed in bfloat16 or wider, within the bound.
No kernel may reach another device: no remote copies, remote signals or barrier semaphores. Data moves between devices by JAX's collectives and lax.ppermute only.
A program may use at most 128 MiB of HBM per device.

```python
import jax
import jax.numpy as jnp
from jax import lax

D = 576
H = 9
KVH = 3
HD = 64
FF = 1536
TOK_DEV = 256
SEQLEN = 8192
ROWS = 4


def packed_layout(key):
    first_len = jax.random.randint(jax.random.fold_in(key, 11), (ROWS, 1), 1, TOK_DEV)
    last_len = jax.random.randint(jax.random.fold_in(key, 12), (ROWS, 1), 1, TOK_DEV)
    offsets = jax.random.randint(jax.random.fold_in(key, 13), (ROWS, 2), 0, min(1024, SEQLEN - TOK_DEV))
    places = jnp.arange(SEQLEN, dtype=jnp.int32)[None, :]
    segment_ids = (places >= first_len).astype(jnp.int32) + (places >= SEQLEN - last_len).astype(jnp.int32)
    seg_begin = jnp.where(segment_ids == 0, 0, jnp.where(segment_ids == 1, first_len, SEQLEN - last_len))
    middle_start = first_len + last_len - 2
    seg_shift = jnp.where(segment_ids == 0, offsets[:, :1], jnp.where(segment_ids == 1, middle_start, offsets[:, 1:]))
    return (segment_ids, places - seg_begin + seg_shift)


def draw_segments(key, part):
    layout = packed_layout(key)
    return layout[0]


def draw_positions(key, part):
    layout = packed_layout(key)
    return layout[1]


def steps_of(rng, dims, cuts, low, largest):
    level = 1.0
    for position, blocks in cuts:
        heights = jax.random.uniform(jax.random.fold_in(jax.random.fold_in(rng, 6), position), (blocks,), jnp.float32, low / len(cuts), largest / len(cuts))
        level = level * jnp.repeat(jnp.exp(heights), dims[position] // blocks).reshape((-1,) + (1,) * (len(dims) - 1 - position))
    return level


def scatter_about(own_key, extent, width, most, pieces=(), kind=jnp.bfloat16):
    entries = width * jax.random.normal(own_key, extent, jnp.float32)
    if pieces:
        entries = entries * steps_of(own_key, extent, pieces, -0.22, 0.18)
    return jnp.clip(entries, -most, most).astype(kind)


def setup_inputs(seed: int = 0) -> dict:
    seeds = jax.random.split(jax.random.key(seed), 14)
    return {
        "tokens": scatter_about(seeds[0], (ROWS, SEQLEN, D), 1.0, 6.0, ((0, 4), (1, 32))),
        "segments": draw_segments(jax.random.fold_in(seeds[13], 71), 0),
        "positions": draw_positions(jax.random.fold_in(seeds[13], 71), 0),
        "norm_gain": jnp.clip(1.0 + 0.1 * jax.random.normal(seeds[3], (D,), jnp.float32), 0.5, 1.5),
        "query_weight": scatter_about(seeds[4], (D, D), D ** -0.5, 0.25),
        "key_weight": scatter_about(seeds[5], (D, KVH * HD), D ** -0.5, 0.25),
        "value_weight": scatter_about(seeds[6], (D, KVH * HD), D ** -0.5, 0.25),
        "output_weight": scatter_about(seeds[7], (D, D), (max(1, D // 256)) ** -0.5, 4.0),
        "mlp_gain": jnp.clip(1.0 + 0.1 * jax.random.normal(seeds[8], (D,), jnp.float32), 0.5, 1.5),
        "gate_weight": scatter_about(seeds[9], (D, FF), D ** -0.5, 0.25),
        "up_weight": scatter_about(seeds[10], (D, FF), D ** -0.5, 0.25),
        "down_weight": scatter_about(seeds[11], (FF, D), FF ** -0.5, 0.15625),
        "cotangent": scatter_about(seeds[12], (ROWS, SEQLEN, D), 1.0, 6.0, ((0, 4), (1, 32))),
    }


EPSILON = 1e-05
ROPE_BASE = 10000.0
NEGATIVE = -1000000000.0
HIGHEST = lax.Precision.HIGHEST

@jax.custom_vjp
def low(v):
    return lax.optimization_barrier(v.astype(jnp.bfloat16)).astype(jnp.float32)

@jax.custom_vjp
def low_back(v):
    return v

def low_keep(v):
    return (low(v), None)

def low_pass(kept, grad):
    return (grad,)

def back_keep(v):
    return (v, None)

def back_low(kept, grad):
    return (low(grad),)
low.defvjp(low_keep, low_pass)
low_back.defvjp(back_keep, back_low)

def two_sided(values):
    return low_back(low(values))

def product(left, right):
    return jnp.dot(left, right, precision=HIGHEST)

def normed(values, gain):
    return values * lax.rsqrt(lax.optimization_barrier(jnp.mean(values * values, axis=-1, keepdims=True)) + EPSILON) * gain

def rotate(values, places):
    half_dim = values.shape[-1] // 2
    freqs = ROPE_BASE ** (-2.0 * jnp.arange(half_dim).astype(jnp.float32) / values.shape[-1])
    angles = places.astype(jnp.float32)[:, None] * freqs[None, :]
    cosine = jnp.cos(angles)[:, None, :]
    sine = jnp.sin(angles)[:, None, :]
    first_half = values[..., :half_dim]
    second_half = values[..., half_dim:]
    return jnp.concatenate([first_half * cosine - second_half * sine, second_half * cosine + first_half * sine], axis=-1)

def row_forward(row_input, row_segs, row_places, weights):
    norm_gain, query_weight, key_weight, value_weight, output_weight, mlp_gain, gate_weight, up_weight, down_weight = weights
    length = row_input.shape[0]
    activation = low(normed(row_input, norm_gain))
    queries = low(rotate(low_back(product(activation, query_weight).reshape(length, H, HD)), row_places))
    key_rows = low(rotate(low_back(product(activation, key_weight).reshape(length, KVH, HD)), row_places))
    value_rows = two_sided(product(activation, value_weight).reshape(length, KVH, HD))
    block_rows = min(512, length)
    query_blocks = queries.reshape(length // block_rows, block_rows, KVH, H // KVH, HD)
    all_rows = jnp.arange(length, dtype=jnp.int32)
    block_starts = jnp.arange(length // block_rows, dtype=jnp.int32) * block_rows

    def attend(block_data):
        query_block, first_row = block_data
        query_rows = first_row + jnp.arange(block_rows, dtype=jnp.int32)
        query_segs = lax.dynamic_slice_in_dim(row_segs, first_row.astype(jnp.int32), block_rows)
        scores = low_back(jnp.einsum('qkgd,skd->kgqs', query_block, key_rows, precision=HIGHEST) * HD ** (-0.5))
        allowed = (all_rows[None, :] <= query_rows[:, None]) & (row_segs[None, :] == query_segs[:, None])
        scores = jnp.where(allowed[None, None], scores, NEGATIVE)
        run_max = lax.optimization_barrier(jnp.max(scores, axis=-1, keepdims=True))
        weights_exp = jnp.exp(scores - run_max)
        prob_block = weights_exp / lax.optimization_barrier(jnp.sum(weights_exp, axis=-1, keepdims=True))
        return jnp.einsum('kgqs,skd->qkgd', low(prob_block), value_rows, precision=HIGHEST)
    attended = lax.map(jax.checkpoint(attend), (query_blocks, block_starts)).reshape(length, D)
    middle = row_input + low_back(product(two_sided(attended), output_weight))
    activation_two = low(normed(middle, mlp_gain))
    gate_value = low_back(product(activation_two, gate_weight))
    up_value = low_back(product(activation_two, up_weight))
    hidden = low(jax.nn.silu(gate_value) * up_value)
    return middle + low_back(product(hidden, down_weight))

def reference(tokens, segments, positions, norm_gain, query_weight, key_weight, value_weight, output_weight, mlp_gain, gate_weight, up_weight, down_weight, cotangent):
    inputs = tokens.astype(jnp.float32)
    params = (norm_gain.astype(jnp.float32), query_weight.astype(jnp.float32), key_weight.astype(jnp.float32), value_weight.astype(jnp.float32), output_weight.astype(jnp.float32), mlp_gain.astype(jnp.float32), gate_weight.astype(jnp.float32), up_weight.astype(jnp.float32), down_weight.astype(jnp.float32))

    def forward(block_input, *weights):

        def per_row(unused, row_data):
            return (unused, row_forward(row_data[0], row_data[1], row_data[2], weights))
        carried, outputs = lax.scan(per_row, jnp.zeros((), jnp.float32), (block_input, segments, positions))
        return outputs
    result, pullback = jax.vjp(forward, inputs, *params)
    gradients = pullback(cotangent.astype(jnp.float32))
    return (result.astype(jnp.bfloat16), gradients[0].astype(jnp.bfloat16), gradients[1], gradients[2], gradients[3], gradients[4], gradients[5], gradients[6], gradients[7], gradients[8], gradients[9])
```

```python
from functools import partial

import jax
import jax.numpy as jnp
from jax import lax
from jax.experimental import pallas as pl
from jax.experimental.pallas import tpu as pltpu
from jax.sharding import Mesh
from jax.sharding import PartitionSpec as P

D = 576
H = 9
KVH = 3
GROUP = H // KVH
HD = 64
FF = 1536
EPSILON = 1e-05
ROPE_BASE = 10000.0
LOG2E = 1.4426950408889634
MASKED = -1e30

TOK = 256
CHUNK = TOK // 2
UNITS = 32
COLS = GROUP * CHUNK
PADROWS = TOK + 16

SEQ = ("x", "z", "core")
ALL = ("dp", "x", "z", "core")
BF = jnp.bfloat16
F32 = jnp.float32
VMEM_LIMIT = 56 * 1024 * 1024

NT = (((1,), (1,)), ((), ()))
NN = (((1,), (0,)), ((), ()))
TN = (((0,), (0,)), ((), ()))


def mm(left, right, dims=NN):
    return lax.dot_general(left, right, dims, preferred_element_type=F32)


def column_info(scalars, marks_ref, kv_ref):
    lo_idx = scalars[0]
    first_len = kv_ref[0, TOK : TOK + 16, 0:128].astype(F32)[0:1, :].astype(jnp.int32)
    first_len = jnp.concatenate([first_len] * (2 * GROUP), axis=1)
    marks = jnp.concatenate([marks_ref[1 - lo_idx, 0:1, :], marks_ref[lo_idx, 0:1, :]], axis=1)
    first_key = jnp.where(marks < 0, first_len, marks)
    lane = lax.broadcasted_iota(jnp.int32, (1, 2 * COLS), 1)
    start = jnp.where(lane < COLS, scalars[2], scalars[1]) * CHUNK
    return first_key, start + lax.rem(lane, CHUNK)


def full_mask(tile, first_key, place, cols):
    keys = tile * TOK + lax.broadcasted_iota(jnp.int32, (TOK, cols), 0)
    return (keys >= first_key[:, :cols]) & (keys <= place[:, :cols])


def tiles(scalars, step):
    lo_diag = scalars[1] // 2
    hi_diag = scalars[2] // 2
    step(0, 2 * COLS, True)

    @pl.loop(1, lo_diag)
    def _(t):
        step(t, 2 * COLS, False)

    @pl.when(lo_diag > 0)
    def _():
        step(lo_diag, 2 * COLS, True)

    @pl.loop(lo_diag + 1, hi_diag)
    def _(t):
        step(t, COLS, False)

    step(hi_diag, COLS, True)


def untranspose(columns, heads_ref, out_ref, scalars):
    for part in range(2):
        index = (1 - scalars[0]) if part == 0 else scalars[0]
        for pair in range(0, H, 2):
            rows = []
            for head in range(pair, min(pair + 2, H)):
                g, j = head // GROUP, head % GROUP
                at = part * COLS + j * CHUNK
                rows.append(heads_ref[g, :, at : at + CHUNK])
            block = jnp.concatenate(rows, axis=0) if len(rows) > 1 else rows[0]
            block = jnp.transpose(block).astype(out_ref.dtype)
            out_ref[index, :, pair * HD : pair * HD + block.shape[1]] = block


def forward_kernel(scalars, marks_ref, q_ref, kv_ref, out_ref, ot_ref, lse_ref, qcat, acc, run_max, heads):
    first_key, place = column_info(scalars, marks_ref, kv_ref)
    lo_idx = scalars[0]
    qcat[:, 0:COLS, :] = q_ref[1 - lo_idx]
    qcat[:, COLS:, :] = q_ref[lo_idx]

    @pl.loop(0, KVH)
    def _(g):
        lanes = pl.ds(pl.multiple_of(g * 128, 128), 128)
        acc[...] = jnp.zeros_like(acc)
        run_max[...] = jnp.full_like(run_max, MASKED)

        def step(tile, cols, whole):
            block = kv_ref[tile, 0:TOK, lanes]
            scores = mm(block, qcat[g, 0:cols, :], NT) * LOG2E
            old_max = run_max[0:1, 0:cols]
            if whole:
                scores = jnp.where(full_mask(tile, first_key, place, cols), scores, MASKED)
                new_max = jnp.maximum(old_max, jnp.max(scores, axis=0, keepdims=True))
                shift = new_max
            else:
                seen = first_key[:, :cols] <= tile * TOK
                new_max = jnp.maximum(old_max, jnp.max(scores, axis=0, keepdims=True))
                new_max = jnp.where(seen, new_max, old_max)
                shift = jnp.where(seen, new_max, -MASKED)
            weights = jnp.exp2(scores - shift).astype(BF)
            factor = jnp.exp2(old_max - new_max)
            values = jnp.concatenate([jnp.ones((16, TOK), BF), jnp.transpose(block)[HD:, :]], axis=0)
            acc[:, 0:cols] = acc[:, 0:cols] * factor + mm(values, weights)
            run_max[0:1, 0:cols] = new_max

        tiles(scalars, step)
        total = acc[0:1, :]
        heads[g] = acc[16:, :] / total
        norm = run_max[0:1, :] + jnp.log2(total)
        for part in range(2):
            index = (1 - lo_idx) if part == 0 else lo_idx
            span = slice(part * COLS, (part + 1) * COLS)
            ot_ref[index, g] = heads[g, :, span]
            lse_ref[index, g] = jnp.broadcast_to(norm[:, span], (8, COLS))

    untranspose(None, heads, out_ref, scalars)


def backward_kernel(
    scalars, marks_ref, q_ref, do_ref, ot_ref, lse_ref, kv_ref, dq_ref, dkv_ref, qcat, docat, heads, norm, delta
):
    first_key, place = column_info(scalars, marks_ref, kv_ref)
    lo_idx = scalars[0]
    qcat[:, 0:COLS, :] = q_ref[1 - lo_idx]
    qcat[:, COLS:, :] = q_ref[lo_idx]
    docat[:, 0:COLS, :] = do_ref[1 - lo_idx]
    docat[:, COLS:, :] = do_ref[lo_idx]
    hi_diag = scalars[2] // 2

    @pl.loop(0, KVH)
    def _(g):
        lanes = pl.ds(pl.multiple_of(g * 128, 128), 128)
        heads[g] = jnp.zeros((HD, 2 * COLS), F32)
        for part in range(2):
            index = (1 - lo_idx) if part == 0 else lo_idx
            span = slice(part * COLS, (part + 1) * COLS)
            grads = jnp.transpose(docat[g, span, :])[HD:, :].astype(F32)
            delta[0:1, span] = jnp.sum(grads * ot_ref[index, g], axis=0, keepdims=True)
            norm[0:1, span] = lse_ref[index, g, 0:1, :]

        def step(tile, cols, whole):
            block = kv_ref[tile, 0:TOK, lanes]
            q_part = qcat[g, 0:cols, :]
            do_part = docat[g, 0:cols, :]
            scores = mm(block, q_part, NT) * LOG2E
            if whole:
                scores = jnp.where(full_mask(tile, first_key, place, cols), scores, MASKED)
                shift = norm[0:1, 0:cols]
            else:
                shift = jnp.where(first_key[:, :cols] <= tile * TOK, norm[0:1, 0:cols], -MASKED)
            probs = jnp.exp2(scores - shift)
            grad_probs = mm(block, do_part, NT)
            grad_scores = (probs * (grad_probs - delta[0:1, 0:cols])).astype(BF)
            grads = mm(grad_scores, q_part) + mm(probs.astype(BF), do_part)
            keys = jnp.transpose(block)[0:HD, :]
            heads[g, :, 0:cols] = heads[g, :, 0:cols] + mm(keys, grad_scores)
            grads = grads.astype(BF)
            dkv_ref[tile, 0:CHUNK, lanes] = grads[0:CHUNK]
            dkv_ref[UNITS - 1 - tile, CHUNK:, lanes] = grads[CHUNK:]

        tiles(scalars, step)

        @pl.loop(hi_diag + 1, UNITS)
        def _(t):
            zero = jnp.zeros((CHUNK, 128), BF)
            dkv_ref[t, 0:CHUNK, lanes] = zero
            dkv_ref[UNITS - 1 - t, CHUNK:, lanes] = zero

        heads[g] = heads[g] * (HD**-0.5)

    untranspose(None, heads, dq_ref, scalars)


def vmem(count):
    return [pl.BlockSpec(memory_space=pltpu.VMEM)] * count


def attend(scalars, marks, queries, keys_values):
    return pl.pallas_call(
        forward_kernel,
        out_shape=(
            jax.ShapeDtypeStruct((2, CHUNK, D), BF),
            jax.ShapeDtypeStruct((2, KVH, HD, COLS), F32),
            jax.ShapeDtypeStruct((2, KVH, 8, COLS), F32),
        ),
        in_specs=[pl.BlockSpec(memory_space=pltpu.SMEM)] + vmem(3),
        out_specs=tuple(vmem(3)),
        scratch_shapes=[
            pltpu.VMEM((KVH, 2 * COLS, 128), BF),
            pltpu.VMEM((16 + HD, 2 * COLS), F32),
            pltpu.VMEM((8, 2 * COLS), F32),
            pltpu.VMEM((KVH, HD, 2 * COLS), F32),
        ],
        compiler_params=pltpu.CompilerParams(vmem_limit_bytes=VMEM_LIMIT),
        cost_estimate=pl.CostEstimate(flops=10 * 10**9, bytes_accessed=7 * 10**6, transcendentals=10**7),
        name="attention_forward",
    )(scalars, marks, queries, keys_values)


def attend_back(scalars, marks, queries, grad_out, attended, norm, keys_values):
    return pl.pallas_call(
        backward_kernel,
        out_shape=(
            jax.ShapeDtypeStruct((2, CHUNK, D), F32),
            jax.ShapeDtypeStruct((UNITS, TOK, 2 * KVH * HD), BF),
        ),
        in_specs=[pl.BlockSpec(memory_space=pltpu.SMEM)] + vmem(6),
        out_specs=tuple(vmem(2)),
        scratch_shapes=[
            pltpu.VMEM((KVH, 2 * COLS, 128), BF),
            pltpu.VMEM((KVH, 2 * COLS, 128), BF),
            pltpu.VMEM((KVH, HD, 2 * COLS), F32),
            pltpu.VMEM((8, 2 * COLS), F32),
            pltpu.VMEM((8, 2 * COLS), F32),
        ],
        compiler_params=pltpu.CompilerParams(vmem_limit_bytes=VMEM_LIMIT),
        cost_estimate=pl.CostEstimate(flops=25 * 10**9, bytes_accessed=14 * 10**6, transcendentals=10**7),
        name="attention_backward",
    )(scalars, marks, queries, grad_out, attended, norm, keys_values)


def mirror(values):
    return lax.ppermute(values, SEQ, [(i, UNITS - 1 - i) for i in range(UNITS)])


def zigzag(values):
    return jnp.concatenate([values[:CHUNK], mirror(values[CHUNK:])], axis=0)


def turns(places):
    half = HD // 2
    freqs = ROPE_BASE ** (-2.0 * jnp.arange(half).astype(F32) / HD)
    angles = places.astype(F32)[:, None] * freqs[None, :]
    return jnp.cos(angles)[:, None, :], jnp.sin(angles)[:, None, :]


def rotate(values, turn, sign=1.0):
    cosine, sine = turn
    sine = sine * sign
    half = HD // 2
    first, second = values[..., :half], values[..., half:]
    return jnp.concatenate([first * cosine - second * sine, second * cosine + first * sine], axis=-1)


def normed(values, gain):
    return values * lax.rsqrt(jnp.mean(values * values, axis=-1, keepdims=True) + EPSILON) * gain


def swiglu(gate_value, up_value):
    return jax.nn.silu(gate_value) * up_value


def pad_heads(values, left):
    heads = values.reshape(2, CHUNK, KVH, GROUP, HD).transpose(0, 2, 3, 1, 4).reshape(2, KVH, COLS, HD)
    return jnp.pad(heads, ((0, 0), (0, 0), (0, 0), (HD, 0) if left else (0, HD)))


def body(
    tokens,
    segments,
    positions,
    norm_gain,
    query_weight,
    key_weight,
    value_weight,
    output_weight,
    mlp_gain,
    gate_weight,
    up_weight,
    down_weight,
    cotangent,
):
    unit = (lax.axis_index("x") * 4 + lax.axis_index("z")) * 2 + lax.axis_index("core")
    tokens = tokens[0]
    segments = segments[0]
    positions = positions[0]

    own = tokens.astype(F32)
    own_act = normed(own, norm_gain).astype(BF)
    own_turn = turns(positions)
    keys = rotate(mm(own_act, key_weight).reshape(TOK, KVH, HD), own_turn).astype(BF)
    values = mm(own_act, value_weight).astype(BF).reshape(TOK, KVH, HD)
    packed = jnp.concatenate([keys, values], axis=-1).reshape(TOK, 2 * KVH * HD)
    first_len = jnp.sum((segments == 0).astype(F32))
    extra = jnp.broadcast_to(first_len.astype(BF), (16, 2 * KVH * HD))
    packed = jnp.concatenate([packed, extra], axis=0)
    gathered = lax.all_gather(packed, SEQ, axis=0, tiled=False)

    third = TOK * unit + jnp.sum((segments < 2).astype(jnp.int32))
    marks = jnp.where(segments == 2, third, jnp.where(segments == 1, -1, 0))
    ints = jnp.stack([marks, positions], axis=1)
    ints = zigzag(ints)
    marks, places = ints[:, 0], ints[:, 1]
    marks = jnp.broadcast_to(jnp.tile(marks.reshape(2, 1, CHUNK), (1, 1, GROUP)), (2, 8, COLS))
    both = zigzag(jnp.concatenate([tokens, cotangent[0]], axis=1))
    inputs = both[:, :D].astype(F32)
    out_low = both[:, D:]
    chunk_a, chunk_b = 2 * unit, 2 * UNITS - 1 - 2 * unit
    lo_idx = (chunk_a > chunk_b).astype(jnp.int32)
    scalars = jnp.stack([lo_idx, jnp.minimum(chunk_a, chunk_b), jnp.maximum(chunk_a, chunk_b), 0])

    first_norm, norm_pull = jax.vjp(normed, inputs, norm_gain)
    activation = first_norm.astype(BF)
    turn = turns(places)
    queries = rotate(mm(activation, query_weight).reshape(TOK, H, HD), turn).astype(BF)
    queries = pad_heads((queries * jnp.asarray(HD**-0.5, BF)).reshape(TOK, D), False)

    attn_low, attended, norm = attend(scalars, marks, queries, gathered)
    attn_low = attn_low.reshape(TOK, D)

    middle = inputs + mm(attn_low, output_weight)
    second_norm, mlp_pull = jax.vjp(normed, middle, mlp_gain)
    activation_two = second_norm.astype(BF)
    gate_value = mm(activation_two, gate_weight)
    up_value = mm(activation_two, up_weight)
    hidden_full, swiglu_pull = jax.vjp(swiglu, gate_value, up_value)
    hidden = hidden_full.astype(BF)
    result = (middle + mm(hidden, down_weight)).astype(BF)
    grad_down = mm(hidden, out_low, TN)
    grad_hidden = mm(out_low, down_weight, NT)
    grad_gate, grad_up = swiglu_pull(grad_hidden)
    gate_low = grad_gate.astype(BF)
    up_low = grad_up.astype(BF)
    grad_gate_weight = mm(activation_two, gate_low, TN)
    grad_up_weight = mm(activation_two, up_low, TN)
    grad_act_two = mm(gate_low, gate_weight, NT) + mm(up_low, up_weight, NT)
    grad_middle_norm, grad_mlp_gain = mlp_pull(grad_act_two)
    grad_middle = out_low.astype(F32) + grad_middle_norm
    middle_low = grad_middle.astype(BF)
    grad_output_weight = mm(attn_low, middle_low, TN)
    grad_attn = pad_heads(mm(middle_low, output_weight, NT).astype(BF), True)

    early = lax.psum(
        tuple(v.astype(BF) for v in (grad_output_weight, grad_gate_weight, grad_up_weight, grad_down)), ALL
    )

    grad_query, key_terms = attend_back(scalars, marks, queries, grad_attn, attended, norm, gathered)
    shares = lax.psum_scatter(key_terms, SEQ, scatter_dimension=0, tiled=False)
    shares = shares.astype(F32).reshape(TOK, KVH, 2 * HD)
    key_low = rotate(shares[..., :HD], turn, -1.0).reshape(TOK, KVH * HD).astype(BF)
    value_low = shares[..., HD:].reshape(TOK, KVH * HD).astype(BF)
    query_low = rotate(grad_query.reshape(TOK, H, HD), turn, -1.0).reshape(TOK, D).astype(BF)
    grad_query_weight = mm(activation, query_low, TN)
    grad_key_weight = mm(activation, key_low, TN)
    grad_value_weight = mm(activation, value_low, TN)
    grad_activation = (
        mm(query_low, query_weight, NT) + mm(key_low, key_weight, NT) + mm(value_low, value_weight, NT)
    )
    grad_input_norm, grad_norm_gain = norm_pull(grad_activation)
    grad_input = (grad_middle + grad_input_norm).astype(BF)
    late = lax.psum(
        tuple(
            v.astype(BF)
            for v in (grad_query_weight, grad_key_weight, grad_value_weight, grad_norm_gain, grad_mlp_gain)
        ),
        ALL,
    )
    early = [v.astype(F32) for v in early]
    late = [v.astype(F32) for v in late]
    result = zigzag(result)
    grad_input = zigzag(grad_input)
    return (
        result[None],
        grad_input[None],
        late[3],
        late[0],
        late[1],
        late[2],
        early[0],
        late[4],
        early[1],
        early[2],
        early[3],
    )


def solution(mesh):
    inner = Mesh(mesh.devices.reshape(4, 4, 4, 2), ALL)
    row = P("dp", SEQ, None)
    flat = P("dp", SEQ)
    return jax.shard_map(
        body,
        mesh=inner,
        in_specs=(row, flat, flat) + (P(),) * 9 + (row,),
        out_specs=(row, row) + (P(),) * 9,
        check_vma=False,
    )
```

```python
from functools import partial

import jax
import jax.numpy as jnp
from jax import lax
from jax.experimental import pallas as pl
from jax.experimental.pallas import tpu as pltpu
from jax.sharding import Mesh
from jax.sharding import PartitionSpec as P

D = 576
H = 9
KVH = 3
GROUP = H // KVH
HD = 64
HALF = HD // 2
FF = 1536
KVW = KVH * HD
EPSILON = 1e-05
ROPE_BASE = 10000.0
LOG2E = 1.4426950408889634
MASKED = -1e30
SCALE = HD**-0.5

TOK = 256
CHUNK = TOK // 2
UNITS = 32
COLS = GROUP * CHUNK
PADROWS = TOK + 16
LATE = 1024
FF_BLOCK = 512

SEQ = ("x", "z", "core")
ALL = ("dp", "x", "z", "core")
BF = jnp.bfloat16
F32 = jnp.float32

NT = (((1,), (1,)), ((), ()))
NN = (((1,), (0,)), ((), ()))
TN = (((0,), (0,)), ((), ()))


def mm(left, right, dims=NN):
    return lax.dot_general(left, right, dims, preferred_element_type=F32)


def vmem(count):
    return [pl.BlockSpec(memory_space=pltpu.VMEM)] * count


def smem():
    return pl.BlockSpec(memory_space=pltpu.SMEM)


def call(kernel, name, out_shape, scalars, arrays, scratch=(), flops=10**8, moved=10**6):
    outs = out_shape if isinstance(out_shape, (tuple, list)) else (out_shape,)
    given = ([] if scalars is None else [scalars]) + list(arrays)
    specs = ([] if scalars is None else [smem()]) + vmem(len(arrays))
    return pl.pallas_call(
        kernel,
        out_shape=out_shape,
        in_specs=specs,
        out_specs=tuple(vmem(len(outs))) if isinstance(out_shape, (tuple, list)) else vmem(1)[0],
        scratch_shapes=list(scratch),
        compiler_params=pltpu.CompilerParams(vmem_limit_bytes=56 * 1024 * 1024),
        cost_estimate=pl.CostEstimate(flops=flops, bytes_accessed=moved, transcendentals=0),
        name=name,
    )(*given)


def shape(*dims, dtype=BF):
    return jax.ShapeDtypeStruct(dims, dtype)


def column_info(scalars, marks_ref, kv_ref):
    lo_idx = scalars[0]
    first_len = kv_ref[0, TOK : TOK + 16, 0:128].astype(F32)[0:1, :].astype(jnp.int32)
    first_len = jnp.concatenate([first_len] * (2 * GROUP), axis=1)
    hi, lo = marks_ref[1 - lo_idx, 0:1, :], marks_ref[lo_idx, 0:1, :]
    marks = jnp.concatenate([hi] * GROUP + [lo] * GROUP, axis=1)
    first_key = jnp.where(marks < 0, first_len, marks)
    lane = lax.broadcasted_iota(jnp.int32, (1, 2 * COLS), 1)
    start = jnp.where(lane < COLS, scalars[2], scalars[1]) * CHUNK
    return first_key, start + lax.rem(lane, CHUNK)


def full_mask(tile, first_key, place, rows, cols):
    keys = tile * TOK + lax.broadcasted_iota(jnp.int32, (rows, cols), 0)
    return (keys >= first_key[:, :cols]) & (keys <= place[:, :cols])


def tiles(scalars, step):
    lo_diag = scalars[1] // 2
    hi_diag = scalars[2] // 2

    @pl.loop(0, jnp.where(lo_diag > 0, 2, 1))
    def _(j):
        step(j * lo_diag, 1, 2 * COLS, True)

    @pl.loop(1, lo_diag)
    def _(t):
        step(t, 1, 2 * COLS, False)

    @pl.loop(0, (hi_diag - lo_diag - 1) // 2)
    def _(j):
        step(lo_diag + 1 + 2 * j, 2, COLS, False)

    step(hi_diag, 1, COLS, True)


def gather_columns(cat_ref, source_ref, scalars, first_row):
    cat_ref[...] = jnp.zeros_like(cat_ref)
    lo_idx = scalars[0]
    for part in range(2):
        index = (1 - lo_idx) if part == 0 else lo_idx
        lanes = pl.ds(pl.multiple_of(index * CHUNK, CHUNK), CHUNK)
        for head in range(H):
            at = part * COLS + (head % GROUP) * CHUNK
            block = source_ref[head * HD : (head + 1) * HD, lanes]
            cat_ref[head // GROUP, first_row : first_row + HD, at : at + CHUNK] = block


def scatter_columns(out_ref, values, group, scalars):
    lo_idx = scalars[0]
    for part in range(2):
        index = (1 - lo_idx) if part == 0 else lo_idx
        lanes = pl.ds(pl.multiple_of(index * CHUNK, CHUNK), CHUNK)
        for j in range(GROUP):
            head = group * GROUP + j
            at = part * COLS + j * CHUNK
            out_ref[head * HD : (head + 1) * HD, lanes] = values[:, at : at + CHUNK]


def forward_kernel(scalars, marks_ref, q_ref, kv_ref, out_ref, lse_ref, qcat, acc, run_max):
    first_key, place = column_info(scalars, marks_ref, kv_ref)
    gather_columns(qcat, q_ref, scalars, 0)
    acc[...] = jnp.zeros_like(acc)
    run_max[...] = jnp.full_like(run_max, MASKED)

    def step(tile, count, cols, whole):
        rows = count * TOK
        if whole:
            allowed = full_mask(tile, first_key, place, rows, cols)
        else:
            seen = first_key[:, :cols] <= tile * TOK
        for g in range(KVH):
            lanes = slice(g * 128, (g + 1) * 128)
            block = kv_ref[pl.ds(tile, count), 0:TOK, lanes].reshape(rows, 128)
            scores = mm(block, qcat[g, :, 0:cols]) * LOG2E
            old_max = run_max[g, 0:1, 0:cols]
            if whole:
                scores = jnp.where(allowed, scores, MASKED)
                new_max = jnp.maximum(old_max, jnp.max(scores, axis=0, keepdims=True))
                shift = new_max
            else:
                new_max = jnp.maximum(old_max, jnp.max(scores, axis=0, keepdims=True))
                new_max = jnp.where(seen, new_max, old_max)
                shift = jnp.where(seen, new_max, -MASKED)
            weights = jnp.exp2(scores - shift).astype(BF)
            factor = jnp.exp2(old_max - new_max)
            values = jnp.concatenate([jnp.ones((16, rows), BF), jnp.transpose(block)[HD:, :]], axis=0)
            acc[g, :, 0:cols] = acc[g, :, 0:cols] * factor + mm(values, weights)
            run_max[g, 0:1, 0:cols] = new_max

    tiles(scalars, step)
    for g in range(KVH):
        total = acc[g, 0:1, :]
        scatter_columns(out_ref, acc[g, 16:, :] / total, g, scalars)
        lse_ref[g] = jnp.broadcast_to(run_max[g, 0:1, :] + jnp.log2(total), (8, 2 * COLS))


def backward_kernel(
    scalars, marks_ref, q_ref, do_ref, out_ref, lse_ref, kv_ref, dq_ref, mine_ref, other_ref, qcat, docat, acc, delta
):
    first_key, place = column_info(scalars, marks_ref, kv_ref)
    gather_columns(qcat, q_ref, scalars, 0)
    gather_columns(docat, do_ref, scalars, HD)
    lo_idx = scalars[0]
    hi_diag = scalars[2] // 2
    my_x, my_z, my_c = scalars[3], scalars[4], scalars[5]
    acc[...] = jnp.zeros_like(acc)
    for part in range(2):
        index = (1 - lo_idx) if part == 0 else lo_idx
        lanes = pl.ds(pl.multiple_of(index * CHUNK, CHUNK), CHUNK)
        for head in range(H):
            rows = slice(head * HD, (head + 1) * HD)
            at = part * COLS + (head % GROUP) * CHUNK
            terms = do_ref[rows, lanes].astype(F32) * out_ref[rows, lanes]
            delta[head // GROUP, 0:1, at : at + CHUNK] = jnp.sum(terms, axis=0, keepdims=True)

    def store(tile, lanes, grads):
        mirrored = UNITS - 1 - tile
        kx, kz = (tile // 8 - my_x) & 3, ((tile // 2) % 4 - my_z) & 3
        mx, mz = (mirrored // 8 - my_x) & 3, ((mirrored // 2) % 4 - my_z) & 3
        same = lax.rem(tile, 2) == my_c

        @pl.when(same)
        def _():
            mine_ref[0, kx, kz, :, lanes] = grads[0:CHUNK]
            other_ref[1, mz, mx, :, lanes] = grads[CHUNK:TOK]

        @pl.when(jnp.logical_not(same))
        def _():
            other_ref[0, kx, kz, :, lanes] = grads[0:CHUNK]
            mine_ref[1, mz, mx, :, lanes] = grads[CHUNK:TOK]

    def step(tile, count, cols, whole):
        rows = count * TOK
        if whole:
            allowed = full_mask(tile, first_key, place, rows, cols)
        else:
            seen = first_key[:, :cols] <= tile * TOK
        all_grads = []
        for g in range(KVH):
            lanes = slice(g * 128, (g + 1) * 128)
            block = kv_ref[pl.ds(tile, count), 0:TOK, lanes].reshape(rows, 128)
            q_part = qcat[g, :, 0:cols]
            do_part = docat[g, :, 0:cols]
            scores = mm(block, q_part) * LOG2E
            shift = lse_ref[g, 0:1, 0:cols]
            if whole:
                scores = jnp.where(allowed, scores, MASKED)
            else:
                shift = jnp.where(seen, shift, -MASKED)
            probs = jnp.exp2(scores - shift)
            grad_probs = mm(block, do_part)
            grad_scores = (probs * (grad_probs - delta[g, 0:1, 0:cols])).astype(BF)
            grads = mm(grad_scores, q_part, NT) + mm(probs.astype(BF), do_part, NT)
            keys = jnp.transpose(block)[0:HD, :]
            acc[g, :, 0:cols] = acc[g, :, 0:cols] + mm(keys, grad_scores)
            all_grads.append(grads.astype(BF))
        grads = jnp.concatenate(all_grads, axis=1)
        for i in range(count):
            store(tile + i, slice(None), grads[i * TOK : (i + 1) * TOK])

    tiles(scalars, step)

    @pl.loop(hi_diag + 1, UNITS)
    def _(t):
        store(t, slice(None), jnp.zeros((TOK, 2 * KVW), BF))

    for g in range(KVH):
        scatter_columns(dq_ref, acc[g] * SCALE, g, scalars)


def attend(scalars, marks, queries, keys_values):
    return call(
        forward_kernel,
        "attention_forward",
        (shape(D, TOK, dtype=F32), shape(KVH, 8, 2 * COLS, dtype=F32)),
        scalars,
        (marks, queries, keys_values),
        (
            pltpu.VMEM((KVH, 128, 2 * COLS), BF),
            pltpu.VMEM((KVH, 16 + HD, 2 * COLS), F32),
            pltpu.VMEM((KVH, 8, 2 * COLS), F32),
        ),
        flops=20 * 10**9,
        moved=7 * 10**6,
    )


def attend_back(scalars, marks, queries, grad_out, attended, norm, keys_values):
    blocks = shape(2, 4, 4, CHUNK, 2 * KVW)
    return call(
        backward_kernel,
        "attention_backward",
        (shape(D, TOK, dtype=F32), blocks, blocks),
        scalars,
        (marks, queries, grad_out, attended, norm, keys_values),
        (
            pltpu.VMEM((KVH, 128, 2 * COLS), BF),
            pltpu.VMEM((KVH, 128, 2 * COLS), BF),
            pltpu.VMEM((KVH, HD, 2 * COLS), F32),
            pltpu.VMEM((KVH, 8, 2 * COLS), F32),
        ),
        flops=40 * 10**9,
        moved=14 * 10**6,
    )


def inverse_rms(values):
    return lax.rsqrt(jnp.mean(values * values, axis=0, keepdims=True) + EPSILON)


def rotated(values, turn, sign):
    cosine, sine = turn[0:HALF], turn[HALF:] * sign
    first, second = values[:HALF], values[HALF:]
    return jnp.concatenate([first * cosine - second * sine, second * cosine + first * sine], axis=0)


def row_sums(values):
    ones = jnp.ones((16, TOK), BF)
    high = values.astype(BF)
    low = (values - high.astype(F32)).astype(BF)
    return mm(ones, high, NT) + mm(ones, low, NT)


def keys_kernel(x_ref, gain_ref, turn_ref, key_ref, value_ref, seg_ref, out_ref):
    x = x_ref[...].astype(F32)
    act = (x * inverse_rms(x) * gain_ref[...]).astype(BF)
    keys = mm(key_ref[...], act)
    values = mm(value_ref[...], act)
    turn = turn_ref[...]
    for g in range(KVH):
        rows = slice(g * HD, (g + 1) * HD)
        block = jnp.concatenate([rotated(keys[rows], turn, 1.0), values[rows]], axis=0)
        out_ref[0:TOK, g * 128 : (g + 1) * 128] = jnp.transpose(block).astype(BF)
    first_len = jnp.sum((seg_ref[...] == 0).astype(F32), axis=1, keepdims=True)
    out_ref[TOK:, :] = jnp.broadcast_to(first_len, (16, 2 * KVW)).astype(BF)


def queries_kernel(x_ref, gain_ref, turn_ref, weight_ref, act_ref, out_ref):
    x = x_ref[...].astype(F32)
    act = (x * inverse_rms(x) * gain_ref[...]).astype(BF)
    act_ref[...] = act
    queries = mm(weight_ref[...], act, TN)
    turn = turn_ref[...]
    for head in range(H):
        rows = slice(head * HD, (head + 1) * HD)
        low = rotated(queries[rows], turn, 1.0).astype(BF)
        out_ref[rows, :] = low * jnp.asarray(SCALE, BF)


def mlp_kernel(
    x_ref, c_ref, attn_ref, gain_ref, out_weight, gate_ref, up_ref, down_ref,
    result_ref, dmid_ref, dattn_ref, gout_ref, ggate_ref, gup_ref, gdown_ref, ggain_ref,
    mid, act, act_cols, c_cols, result, dact,
):
    block = pl.program_id(0)

    @pl.when(block == 0)
    def _():
        low = attn_ref[...].astype(BF)
        middle = x_ref[...].astype(F32) + mm(out_weight[...], low, TN)
        mid[...] = middle
        normal = (middle * inverse_rms(middle) * gain_ref[...]).astype(BF)
        act_cols[...] = normal
        act[...] = jnp.transpose(normal)
        c_cols[...] = jnp.transpose(c_ref[...])
        result[...] = jnp.zeros_like(result)
        dact[...] = jnp.zeros_like(dact)

    gate = mm(act[...], gate_ref[...])
    up = mm(act[...], up_ref[...])
    sigmoid = 1.0 / (1.0 + jnp.exp(-gate))
    silu = gate * sigmoid
    hidden = (silu * up).astype(BF)
    dhidden = mm(c_cols[...], down_ref[...])
    dup = (dhidden * silu).astype(BF)
    dgate = (dhidden * up * (sigmoid * (1.0 + gate * (1.0 - sigmoid)))).astype(BF)
    result[...] += mm(down_ref[...], hidden, NT)
    gdown_ref[...] = mm(c_ref[...], hidden).astype(BF)
    ggate_ref[...] = mm(act_cols[...], dgate).astype(BF)
    gup_ref[...] = mm(act_cols[...], dup).astype(BF)
    dact[...] += mm(gate_ref[...], dgate, NT) + mm(up_ref[...], dup, NT)

    @pl.when(block == FF // FF_BLOCK - 1)
    def _():
        middle = mid[...]
        gain = gain_ref[...]
        rms = inverse_rms(middle)
        grads = dact[...]
        result_ref[...] = (middle + result[...]).astype(BF)
        ggain_ref[...] = row_sums(grads * middle * rms)
        pulled = grads * gain
        inner = jnp.mean(pulled * middle, axis=0, keepdims=True)
        dmid = c_ref[...].astype(F32) + (pulled * rms - middle * (rms * rms * rms * inner))
        dmid_ref[...] = dmid
        low = dmid.astype(BF)
        gout_ref[...] = mm(attn_ref[...].astype(BF), low, NT).astype(BF)
        dattn_ref[...] = mm(out_weight[...], low).astype(BF)


def feed_forward(x, cotangent, attended, gain, out_weight, gate_weight, up_weight, down_weight):
    whole = lambda *dims: pl.BlockSpec(dims, lambda f: (0,) * len(dims))
    part = pl.BlockSpec((D, FF_BLOCK), lambda f: (0, f))
    return pl.pallas_call(
        mlp_kernel,
        grid=(FF // FF_BLOCK,),
        out_shape=(
            shape(D, TOK), shape(D, TOK, dtype=F32), shape(D, TOK), shape(D, D),
            shape(D, FF), shape(D, FF), shape(D, FF), shape(16, D, dtype=F32),
        ),
        in_specs=[whole(D, TOK), whole(D, TOK), whole(D, TOK), whole(D, 1), whole(D, D), part, part, part],
        out_specs=(whole(D, TOK), whole(D, TOK), whole(D, TOK), whole(D, D), part, part, part, whole(16, D)),
        scratch_shapes=[
            pltpu.VMEM((D, TOK), F32), pltpu.VMEM((TOK, D), BF), pltpu.VMEM((D, TOK), BF),
            pltpu.VMEM((TOK, D), BF), pltpu.VMEM((D, TOK), F32), pltpu.VMEM((D, TOK), F32),
        ],
        compiler_params=pltpu.CompilerParams(vmem_limit_bytes=56 * 1024 * 1024),
        cost_estimate=pl.CostEstimate(flops=5 * 10**9, bytes_accessed=14 * 10**6, transcendentals=10**6),
        name="feed_forward",
    )(x, cotangent, attended, gain, out_weight, gate_weight, up_weight, down_weight)


def query_tail_kernel(dq_ref, turn_ref, act_ref, weight_ref, gquery_ref, dact_ref):
    turn = turn_ref[...]
    heads = [rotated(dq_ref[h * HD : (h + 1) * HD, :], turn, -1.0).astype(BF) for h in range(H)]
    low = jnp.concatenate(heads, axis=0)
    gquery_ref[...] = mm(act_ref[...], low, NT).astype(BF)
    dact_ref[...] = mm(weight_ref[...], low)


def tail_kernel(
    scalars, a0, a1, a2, a3, b0, b1, b2, b3, turn_ref, act_ref, x_ref, gain_ref, key_ref, value_ref, dact_ref, dmid_ref,
    gquery_ref, ggain_ref, grad_ref, mine_ref, other_ref, late,
):
    turn = turn_ref[...]
    summed = []
    for parts in ((a0, a1, a2, a3), (b0, b1, b2, b3)):
        total = parts[0][...].astype(F32)
        for part in parts[1:]:
            total = total + part[...].astype(F32)
        summed.append(total)
    keys, values = [], []
    for g in range(KVH):
        columns = [jnp.transpose(t[:, g * 128 : (g + 1) * 128]) for t in summed]
        columns = jnp.concatenate(columns, axis=1)
        keys.append(rotated(columns[:HD], turn, -1.0).astype(BF))
        values.append(columns[HD:].astype(BF))
    keys, values = jnp.concatenate(keys, axis=0), jnp.concatenate(values, axis=0)
    act = act_ref[...]
    half = LATE // 2
    late[0:D, :] = gquery_ref[...]
    late[D : D + KVW, :] = mm(keys, act, NT).astype(BF)
    late[D + KVW : D + 2 * KVW, :] = mm(values, act, NT).astype(BF)
    grads = dact_ref[...] + mm(key_ref[...], keys, TN) + mm(value_ref[...], values, TN)
    x = x_ref[...].astype(F32)
    rms = inverse_rms(x)
    pulled = grads * gain_ref[...]
    inner = jnp.mean(pulled * x, axis=0, keepdims=True)
    grad_ref[...] = (dmid_ref[...] + (pulled * rms - x * (rms * rms * rms * inner))).astype(BF)
    at = D + 2 * KVW
    late[at : at + 16, :] = ggain_ref[...].astype(BF)
    late[at + 16 : at + 32, :] = row_sums(grads * x * rms).astype(BF)
    late[at + 32 :, :] = jnp.zeros((LATE - at - 32, D), BF)
    core = scalars[5]
    mine_ref[...] = late[pl.ds(pl.multiple_of(core * half, half), half), :]
    other_ref[...] = late[pl.ds(pl.multiple_of((1 - core) * half, half), half), :]


def shift(values, axis, by):
    return lax.ppermute(values, axis, [(i, (i + by) % 4) for i in range(4)])


def swap(values):
    return lax.ppermute(values, "core", [(0, 1), (1, 0)])


def mirror(values):
    return lax.ppermute(values, SEQ, [(i, UNITS - 1 - i) for i in range(UNITS)])


def zigzag(values):
    return jnp.concatenate([values[:, :CHUNK], mirror(values[:, CHUNK:])], axis=1)


def add_pick_kernel(count, scalars, *refs):
    total = refs[0][...].astype(F32)
    for ref in refs[1:count]:
        total = total + ref[...].astype(F32)
    scratch = refs[-1]
    scratch[...] = total.astype(BF).reshape(scratch.shape)
    for k, out in enumerate(refs[count:-1]):
        out[...] = scratch[(scalars[0] + k) & 3]


def add_pick(parts, index):
    rows, width = parts[0].shape
    out = shape(rows // 4, width)
    return call(
        partial(add_pick_kernel, len(parts)), "sum_and_split", (out,) * 4, index, parts,
        (pltpu.VMEM((4, rows // 4, width), BF),),
    )


def place_kernel(count, scalars, *refs):
    out = refs[count]
    for k in range(count):
        out[(scalars[0] - k + 4) & (count - 1)] = refs[k][...]


def place(parts, index):
    rows, width = parts[0].shape
    stacked = call(partial(place_kernel, len(parts)), "place", shape(len(parts), rows, width), index, parts)
    return stacked.reshape(len(parts) * rows, width)


def add_placed_kernel(scalars, p0, p1, p2, p3, out, scratch):
    for k, ref in enumerate((p0, p1, p2, p3)):
        scratch[(scalars[0] - k + 4) & 3] = ref[...].astype(F32)
    out[...] = ((scratch[0] + scratch[1]) + (scratch[2] + scratch[3])).astype(BF)


def add_placed(parts, index):
    rows, width = parts[0].shape
    return call(
        add_placed_kernel, "sum", shape(rows, width), index, parts, (pltpu.VMEM((4, rows, width), F32),)
    )


def plain_sum_kernel(*refs):
    total = refs[0][...].astype(F32)
    for ref in refs[1:-1]:
        total = total + ref[...].astype(F32)
    refs[-1][...] = total.astype(refs[-1].dtype)


def plain_sum(parts):
    return call(plain_sum_kernel, "sum", shape(*parts[0].shape), None, parts)


def sum_everywhere(mine, other, at):
    pieces = add_pick([mine, swap(other)], at["x"])
    pieces = add_pick([pieces[0]] + [shift(pieces[k], "x", k) for k in (1, 2, 3)], at["dp"])
    small = plain_sum([pieces[0]] + [shift(pieces[k], "dp", k) for k in (1, 2, 3)])
    small = add_placed([small] + [shift(small, "z", k) for k in (1, 2, 3)], at["z"])
    part = place([small] + [shift(small, "dp", k) for k in (1, 2, 3)], at["dp"])
    part = place([part] + [shift(part, "x", k) for k in (1, 2, 3)], at["x"])
    return place([part, swap(part)], at["core"])


def turns(places):
    freqs = ROPE_BASE ** (-2.0 * jnp.arange(HALF).astype(F32) / HD)
    angles = freqs[:, None] * places.astype(F32)
    return jnp.concatenate([jnp.cos(angles), jnp.sin(angles)], axis=0)


def body(
    tokens,
    segments,
    positions,
    norm_gain,
    query_weight,
    key_weight,
    value_weight,
    output_weight,
    mlp_gain,
    gate_weight,
    up_weight,
    down_weight,
    cotangent,
):
    axis = {name: lax.axis_index(name) for name in ALL}
    at = {name: index.reshape(1) for name, index in axis.items()}
    unit = (axis["x"] * 4 + axis["z"]) * 2 + axis["core"]
    x_own = tokens[0].T
    key_cols, value_cols, down_cols = key_weight.T, value_weight.T, down_weight.T
    norm_gain = norm_gain.reshape(D, 1)
    mlp_gain = mlp_gain.reshape(D, 1)

    packed = call(
        keys_kernel, "keys_values", shape(PADROWS, 2 * KVW), None,
        (x_own, norm_gain, turns(positions), key_cols, value_cols, segments),
    )
    gathered = lax.all_gather(packed, SEQ, axis=0, tiled=False)

    third = TOK * unit + jnp.sum((segments < 2).astype(jnp.int32))
    marks = jnp.where(segments == 2, third, jnp.where(segments == 1, -1, 0))
    ints = zigzag(jnp.concatenate([marks, positions], axis=0))
    marks, places = ints[0:1], ints[1:2]
    marks = jnp.broadcast_to(marks.reshape(2, 1, CHUNK), (2, 8, CHUNK))
    both = zigzag(jnp.concatenate([x_own, cotangent[0].T], axis=0))
    x, out_grad = both[:D], both[D:]
    chunk_a, chunk_b = 2 * unit, 2 * UNITS - 1 - 2 * unit
    scalars = jnp.stack([
        (chunk_a > chunk_b).astype(jnp.int32), jnp.minimum(chunk_a, chunk_b), jnp.maximum(chunk_a, chunk_b),
        axis["x"], axis["z"], axis["core"],
    ])
    turn = turns(places)
    act, queries = call(
        queries_kernel, "queries", (shape(D, TOK), shape(D, TOK)), None, (x, norm_gain, turn, query_weight)
    )

    attended, norm = attend(scalars, marks, queries, gathered)
    result, dmid, dattn, gout, ggate, gup, gdown, ggain = feed_forward(
        x, out_grad, attended, mlp_gain, output_weight, gate_weight, up_weight, down_cols
    )
    gout, ggate, gup, gdown = lax.psum((gout, ggate, gup, gdown), ALL)

    dq, mine, other = attend_back(scalars, marks, queries, dattn, attended, norm, gathered)

    came = swap(other)
    add = lambda *parts: sum(p.astype(F32) for p in parts).astype(BF)
    first = [add(mine[0, k], came[0, k]) for k in range(4)]
    second = [add(mine[1, k], came[1, k]) for k in range(4)]
    first = [first[0]] + [shift(first[k], "x", k) for k in (1, 2, 3)]
    second = [second[0]] + [shift(second[k], "z", k) for k in (1, 2, 3)]
    gquery, dact = call(
        query_tail_kernel, "queries_back", (shape(D, D), shape(D, TOK, dtype=F32)), None,
        (dq, turn, act, query_weight),
    )
    first = [add(*(p[k] for p in first)) for k in range(4)]
    second = [add(*(p[k] for p in second)) for k in range(4)]
    first = [first[0]] + [shift(first[k], "z", k) for k in (1, 2, 3)]
    second = [second[0]] + [shift(second[k], "x", k) for k in (1, 2, 3)]

    input_grad, mine, other = call(
        tail_kernel, "tail", (shape(D, TOK), shape(LATE // 2, D), shape(LATE // 2, D)), scalars,
        (*first, *second, turn, act, x, norm_gain, key_cols, value_cols, dact, dmid, gquery, ggain),
        (pltpu.VMEM((LATE, D), BF),),
    )
    late = sum_everywhere(mine, other, at)
    result = zigzag(result)
    input_grad = zigzag(input_grad)
    at_gain = D + 2 * KVW
    return (
        result.T[None],
        input_grad.T[None],
        late[at_gain + 16].astype(F32),
        late[0:D].astype(F32),
        late[D : D + KVW].T.astype(F32),
        late[D + KVW : D + 2 * KVW].T.astype(F32),
        gout.astype(F32),
        late[at_gain].astype(F32),
        ggate.astype(F32),
        gup.astype(F32),
        gdown.T.astype(F32),
    )


def solution(mesh):
    inner = Mesh(mesh.devices.reshape(4, 4, 4, 2), ALL)
    row = P("dp", SEQ, None)
    flat = P("dp", SEQ)
    return jax.shard_map(
        body,
        mesh=inner,
        in_specs=(row, flat, flat) + (P(),) * 9 + (row,),
        out_specs=(row, row) + (P(),) * 9,
        check_vma=False,
    )
```

```python
from functools import partial

import jax
import jax.numpy as jnp
from jax import lax
from jax.experimental import pallas as pl
from jax.experimental.pallas import tpu as pltpu
from jax.sharding import Mesh
from jax.sharding import PartitionSpec as P

D = 576
H = 9
KVH = 3
GROUP = H // KVH
HD = 64
HALF = HD // 2
FF = 1536
KVW = KVH * HD
EPSILON = 1e-05
ROPE_BASE = 10000.0
LOG2E = 1.4426950408889634
MASKED = -1e30
SCALE = HD**-0.5

TOK = 256
CHUNK = TOK // 2
UNITS = 32
COLS = GROUP * CHUNK
PADROWS = TOK + 16
KVC = 2 * KVW + 128
SHARD = 96
GROUPS = 32
LATE_SHARD = 144
FF_BLOCK = 512

SEQ = ("x", "z", "core")
ALL = ("dp", "x", "z", "core")
CHIPS = ("dp", "x", "z")
BF = jnp.bfloat16
F32 = jnp.float32

NT = (((1,), (1,)), ((), ()))
NN = (((1,), (0,)), ((), ()))
TN = (((0,), (0,)), ((), ()))


def mm(left, right, dims=NN):
    return lax.dot_general(left, right, dims, preferred_element_type=F32)


def vmem(count):
    return [pl.BlockSpec(memory_space=pltpu.VMEM)] * count


def smem():
    return pl.BlockSpec(memory_space=pltpu.SMEM)


def call(kernel, name, out_shape, scalars, arrays, scratch=(), flops=10**8, moved=10**6):
    outs = out_shape if isinstance(out_shape, (tuple, list)) else (out_shape,)
    given = ([] if scalars is None else [scalars]) + list(arrays)
    specs = ([] if scalars is None else [smem()]) + vmem(len(arrays))
    return pl.pallas_call(
        kernel,
        out_shape=out_shape,
        in_specs=specs,
        out_specs=tuple(vmem(len(outs))) if isinstance(out_shape, (tuple, list)) else vmem(1)[0],
        scratch_shapes=list(scratch),
        compiler_params=pltpu.CompilerParams(vmem_limit_bytes=56 * 1024 * 1024),
        cost_estimate=pl.CostEstimate(flops=flops, bytes_accessed=moved, transcendentals=0),
        name=name,
    )(*given)


def shape(*dims, dtype=BF):
    return jax.ShapeDtypeStruct(dims, dtype)


def column_info(scalars, marks_ref, kv_ref):
    lo_idx = scalars[0]
    first_len = kv_ref[0, TOK : TOK + 16, 0:128].astype(F32)[0:1, :].astype(jnp.int32)
    first_len = jnp.concatenate([first_len] * (2 * GROUP), axis=1)
    hi, lo = marks_ref[1 - lo_idx, 0:1, :], marks_ref[lo_idx, 0:1, :]
    marks = jnp.concatenate([hi] * GROUP + [lo] * GROUP, axis=1)
    first_key = jnp.where(marks < 0, first_len, marks)
    lane = lax.broadcasted_iota(jnp.int32, (1, 2 * COLS), 1)
    start = jnp.where(lane < COLS, scalars[2], scalars[1]) * CHUNK
    return first_key, start + lax.rem(lane, CHUNK)


def full_mask(tile, first_key, place, rows, cols):
    keys = tile * TOK + lax.broadcasted_iota(jnp.int32, (rows, cols), 0)
    return (keys >= first_key[:, :cols]) & (keys <= place[:, :cols])


def tiles(scalars, step):
    lo_diag = scalars[1] // 2
    hi_diag = scalars[2] // 2

    @pl.loop(0, jnp.where(lo_diag > 0, 2, 1))
    def _(j):
        step(j * lo_diag, 1, 2 * COLS, True)

    @pl.loop(1, lo_diag)
    def _(t):
        step(t, 1, 2 * COLS, False)

    @pl.loop(0, (hi_diag - lo_diag - 1) // 2)
    def _(j):
        step(lo_diag + 1 + 2 * j, 2, COLS, False)

    step(hi_diag, 1, COLS, True)


def gather_columns(cat_ref, source_ref, scalars, first_row):
    cat_ref[...] = jnp.zeros_like(cat_ref)
    lo_idx = scalars[0]
    for part in range(2):
        index = (1 - lo_idx) if part == 0 else lo_idx
        lanes = pl.ds(pl.multiple_of(index * CHUNK, CHUNK), CHUNK)
        for head in range(H):
            at = part * COLS + (head % GROUP) * CHUNK
            block = source_ref[head * HD : (head + 1) * HD, lanes]
            cat_ref[head // GROUP, first_row : first_row + HD, at : at + CHUNK] = block


def scatter_columns(out_ref, values, group, scalars):
    lo_idx = scalars[0]
    for part in range(2):
        index = (1 - lo_idx) if part == 0 else lo_idx
        lanes = pl.ds(pl.multiple_of(index * CHUNK, CHUNK), CHUNK)
        for j in range(GROUP):
            head = group * GROUP + j
            at = part * COLS + j * CHUNK
            out_ref[head * HD : (head + 1) * HD, lanes] = values[:, at : at + CHUNK]


def forward_kernel(scalars, marks_ref, q_ref, kv_ref, out_ref, lse_ref, qcat, acc, run_max):
    first_key, place = column_info(scalars, marks_ref, kv_ref)
    gather_columns(qcat, q_ref, scalars, 0)
    acc[...] = jnp.zeros_like(acc)
    run_max[...] = jnp.full_like(run_max, MASKED)

    def step(tile, count, cols, whole):
        rows = count * TOK
        if whole:
            allowed = full_mask(tile, first_key, place, rows, cols)
        else:
            seen = first_key[:, :cols] <= tile * TOK
        for g in range(KVH):
            lanes = slice(g * 128, (g + 1) * 128)
            block = kv_ref[pl.ds(tile, count), 0:TOK, lanes].reshape(rows, 128)
            scores = mm(block, qcat[g, :, 0:cols]) * LOG2E
            old_max = run_max[g, 0:1, 0:cols]
            if whole:
                scores = jnp.where(allowed, scores, MASKED)
                new_max = jnp.maximum(old_max, jnp.max(scores, axis=0, keepdims=True))
                shift = new_max
            else:
                new_max = jnp.maximum(old_max, jnp.max(scores, axis=0, keepdims=True))
                new_max = jnp.where(seen, new_max, old_max)
                shift = jnp.where(seen, new_max, -MASKED)
            weights = jnp.exp2(scores - shift).astype(BF)
            factor = jnp.exp2(old_max - new_max)
            values = jnp.concatenate([jnp.ones((16, rows), BF), jnp.transpose(block)[HD:, :]], axis=0)
            acc[g, :, 0:cols] = acc[g, :, 0:cols] * factor + mm(values, weights)
            run_max[g, 0:1, 0:cols] = new_max

    tiles(scalars, step)
    for g in range(KVH):
        total = acc[g, 0:1, :]
        scatter_columns(out_ref, acc[g, 16:, :] / total, g, scalars)
        lse_ref[g] = jnp.broadcast_to(run_max[g, 0:1, :] + jnp.log2(total), (8, 2 * COLS))


def turned_back(grads, table):
    lane = lax.broadcasted_iota(jnp.int32, table.shape, 1)
    table = table + pltpu.roll(table, 64, 1)
    first = (lane & HALF) == 0
    cosine = jnp.where(lane < HD, jnp.where(first, table, pltpu.roll(table, HALF, 1)), 1.0)
    sine = jnp.where(first, pltpu.roll(table, 128 - HALF, 1), -table)
    sine = jnp.where(lane < HD, sine, 0.0)
    out = []
    for grad in grads:
        grad = grad.astype(F32)
        partner = jnp.where(first, pltpu.roll(grad, 128 - HALF, 1), pltpu.roll(grad, HALF, 1))
        out.append((grad * cosine + partner * sine).astype(BF))
    return jnp.concatenate(out, axis=1)


def backward_kernel(
    scalars, marks_ref, q_ref, do_ref, out_ref, lse_ref, kv_ref, dq_ref, mine_ref, other_ref, qcat, docat, acc, delta
):
    first_key, place = column_info(scalars, marks_ref, kv_ref)
    gather_columns(qcat, q_ref, scalars, 0)
    gather_columns(docat, do_ref, scalars, HD)
    lo_idx = scalars[0]
    hi_diag = scalars[2] // 2
    my_x, my_z, my_c = scalars[3], scalars[4], scalars[5]
    acc[...] = jnp.zeros_like(acc)
    for part in range(2):
        index = (1 - lo_idx) if part == 0 else lo_idx
        lanes = pl.ds(pl.multiple_of(index * CHUNK, CHUNK), CHUNK)
        for head in range(H):
            rows = slice(head * HD, (head + 1) * HD)
            at = part * COLS + (head % GROUP) * CHUNK
            terms = do_ref[rows, lanes].astype(F32) * out_ref[rows, lanes]
            delta[head // GROUP, 0:1, at : at + CHUNK] = jnp.sum(terms, axis=0, keepdims=True)

    def store(tile, grads):
        mirrored = UNITS - 1 - tile
        kx, kz = (tile // 8 - my_x) & 3, ((tile // 2) % 4 - my_z) & 3
        mx, mz = (mirrored // 8 - my_x) & 3, ((mirrored // 2) % 4 - my_z) & 3
        same = lax.rem(tile, 2) == my_c

        def put(first_ref, second_ref):
            for g, grad in enumerate(grads):
                first_ref[0, kx, kz, g * CHUNK : (g + 1) * CHUNK, :] = grad[0:CHUNK]
                second_ref[1, mz, mx, g * CHUNK : (g + 1) * CHUNK, :] = grad[CHUNK:TOK]

        @pl.when(same)
        def _():
            put(mine_ref, other_ref)

        @pl.when(jnp.logical_not(same))
        def _():
            put(other_ref, mine_ref)

    def step(tile, count, cols, whole):
        rows = count * TOK
        if whole:
            allowed = full_mask(tile, first_key, place, rows, cols)
        else:
            seen = first_key[:, :cols] <= tile * TOK
        all_grads = []
        for g in range(KVH):
            lanes = slice(g * 128, (g + 1) * 128)
            block = kv_ref[pl.ds(tile, count), 0:TOK, lanes].reshape(rows, 128)
            q_part = qcat[g, :, 0:cols]
            do_part = docat[g, :, 0:cols]
            scores = mm(block, q_part) * LOG2E
            shift = lse_ref[g, 0:1, 0:cols]
            if whole:
                scores = jnp.where(allowed, scores, MASKED)
            else:
                shift = jnp.where(seen, shift, -MASKED)
            probs = jnp.exp2(scores - shift)
            grad_probs = mm(block, do_part)
            grad_scores = (probs * (grad_probs - delta[g, 0:1, 0:cols])).astype(BF)
            all_grads.append(mm(grad_scores, q_part, NT) + mm(probs.astype(BF), do_part, NT))
            keys = jnp.transpose(block)[0:HD, :]
            acc[g, :, 0:cols] = acc[g, :, 0:cols] + mm(keys, grad_scores)
        for i in range(count):
            store(tile + i, [grad[i * TOK : (i + 1) * TOK].astype(BF) for grad in all_grads])

    tiles(scalars, step)

    @pl.loop(hi_diag + 1, UNITS)
    def _(t):
        store(t, [jnp.zeros((TOK, 128), BF)] * KVH)

    for g in range(KVH):
        scatter_columns(dq_ref, acc[g] * SCALE, g, scalars)


def attend(scalars, marks, queries, keys_values):
    return call(
        forward_kernel,
        "attention_forward",
        (shape(D, TOK, dtype=F32), shape(KVH, 8, 2 * COLS, dtype=F32)),
        scalars,
        (marks, queries, keys_values),
        (
            pltpu.VMEM((KVH, 128, 2 * COLS), BF),
            pltpu.VMEM((KVH, 16 + HD, 2 * COLS), F32),
            pltpu.VMEM((KVH, 8, 2 * COLS), F32),
        ),
        flops=20 * 10**9,
        moved=7 * 10**6,
    )


def attend_back(scalars, marks, queries, grad_out, attended, norm, keys_values):
    blocks = shape(2, 4, 4, KVH * CHUNK, 128)
    return call(
        backward_kernel,
        "attention_backward",
        (shape(D, TOK, dtype=F32), blocks, blocks),
        scalars,
        (marks, queries, grad_out, attended, norm, keys_values),
        (
            pltpu.VMEM((KVH, 128, 2 * COLS), BF),
            pltpu.VMEM((KVH, 128, 2 * COLS), BF),
            pltpu.VMEM((KVH, HD, 2 * COLS), F32),
            pltpu.VMEM((KVH, 8, 2 * COLS), F32),
        ),
        flops=40 * 10**9,
        moved=24 * 10**6,
    )


def inverse_rms(values):
    return lax.rsqrt(jnp.mean(values * values, axis=0, keepdims=True) + EPSILON)


def rotated(values, turn, sign):
    cosine, sine = turn[0:HALF], turn[HALF:] * sign
    first, second = values[:HALF], values[HALF:]
    return jnp.concatenate([first * cosine - second * sine, second * cosine + first * sine], axis=0)


def row_sums(values):
    ones = jnp.ones((16, values.shape[1]), BF)
    high = values.astype(BF)
    low = (values - high.astype(F32)).astype(BF)
    return mm(ones, high, NT) + mm(ones, low, NT)


def keys_kernel(x_ref, gain_ref, turn_ref, key_ref, value_ref, seg_ref, out_ref, act_ref):
    x = x_ref[...].astype(F32)
    act = (x * inverse_rms(x) * gain_ref[...]).astype(BF)
    act_ref[...] = act
    keys = mm(key_ref[...], act)
    values = mm(value_ref[...], act)
    turn = turn_ref[...]
    for g in range(KVH):
        rows = slice(g * HD, (g + 1) * HD)
        block = jnp.concatenate([rotated(keys[rows], turn, 1.0), values[rows]], axis=0)
        out_ref[0:TOK, g * 128 : (g + 1) * 128] = jnp.transpose(block).astype(BF)
    high = turn.astype(BF).astype(F32)
    out_ref[0:TOK, 2 * KVW :] = jnp.transpose(jnp.concatenate([high, turn - high], axis=0)).astype(BF)
    first_len = jnp.sum((seg_ref[...] == 0).astype(F32), axis=1, keepdims=True)
    out_ref[TOK:, :] = jnp.broadcast_to(first_len, (16, KVC)).astype(BF)


def queries_kernel(x_ref, gain_ref, turn_ref, weight_ref, act_ref, out_ref):
    x = x_ref[...].astype(F32)
    act = (x * inverse_rms(x) * gain_ref[...]).astype(BF)
    act_ref[...] = act
    queries = mm(weight_ref[...], act, TN)
    turn = turn_ref[...]
    for head in range(H):
        rows = slice(head * HD, (head + 1) * HD)
        low = rotated(queries[rows], turn, 1.0).astype(BF)
        out_ref[rows, :] = low * jnp.asarray(SCALE, BF)


def mlp_kernel(
    scalars, x_ref, c_ref, attn_ref, gain_ref, out_weight, gate_ref, up_ref, down_ref,
    result_ref, dmid_ref, dattn_ref, ggain_ref, mine_ref, other_ref,
    mid, act, act_cols, c_cols, result, dact, shards, sems,
):
    block = pl.program_id(0)
    my_c = scalars[5]

    def put(group, values):
        for k in range(values.shape[1] // 128):
            for i in range(values.shape[0] // SHARD):
                j = k * (values.shape[0] // SHARD) + i
                piece = values[i * SHARD : (i + 1) * SHARD, k * 128 : (k + 1) * 128]
                shards[group + j // 8, j % 8] = piece

    def send(group):
        @pl.when(group // 16 == my_c)
        def _():
            pltpu.make_async_copy(shards.at[group], mine_ref.at[group % 16], sems.at[0]).start()

        @pl.when(group // 16 != my_c)
        def _():
            pltpu.make_async_copy(shards.at[group], other_ref.at[group % 16], sems.at[1]).start()

    @pl.when(block == 0)
    def _():
        low = attn_ref[...].astype(BF)
        middle = x_ref[...].astype(F32) + mm(out_weight[...], low, TN)
        mid[...] = middle
        normal = (middle * inverse_rms(middle) * gain_ref[...]).astype(BF)
        act_cols[...] = normal
        act[...] = jnp.transpose(normal)
        c_cols[...] = jnp.transpose(c_ref[...])
        result[...] = jnp.zeros_like(result)
        dact[...] = jnp.zeros_like(dact)

    gate = mm(act[...], gate_ref[...])
    up = mm(act[...], up_ref[...])
    sigmoid = 1.0 / (1.0 + jnp.exp(-gate))
    silu = gate * sigmoid
    hidden = (silu * up).astype(BF)
    dhidden = mm(c_cols[...], down_ref[...])
    dup = (dhidden * silu).astype(BF)
    dgate = (dhidden * up * (sigmoid * (1.0 + gate * (1.0 - sigmoid)))).astype(BF)
    result[...] += mm(down_ref[...], hidden, NT)
    put(block * 9, mm(act_cols[...], dgate).astype(BF))
    put(block * 9 + 3, mm(act_cols[...], dup).astype(BF))
    put(block * 9 + 6, mm(c_ref[...], hidden).astype(BF))
    for group in range(9):
        send(block * 9 + group)
    dact[...] += mm(gate_ref[...], dgate, NT) + mm(up_ref[...], dup, NT)

    @pl.when(block == FF // FF_BLOCK - 1)
    def _():
        middle = mid[...]
        gain = gain_ref[...]
        rms = inverse_rms(middle)
        grads = dact[...]
        result_ref[...] = (middle + result[...]).astype(BF)
        ggain_ref[...] = row_sums(grads * middle * rms)
        pulled = grads * gain
        inner = jnp.mean(pulled * middle, axis=0, keepdims=True)
        dmid = c_ref[...].astype(F32) + (pulled * rms - middle * (rms * rms * rms * inner))
        dmid_ref[...] = dmid
        low = dmid.astype(BF)
        dattn_ref[...] = mm(out_weight[...], low).astype(BF)
        gout = mm(attn_ref[...].astype(BF), low, NT).astype(BF)
        put(27, gout[:, :512])
        shards[30:32] = jnp.zeros((2, 8, SHARD, 128), BF)
        put(30, jnp.concatenate([gout[: D // 2, 512:], gout[D // 2 :, 512:]], axis=1))
        for group in range(27, 32):
            send(group)
        for i, ref in enumerate((mine_ref, other_ref)):
            pltpu.make_async_copy(ref, ref, sems.at[i]).wait()


def feed_forward(scalars, x, cotangent, attended, gain, out_weight, gate_weight, up_weight, down_weight):
    whole = lambda *dims: pl.BlockSpec(dims, lambda f: (0,) * len(dims))
    part = pl.BlockSpec((D, FF_BLOCK), lambda f: (0, f))
    return pl.pallas_call(
        mlp_kernel,
        grid=(FF // FF_BLOCK,),
        out_shape=(shape(D, TOK), shape(D, TOK, dtype=F32), shape(D, TOK), shape(16, D, dtype=F32))
        + (shape(GROUPS // 2, 8, SHARD, 128),) * 2,
        in_specs=[smem(), whole(D, TOK), whole(D, TOK), whole(D, TOK), whole(D, 1), whole(D, D), part, part, part],
        out_specs=(whole(D, TOK), whole(D, TOK), whole(D, TOK), whole(16, D))
        + (pl.BlockSpec(memory_space=pl.ANY),) * 2,
        scratch_shapes=[
            pltpu.VMEM((D, TOK), F32), pltpu.VMEM((TOK, D), BF), pltpu.VMEM((D, TOK), BF),
            pltpu.VMEM((TOK, D), BF), pltpu.VMEM((D, TOK), F32), pltpu.VMEM((D, TOK), F32),
            pltpu.VMEM((GROUPS, 8, SHARD, 128), BF), pltpu.SemaphoreType.DMA((2,)),
        ],
        compiler_params=pltpu.CompilerParams(vmem_limit_bytes=56 * 1024 * 1024),
        cost_estimate=pl.CostEstimate(flops=5 * 10**9, bytes_accessed=14 * 10**6, transcendentals=10**6),
        name="feed_forward",
    )(scalars, x, cotangent, attended, gain, out_weight, gate_weight, up_weight, down_weight)


def early_finish_kernel(shards, gate_ref, up_ref, down_ref, out_ref):
    block = pl.program_id(0)

    def get(group, k):
        pieces = []
        for i in range(D // SHARD):
            piece = group * 8 + D // SHARD * k + i
            half, piece = piece // (GROUPS * 4), piece % (GROUPS * 4)
            pieces.append(shards[piece // 2, half, piece % 2])
        return jnp.concatenate(pieces, axis=0).astype(F32)

    for kind, ref in enumerate((gate_ref, up_ref, down_ref)):
        for k in range(4):
            ref[:, k * 128 : (k + 1) * 128] = get(block * 9 + kind * 3, k)

    @pl.when(block == FF // FF_BLOCK - 1)
    def _():
        for k in range(4):
            out_ref[:, k * 128 : (k + 1) * 128] = get(27, k)
        rest = get(30, 0)[: D // 2]
        out_ref[:, 512:] = jnp.concatenate([rest[:, :HD], rest[:, HD:]], axis=0)


def early_finish(shards):
    part = pl.BlockSpec((D, FF_BLOCK), lambda f: (0, f))
    return pl.pallas_call(
        early_finish_kernel,
        grid=(FF // FF_BLOCK,),
        out_shape=(shape(D, FF, dtype=F32),) * 3 + (shape(D, D, dtype=F32),),
        in_specs=[pl.BlockSpec(shards.shape, lambda f: (0,) * 5)],
        out_specs=(part, part, part, pl.BlockSpec((D, D), lambda f: (0, 0))),
        compiler_params=pltpu.CompilerParams(vmem_limit_bytes=56 * 1024 * 1024),
        cost_estimate=pl.CostEstimate(flops=10**7, bytes_accessed=19 * 10**6, transcendentals=0),
        name="early_gradients",
    )(shards)


def late_rows():
    return 0, 2592, 4320, 4400


def pack(buffer, at, values):
    count = values.shape[0]
    for k in range(4):
        buffer[at + k * count : at + (k + 1) * count, :] = values[:, k * 128 : (k + 1) * 128]
    if count > 16:
        rest = jnp.concatenate([values[: count // 2, 512:], values[count // 2 :, 512:]], axis=1)
        buffer[at + 4 * count : at + 4 * count + count // 2, :] = rest
    else:
        buffer[at + 4 * count : at + 5 * count, 0:64] = values[:, 512:]


def unpack(buffer, at, count):
    blocks = [buffer[at + k * count : at + (k + 1) * count, :] for k in range(4)]
    if count > 16:
        rest = buffer[at + 4 * count : at + 4 * count + count // 2, :]
        rest = jnp.concatenate([rest[:, :64], rest[:, 64:]], axis=0)
    else:
        rest = buffer[at + 4 * count : at + 5 * count, 0:64]
    return jnp.concatenate(blocks + [rest], axis=1)


def late_kernel(
    scalars, dq_ref, turn_ref, act_ref, weight_ref, key_ref, value_ref, gain_ref, ggain_ref, kv_ref, acts_ref,
    dkv_mine, dkv_other, dact_ref, mine_ref, other_ref, late, gkv,
):
    my_x, my_z, my_c, my_y = scalars[3], scalars[4], scalars[5], scalars[6]
    gkv[...] = jnp.zeros_like(gkv)

    @pl.loop(0, 16)
    def _(step):
        kx, kz = step // 4, step % 4
        x, z = (my_x + kx) & 3, (my_z + kz) & 3
        mx, mz = (3 - x - my_x) & 3, (3 - z - my_z) & 3
        total = None
        for core, first_ref, second_ref in ((my_c, dkv_mine, dkv_other), (1 - my_c, dkv_other, dkv_mine)):
            unit = x * 8 + z * 2 + core
            first, second = first_ref[0, kx, kz], second_ref[1, mz, mx]
            grads = []
            for g in range(KVH):
                rows = slice(g * CHUNK, (g + 1) * CHUNK)
                grads.append(jnp.concatenate([first[rows], second[rows]], axis=0))
            turned = turned_back(grads, kv_ref[unit, 0:TOK, 2 * KVW :].astype(F32))
            product = mm(acts_ref[unit], turned)
            total = product if total is None else total + product
        gkv[...] += total

    turn = turn_ref[...]
    heads = [rotated(dq_ref[h * HD : (h + 1) * HD, :], turn, -1.0).astype(BF) for h in range(H)]
    low = jnp.concatenate(heads, axis=0)
    weight = weight_ref[...]
    gquery = mm(act_ref[...], low, NT)
    dact_ref[...] = mm(weight, low)
    at_q, at_kv, at_n, at_m = late_rows()
    late[at_n:, :] = jnp.zeros((32 * LATE_SHARD - at_n, 128), BF)
    pack(late, at_q, gquery.astype(BF))
    gain = row_sums(gquery * weight.astype(F32))
    for g in range(KVH):
        rows = slice(g * HD, (g + 1) * HD)
        grad = gkv[:, g * 128 : (g + 1) * 128]
        late[at_kv + g * D : at_kv + (g + 1) * D, :] = grad.astype(BF)
        columns = jnp.transpose(jnp.concatenate([key_ref[rows, :], value_ref[rows, :]], axis=0))
        gain = gain + row_sums(grad * columns.astype(F32))
    pack(late, at_n, (gain / gain_ref[...]).astype(BF))
    pack(late, at_m, ggain_ref[...].astype(BF))
    for x in range(4):
        for z in range(4):
            index = ((x - my_x) & 3, (z - my_z) & 3)
            for target, core in ((mine_ref, my_c), (other_ref, 1 - my_c)):
                at = ((core * 4 + x) * 4 + z) * LATE_SHARD
                target[index] = late[pl.ds(pl.multiple_of(at, LATE_SHARD), LATE_SHARD), :]


def join_kernel(mine_ref, came_ref, late_mine, late_came, *outs):
    for k in range(4):
        for j in range(4):
            outs[k][j, 0 : KVH * CHUNK, :] = add(mine_ref[0, k, j], came_ref[0, k, j])
            outs[k][j, KVH * CHUNK :, :] = add(late_mine[k, j], late_came[k, j])
            outs[4 + k][j] = add(mine_ref[1, k, j], came_ref[1, k, j])


def late_finish_kernel(scalars, own_ref, came_ref, gquery_ref, gkey_ref, gvalue_ref, gnorm_ref, gmlp_ref, late):
    my_x, my_z, my_c = scalars[3], scalars[4], scalars[5]
    for source, core in ((own_ref, my_c), (came_ref, 1 - my_c)):
        for x in range(4):
            for z in range(4):
                at = ((core * 4 + ((my_x - x) & 3)) * 4 + ((my_z - z) & 3)) * LATE_SHARD
                late[pl.ds(pl.multiple_of(at, LATE_SHARD), LATE_SHARD), :] = source[x, z]
    at_q, at_kv, at_n, at_m = late_rows()
    gquery_ref[...] = unpack(late, at_q, D).astype(F32)
    for g in range(KVH):
        grad = jnp.transpose(late[at_kv + g * D : at_kv + (g + 1) * D, :].astype(F32))
        gkey_ref[g * HD : (g + 1) * HD, :] = grad[:HD]
        gvalue_ref[g * HD : (g + 1) * HD, :] = grad[HD:]
    gnorm_ref[...] = unpack(late, at_n, 16).astype(F32)[0:1]
    gmlp_ref[...] = unpack(late, at_m, 16).astype(F32)[0:1]


def tail_kernel(
    a0, a1, a2, a3, b0, b1, b2, b3, turn_ref, x_ref, gain_ref, key_ref, value_ref, dact_ref, dmid_ref, grad_ref
):
    turn = turn_ref[...]
    summed = []
    for parts in ((a0, a1, a2, a3), (b0, b1, b2, b3)):
        total = parts[0][0 : KVH * CHUNK, :].astype(F32)
        for part in parts[1:]:
            total = total + part[0 : KVH * CHUNK, :].astype(F32)
        summed.append(total)
    keys, values = [], []
    for g in range(KVH):
        columns = [jnp.transpose(t[g * CHUNK : (g + 1) * CHUNK, :]) for t in summed]
        columns = jnp.concatenate(columns, axis=1)
        keys.append(rotated(columns[:HD], turn, -1.0).astype(BF))
        values.append(columns[HD:].astype(BF))
    keys, values = jnp.concatenate(keys, axis=0), jnp.concatenate(values, axis=0)
    grads = dact_ref[...] + mm(key_ref[...], keys, TN) + mm(value_ref[...], values, TN)
    x = x_ref[...].astype(F32)
    rms = inverse_rms(x)
    pulled = grads * gain_ref[...]
    inner = jnp.mean(pulled * x, axis=0, keepdims=True)
    grad_ref[...] = (dmid_ref[...] + (pulled * rms - x * (rms * rms * rms * inner))).astype(BF)


def shift(values, axis, by):
    return lax.ppermute(values, axis, [(i, (i + by) % 4) for i in range(4)])


def swap(values):
    return lax.ppermute(values, "core", [(0, 1), (1, 0)])


def mirror(values):
    return lax.ppermute(values, SEQ, [(i, UNITS - 1 - i) for i in range(UNITS)])


def zigzag(values):
    return jnp.concatenate([values[:, :CHUNK], mirror(values[:, CHUNK:])], axis=1)


def add(*parts):
    parts = [p.astype(F32) for p in parts]
    total = parts[0] + parts[1] if len(parts) == 2 else (parts[0] + parts[2]) + (parts[1] + parts[3])
    return total.astype(BF)


def spread(parts, axis):
    return [parts[0]] + [shift(parts[k], axis, k) for k in (1, 2, 3)]


def collect(values, axis):
    return [values] + [shift(values, axis, k) for k in (1, 2, 3)]


def turns(places):
    freqs = ROPE_BASE ** (-2.0 * jnp.arange(HALF).astype(F32) / HD)
    angles = freqs[:, None] * places.astype(F32)
    return jnp.concatenate([jnp.cos(angles), jnp.sin(angles)], axis=0)


def body(
    tokens,
    segments,
    positions,
    norm_gain,
    query_weight,
    key_weight,
    value_weight,
    output_weight,
    mlp_gain,
    gate_weight,
    up_weight,
    down_weight,
    cotangent,
):
    axis = {name: lax.axis_index(name) for name in ALL}
    at = {name: index.reshape(1) for name, index in axis.items()}
    unit = (axis["x"] * 4 + axis["z"]) * 2 + axis["core"]
    x_own = tokens[0].T
    key_cols, value_cols, down_cols = key_weight.T, value_weight.T, down_weight.T
    norm_gain_row = norm_gain.reshape(1, D)
    norm_gain = norm_gain.reshape(D, 1)
    mlp_gain = mlp_gain.reshape(D, 1)

    packed, own_act = call(
        keys_kernel, "keys_values", (shape(PADROWS, KVC), shape(D, TOK)), None,
        (x_own, norm_gain, turns(positions), key_cols, value_cols, segments),
    )
    gathered = lax.all_gather(packed, SEQ, axis=0, tiled=False)
    acts = lax.all_gather(own_act, SEQ, axis=0, tiled=False)
    x_own, segments, positions, packed = lax.optimization_barrier((x_own, segments, positions, packed))

    third = TOK * unit + jnp.sum((segments < 2).astype(jnp.int32))
    marks = jnp.where(segments == 2, third, jnp.where(segments == 1, -64, 0))
    ints = jnp.concatenate([positions >> 6, positions & 63, marks >> 6, marks & 63], axis=0)
    ints = jnp.pad(ints, ((0, 12), (0, 0))).astype(BF)
    both = zigzag(jnp.concatenate([x_own, cotangent[0].T, ints], axis=0))
    x, out_grad = both[:D], both[D : 2 * D]
    ints = both[2 * D :].astype(jnp.int32)
    places = ints[0:1] * 64 + ints[1:2]
    marks = ints[2:3] * 64 + ints[3:4]
    marks = jnp.broadcast_to(marks.reshape(2, 1, CHUNK), (2, 8, CHUNK))
    chunk_a, chunk_b = 2 * unit, 2 * UNITS - 1 - 2 * unit
    scalars = jnp.stack([
        (chunk_a > chunk_b).astype(jnp.int32), jnp.minimum(chunk_a, chunk_b), jnp.maximum(chunk_a, chunk_b),
        axis["x"], axis["z"], axis["core"], axis["dp"],
    ])
    turn = turns(places)
    act, queries = call(
        queries_kernel, "queries", (shape(D, TOK), shape(D, TOK)), None, (x, norm_gain, turn, query_weight)
    )

    attended, norm = attend(scalars, marks, queries, gathered)
    result, dmid, dattn, ggain, mine, other = feed_forward(
        scalars, x, out_grad, attended, mlp_gain, output_weight, gate_weight, up_weight, down_cols
    )

    early = add(mine, swap(other))
    early, dattn = lax.optimization_barrier((early, dattn))
    early = lax.all_to_all(early.reshape(64, 2, SHARD, 128), CHIPS, 0, 0, tiled=True)

    dq, mine, other = attend_back(scalars, marks, queries, dattn, attended, norm, gathered)
    early = jnp.sum(early.astype(F32), axis=0).astype(BF)
    other, early = lax.optimization_barrier((other, early))
    early = lax.all_gather(early, ALL, axis=0, tiled=False)

    came = swap(other)
    blocks = shape(4, 4, LATE_SHARD, 128)
    dact, late_mine, late_other = call(
        late_kernel, "late_gradients", (shape(D, TOK, dtype=F32), blocks, blocks), scalars,
        (dq, turn, act, query_weight, key_cols, value_cols, norm_gain_row, ggain, gathered, acts, mine, other),
        (pltpu.VMEM((32 * LATE_SHARD, 128), BF), pltpu.VMEM((D, 2 * KVW), F32)),
    )
    halves = call(
        join_kernel, "join", (shape(4, KVH * CHUNK + LATE_SHARD, 128),) * 4 + (shape(4, KVH * CHUNK, 128),) * 4, None,
        (mine, came, late_mine, swap(late_other)),
    )
    first_came, second_came = spread(halves[:4], "x"), spread(halves[4:], "z")
    first = [add(*(c[k] for c in first_came)) for k in range(4)]
    second = [add(*(c[k] for c in second_came)) for k in range(4)]
    first, second = lax.optimization_barrier((first, second))
    first_came, second_came = spread(first, "z"), spread(second, "x")
    late = add(*(part[KVH * CHUNK :] for part in first_came))
    late, second_came = lax.optimization_barrier((late, second_came))
    late_came = collect(late, "dp")
    input_grad = call(
        tail_kernel, "tail", shape(D, TOK), None,
        (*first_came, *second_came, turn, x, norm_gain, key_cols, value_cols, dact, dmid),
    )
    late = add(*late_came)
    late, input_grad, result = lax.optimization_barrier((late, input_grad, result))
    late = jnp.stack(collect(late, "z"))
    input_grad, result = zigzag(input_grad), zigzag(result)
    late = jnp.stack(collect(late, "x"))
    late = call(
        late_finish_kernel, "late_finish",
        (shape(D, D, dtype=F32), shape(KVW, D, dtype=F32), shape(KVW, D, dtype=F32))
        + (shape(1, D, dtype=F32),) * 2,
        scalars, (late, swap(late)), (pltpu.VMEM((32 * LATE_SHARD, 128), BF),),
    )
    early = early_finish(early.reshape(64, 2, 2, SHARD, 128))
    return (
        result.T[None],
        input_grad.T[None],
        late[3].reshape(D),
        late[0],
        late[1].T,
        late[2].T,
        early[3],
        late[4].reshape(D),
        early[0],
        early[1],
        early[2].T,
    )


def solution(mesh):
    inner = Mesh(mesh.devices.reshape(4, 4, 4, 2), ALL)
    row = P("dp", SEQ, None)
    flat = P("dp", SEQ)
    return jax.shard_map(
        body,
        mesh=inner,
        in_specs=(row, flat, flat) + (P(),) * 9 + (row,),
        out_specs=(row, row) + (P(),) * 9,
        check_vma=False,
    )
```

```python
from functools import partial

import jax
import jax.numpy as jnp
from jax import lax
from jax.experimental import pallas as pl
from jax.experimental.pallas import tpu as pltpu
from jax.sharding import Mesh
from jax.sharding import PartitionSpec as P

D = 576
H = 9
KVH = 3
GROUP = H // KVH
HD = 64
HALF = HD // 2
FF = 1536
KVW = KVH * HD
EPSILON = 1e-05
ROPE_BASE = 10000.0
LOG2E = 1.4426950408889634
MASKED = -1e30
SCALE = HD**-0.5

TOK = 256
CHUNK = TOK // 2
UNITS = 32
COLS = GROUP * CHUNK
PADROWS = TOK + 16
ACTR = D + 4 * HALF
SHARD = 96
GROUPS = 32
LATE_SHARD = 144
LATE_SPLIT = 80
KVR = KVH * CHUNK
FF_BLOCK = 512

SEQ = ("x", "z", "core")
ALL = ("dp", "x", "z", "core")
CHIPS = ("dp", "x", "z")
BF = jnp.bfloat16
F32 = jnp.float32

NT = (((1,), (1,)), ((), ()))
NN = (((1,), (0,)), ((), ()))
TN = (((0,), (0,)), ((), ()))


def mm(left, right, dims=NN):
    return lax.dot_general(left, right, dims, preferred_element_type=F32)


def vmem(count):
    return [pl.BlockSpec(memory_space=pltpu.VMEM)] * count


def smem():
    return pl.BlockSpec(memory_space=pltpu.SMEM)


def call(kernel, name, out_shape, scalars, arrays, scratch=(), flops=10**8, moved=10**6):
    outs = out_shape if isinstance(out_shape, (tuple, list)) else (out_shape,)
    given = ([] if scalars is None else [scalars]) + list(arrays)
    specs = ([] if scalars is None else [smem()]) + vmem(len(arrays))
    return pl.pallas_call(
        kernel,
        out_shape=out_shape,
        in_specs=specs,
        out_specs=tuple(vmem(len(outs))) if isinstance(out_shape, (tuple, list)) else vmem(1)[0],
        scratch_shapes=list(scratch),
        compiler_params=pltpu.CompilerParams(vmem_limit_bytes=56 * 1024 * 1024),
        cost_estimate=pl.CostEstimate(flops=flops, bytes_accessed=moved, transcendentals=0),
        name=name,
    )(*given)


def shape(*dims, dtype=BF):
    return jax.ShapeDtypeStruct(dims, dtype)


def column_info(scalars, marks_ref, kv_ref):
    lo_idx = scalars[0]
    first_len = kv_ref[0, TOK : TOK + 16, 0:128].astype(F32)[0:1, :].astype(jnp.int32)
    first_len = jnp.concatenate([first_len] * (2 * GROUP), axis=1)
    hi, lo = marks_ref[1 - lo_idx, 0:1, :], marks_ref[lo_idx, 0:1, :]
    marks = jnp.concatenate([hi] * GROUP + [lo] * GROUP, axis=1)
    first_key = jnp.where(marks < 0, first_len, marks)
    lane = lax.broadcasted_iota(jnp.int32, (1, 2 * COLS), 1)
    start = jnp.where(lane < COLS, scalars[2], scalars[1]) * CHUNK
    return first_key, start + lax.rem(lane, CHUNK)


def full_mask(tile, first_key, place, rows, cols):
    keys = tile * TOK + lax.broadcasted_iota(jnp.int32, (rows, cols), 0)
    return (keys >= first_key[:, :cols]) & (keys <= place[:, :cols])


def tiles(scalars, step, most):
    lo_diag = scalars[1] // 2
    hi_diag = scalars[2] // 2
    joint = jnp.maximum(lo_diag - 1, 0)
    single = hi_diag - lo_diag - 1

    @pl.loop(0, jnp.where(lo_diag > 0, 2, 1))
    def _(j):
        step(j * lo_diag, 1, 2 * COLS, True)

    @pl.loop(0, joint // 2)
    def _(j):
        step(1 + 2 * j, 2, 2 * COLS, False)

    @pl.when(joint % 2 == 1)
    def _():
        step(lo_diag - 1, 1, 2 * COLS, False)

    @pl.loop(0, single // most)
    def _(j):
        step(lo_diag + 1 + most * j, most, COLS, False)

    if most == 4:

        @pl.when(single % 4 == 2)
        def _():
            step(hi_diag - 2, 2, COLS, False)

    step(hi_diag, 1, COLS, True)


def gather_columns(cat_ref, source_ref, scalars, first_row):
    cat_ref[...] = jnp.zeros_like(cat_ref)
    lo_idx = scalars[0]
    for part in range(2):
        index = (1 - lo_idx) if part == 0 else lo_idx
        lanes = pl.ds(pl.multiple_of(index * CHUNK, CHUNK), CHUNK)
        for head in range(H):
            at = part * COLS + (head % GROUP) * CHUNK
            block = source_ref[head * HD : (head + 1) * HD, lanes]
            cat_ref[head // GROUP, first_row : first_row + HD, at : at + CHUNK] = block


def scatter_columns(out_ref, values, group, scalars):
    lo_idx = scalars[0]
    for part in range(2):
        index = (1 - lo_idx) if part == 0 else lo_idx
        lanes = pl.ds(pl.multiple_of(index * CHUNK, CHUNK), CHUNK)
        for j in range(GROUP):
            head = group * GROUP + j
            at = part * COLS + j * CHUNK
            out_ref[head * HD : (head + 1) * HD, lanes] = values[:, at : at + CHUNK]


def forward_kernel(scalars, marks_ref, q_ref, kv_ref, out_ref, lse_ref, qcat, acc, run_max):
    first_key, place = column_info(scalars, marks_ref, kv_ref)
    gather_columns(qcat, q_ref, scalars, 0)
    acc[...] = jnp.zeros_like(acc)
    run_max[...] = jnp.full_like(run_max, MASKED)

    def step(tile, count, cols, whole):
        rows = count * TOK
        if whole:
            allowed = full_mask(tile, first_key, place, rows, cols)
        else:
            seen = first_key[:, :cols] <= tile * TOK
        for g in range(KVH):
            lanes = slice(g * 128, (g + 1) * 128)
            block = kv_ref[pl.ds(tile, count), 0:TOK, lanes].reshape(rows, 128)
            scores = mm(block, qcat[g, :, 0:cols]) * LOG2E
            old_max = run_max[g, 0:1, 0:cols]
            if whole:
                scores = jnp.where(allowed, scores, MASKED)
                new_max = jnp.maximum(old_max, jnp.max(scores, axis=0, keepdims=True))
                shift = new_max
            else:
                new_max = jnp.maximum(old_max, jnp.max(scores, axis=0, keepdims=True))
                new_max = jnp.where(seen, new_max, old_max)
                shift = jnp.where(seen, new_max, -MASKED)
            weights = jnp.exp2(scores - shift).astype(BF)
            factor = jnp.exp2(old_max - new_max)
            values = jnp.concatenate([jnp.ones((16, rows), BF), jnp.transpose(block)[HD:, :]], axis=0)
            acc[g, :, 0:cols] = acc[g, :, 0:cols] * factor + mm(values, weights)
            run_max[g, 0:1, 0:cols] = new_max

    tiles(scalars, step, 4)
    for g in range(KVH):
        total = acc[g, 0:1, :]
        scatter_columns(out_ref, acc[g, 16:, :] / total, g, scalars)
        lse_ref[g] = jnp.broadcast_to(run_max[g, 0:1, :] + jnp.log2(total), (8, 2 * COLS))


def backward_kernel(
    scalars, marks_ref, q_ref, do_ref, out_ref, lse_ref, kv_ref, dq_ref, mine_ref, other_ref, qcat, docat, acc, delta
):
    first_key, place = column_info(scalars, marks_ref, kv_ref)
    gather_columns(qcat, q_ref, scalars, 0)
    gather_columns(docat, do_ref, scalars, HD)
    lo_idx = scalars[0]
    hi_diag = scalars[2] // 2
    my_x, my_z, my_c = scalars[3], scalars[4], scalars[5]
    acc[...] = jnp.zeros_like(acc)
    for part in range(2):
        index = (1 - lo_idx) if part == 0 else lo_idx
        lanes = pl.ds(pl.multiple_of(index * CHUNK, CHUNK), CHUNK)
        for head in range(H):
            rows = slice(head * HD, (head + 1) * HD)
            at = part * COLS + (head % GROUP) * CHUNK
            terms = do_ref[rows, lanes].astype(F32) * out_ref[rows, lanes]
            delta[head // GROUP, 0:1, at : at + CHUNK] = jnp.sum(terms, axis=0, keepdims=True)

    def store(tile, grads):
        mirrored = UNITS - 1 - tile
        kx, kz = (tile // 8 - my_x) & 3, ((tile // 2) % 4 - my_z) & 3
        mx, mz = (mirrored // 8 - my_x) & 3, ((mirrored // 2) % 4 - my_z) & 3
        same = lax.rem(tile, 2) == my_c

        def put(first_ref, second_ref):
            for g, grad in enumerate(grads):
                first_ref[0, kx, kz, g * CHUNK : (g + 1) * CHUNK, :] = grad[0:CHUNK]
                second_ref[1, mz, mx, g * CHUNK : (g + 1) * CHUNK, :] = grad[CHUNK:TOK]

        @pl.when(same)
        def _():
            put(mine_ref, other_ref)

        @pl.when(jnp.logical_not(same))
        def _():
            put(other_ref, mine_ref)

    def step(tile, count, cols, whole):
        rows = count * TOK
        if whole:
            allowed = full_mask(tile, first_key, place, rows, cols)
        else:
            seen = first_key[:, :cols] <= tile * TOK
        all_grads = []
        for g in range(KVH):
            lanes = slice(g * 128, (g + 1) * 128)
            block = kv_ref[pl.ds(tile, count), 0:TOK, lanes].reshape(rows, 128)
            q_part = qcat[g, :, 0:cols]
            do_part = docat[g, :, 0:cols]
            scores = mm(block, q_part) * LOG2E
            shift = lse_ref[g, 0:1, 0:cols]
            if whole:
                scores = jnp.where(allowed, scores, MASKED)
            else:
                shift = jnp.where(seen, shift, -MASKED)
            probs = jnp.exp2(scores - shift)
            grad_probs = mm(block, do_part)
            grad_scores = (probs * (grad_probs - delta[g, 0:1, 0:cols])).astype(BF)
            all_grads.append(mm(grad_scores, q_part, NT) + mm(probs.astype(BF), do_part, NT))
            keys = jnp.transpose(block)[0:HD, :]
            acc[g, :, 0:cols] = acc[g, :, 0:cols] + mm(keys, grad_scores)
        for i in range(count):
            store(tile + i, [grad[i * TOK : (i + 1) * TOK].astype(BF) for grad in all_grads])

    tiles(scalars, step, 2)

    @pl.loop(hi_diag + 1, UNITS)
    def _(t):
        store(t, [jnp.zeros((TOK, 128), BF)] * KVH)

    for g in range(KVH):
        scatter_columns(dq_ref, acc[g] * SCALE, g, scalars)


def attend(scalars, marks, queries, keys_values):
    return call(
        forward_kernel,
        "attention_forward",
        (shape(D, TOK, dtype=F32), shape(KVH, 8, 2 * COLS, dtype=F32)),
        scalars,
        (marks, queries, keys_values),
        (
            pltpu.VMEM((KVH, 128, 2 * COLS), BF),
            pltpu.VMEM((KVH, 16 + HD, 2 * COLS), F32),
            pltpu.VMEM((KVH, 8, 2 * COLS), F32),
        ),
        flops=20 * 10**9,
        moved=7 * 10**6,
    )


def attend_back(scalars, marks, queries, grad_out, attended, norm, keys_values):
    blocks = shape(2, 4, 4, KVH * CHUNK, 128)
    return call(
        backward_kernel,
        "attention_backward",
        (shape(D, TOK, dtype=F32), blocks, blocks),
        scalars,
        (marks, queries, grad_out, attended, norm, keys_values),
        (
            pltpu.VMEM((KVH, 128, 2 * COLS), BF),
            pltpu.VMEM((KVH, 128, 2 * COLS), BF),
            pltpu.VMEM((KVH, HD, 2 * COLS), F32),
            pltpu.VMEM((KVH, 8, 2 * COLS), F32),
        ),
        flops=40 * 10**9,
        moved=24 * 10**6,
    )


def inverse_rms(values):
    return lax.rsqrt(jnp.mean(values * values, axis=0, keepdims=True) + EPSILON)


def rotated(values, turn, sign):
    cosine, sine = turn[0], turn[1] * sign
    first, second = values[:HALF], values[HALF:]
    return jnp.concatenate([first * cosine - second * sine, second * cosine + first * sine], axis=0)


def row_sums(values):
    ones = jnp.ones((16, values.shape[1]), BF)
    high = values.astype(BF)
    low = (values - high.astype(F32)).astype(BF)
    return mm(ones, high, NT) + mm(ones, low, NT)


def column(ref):
    row = ref[...].reshape(1, ref.shape[0])
    return jnp.transpose(jnp.broadcast_to(row, (8, ref.shape[0])))[:, 0:1]


def keys_kernel(x_ref, gain_ref, cos_ref, sin_ref, key_ref, value_ref, seg_ref, out_ref, act_ref):
    x = x_ref[...].astype(F32)
    act = (x * inverse_rms(x) * column(gain_ref)).astype(BF)
    act_ref[0:D, :] = act
    keys = mm(key_ref[...], act)
    values = mm(value_ref[...], act)
    turn = (cos_ref[...], sin_ref[...])
    for g in range(KVH):
        rows = slice(g * HD, (g + 1) * HD)
        block = jnp.concatenate([rotated(keys[rows], turn, 1.0), values[rows]], axis=0)
        out_ref[0:TOK, g * 128 : (g + 1) * 128] = jnp.transpose(block).astype(BF)
    table = jnp.concatenate(turn, axis=0)
    high = table.astype(BF)
    act_ref[D : D + HD, :] = high
    act_ref[D + HD :, :] = (table - high.astype(F32)).astype(BF)
    first_len = jnp.sum((seg_ref[...] == 0).astype(F32), axis=1, keepdims=True)
    out_ref[TOK:, :] = jnp.broadcast_to(first_len, (16, 2 * KVW)).astype(BF)


def queries_kernel(x_ref, gain_ref, cos_ref, sin_ref, weight_ref, act_ref, out_ref):
    x = x_ref[...].astype(F32)
    act = (x * inverse_rms(x) * column(gain_ref)).astype(BF)
    act_ref[...] = act
    queries = mm(weight_ref[...], act, TN)
    turn = (cos_ref[...], sin_ref[...])
    for head in range(H):
        rows = slice(head * HD, (head + 1) * HD)
        low = rotated(queries[rows], turn, 1.0).astype(BF)
        out_ref[rows, :] = low * jnp.asarray(SCALE, BF)


def mlp_kernel(
    scalars, x_ref, c_ref, attn_ref, gain_ref, out_weight, gate_ref, up_ref, down_ref,
    result_ref, dmid_ref, dattn_ref, ggain_ref, mine_ref, other_ref,
    mid, act, act_cols, c_cols, result, dact, shards, sems,
):
    block = pl.program_id(0)
    my_c = scalars[5]

    def put(group, values):
        for k in range(values.shape[1] // 128):
            for i in range(values.shape[0] // SHARD):
                j = k * (values.shape[0] // SHARD) + i
                piece = values[i * SHARD : (i + 1) * SHARD, k * 128 : (k + 1) * 128]
                shards[group + j // 8, j % 8] = piece

    def send(group):
        @pl.when(group // 16 == my_c)
        def _():
            pltpu.make_async_copy(shards.at[group], mine_ref.at[group % 16], sems.at[0]).start()

        @pl.when(group // 16 != my_c)
        def _():
            pltpu.make_async_copy(shards.at[group], other_ref.at[group % 16], sems.at[1]).start()

    @pl.when(block == 0)
    def _():
        low = attn_ref[...].astype(BF)
        middle = x_ref[...].astype(F32) + mm(out_weight[...], low, TN)
        mid[...] = middle
        normal = (middle * inverse_rms(middle) * column(gain_ref)).astype(BF)
        act_cols[...] = normal
        act[...] = jnp.transpose(normal)
        c_cols[...] = jnp.transpose(c_ref[...])
        result[...] = jnp.zeros_like(result)
        dact[...] = jnp.zeros_like(dact)

    gate = mm(act[...], gate_ref[...])
    up = mm(act[...], up_ref[...])
    sigmoid = 1.0 / (1.0 + jnp.exp(-gate))
    silu = gate * sigmoid
    hidden = (silu * up).astype(BF)
    dhidden = mm(c_cols[...], down_ref[...])
    dup = (dhidden * silu).astype(BF)
    dgate = (dhidden * up * (sigmoid * (1.0 + gate * (1.0 - sigmoid)))).astype(BF)
    result[...] += mm(down_ref[...], hidden, NT)
    put(block * 9, mm(act_cols[...], dgate).astype(BF))
    put(block * 9 + 3, mm(act_cols[...], dup).astype(BF))
    put(block * 9 + 6, mm(c_ref[...], hidden).astype(BF))
    for group in range(9):
        send(block * 9 + group)
    dact[...] += mm(gate_ref[...], dgate, NT) + mm(up_ref[...], dup, NT)

    @pl.when(block == FF // FF_BLOCK - 1)
    def _():
        middle = mid[...]
        gain = column(gain_ref)
        rms = inverse_rms(middle)
        grads = dact[...]
        result_ref[...] = (middle + result[...]).astype(BF)
        ggain_ref[...] = row_sums(grads * middle * rms)
        pulled = grads * gain
        inner = jnp.mean(pulled * middle, axis=0, keepdims=True)
        dmid = c_ref[...].astype(F32) + (pulled * rms - middle * (rms * rms * rms * inner))
        dmid_ref[...] = dmid
        low = dmid.astype(BF)
        dattn_ref[...] = mm(out_weight[...], low).astype(BF)
        gout = mm(attn_ref[...].astype(BF), low, NT).astype(BF)
        put(27, gout[:, :512])
        shards[30:32] = jnp.zeros((2, 8, SHARD, 128), BF)
        put(30, jnp.concatenate([gout[: D // 2, 512:], gout[D // 2 :, 512:]], axis=1))
        for group in range(27, 32):
            send(group)
        for i, ref in enumerate((mine_ref, other_ref)):
            pltpu.make_async_copy(ref, ref, sems.at[i]).wait()


def feed_forward(scalars, x, cotangent, attended, gain, out_weight, gate_weight, up_weight, down_weight):
    whole = lambda *dims: pl.BlockSpec(dims, lambda f: (0,) * len(dims))
    part = pl.BlockSpec((D, FF_BLOCK), lambda f: (0, f))
    return pl.pallas_call(
        mlp_kernel,
        grid=(FF // FF_BLOCK,),
        out_shape=(shape(D, TOK), shape(D, TOK, dtype=F32), shape(D, TOK), shape(16, D, dtype=F32))
        + (shape(GROUPS // 2, 8, SHARD, 128),) * 2,
        in_specs=[smem(), whole(D, TOK), whole(D, TOK), whole(D, TOK), whole(D), whole(D, D), part, part, part],
        out_specs=(whole(D, TOK), whole(D, TOK), whole(D, TOK), whole(16, D))
        + (pl.BlockSpec(memory_space=pl.ANY),) * 2,
        scratch_shapes=[
            pltpu.VMEM((D, TOK), F32), pltpu.VMEM((TOK, D), BF), pltpu.VMEM((D, TOK), BF),
            pltpu.VMEM((TOK, D), BF), pltpu.VMEM((D, TOK), F32), pltpu.VMEM((D, TOK), F32),
            pltpu.VMEM((GROUPS, 8, SHARD, 128), BF), pltpu.SemaphoreType.DMA((2,)),
        ],
        compiler_params=pltpu.CompilerParams(vmem_limit_bytes=56 * 1024 * 1024),
        cost_estimate=pl.CostEstimate(flops=5 * 10**9, bytes_accessed=14 * 10**6, transcendentals=10**6),
        name="feed_forward",
    )(scalars, x, cotangent, attended, gain, out_weight, gate_weight, up_weight, down_weight)


def early_finish_kernel(shards, gate_ref, up_ref, down_ref, out_ref):
    block = pl.program_id(0)

    def get(group, k):
        pieces = []
        for i in range(D // SHARD):
            piece = group * 8 + D // SHARD * k + i
            half, piece = piece // (GROUPS * 4), piece % (GROUPS * 4)
            pieces.append(shards[piece // 2, half, piece % 2])
        return jnp.concatenate(pieces, axis=0).astype(F32)

    for kind, ref in enumerate((gate_ref, up_ref, down_ref)):
        for k in range(4):
            ref[:, k * 128 : (k + 1) * 128] = get(block * 9 + kind * 3, k)

    @pl.when(block == FF // FF_BLOCK - 1)
    def _():
        for k in range(4):
            out_ref[:, k * 128 : (k + 1) * 128] = get(27, k)
        rest = get(30, 0)[: D // 2]
        out_ref[:, 512:] = jnp.concatenate([rest[:, :HD], rest[:, HD:]], axis=0)


def early_finish(shards):
    part = pl.BlockSpec((D, FF_BLOCK), lambda f: (0, f))
    return pl.pallas_call(
        early_finish_kernel,
        grid=(FF // FF_BLOCK,),
        out_shape=(shape(D, FF, dtype=F32),) * 3 + (shape(D, D, dtype=F32),),
        in_specs=[pl.BlockSpec(shards.shape, lambda f: (0,) * 5)],
        out_specs=(part, part, part, pl.BlockSpec((D, D), lambda f: (0, 0))),
        compiler_params=pltpu.CompilerParams(vmem_limit_bytes=56 * 1024 * 1024),
        cost_estimate=pl.CostEstimate(flops=10**7, bytes_accessed=19 * 10**6, transcendentals=0),
        name="early_gradients",
    )(shards)


def late_rows():
    return 0, 2592, 4320, 4400


def pack(buffer, at, values):
    count = values.shape[0]
    for k in range(4):
        buffer[at + k * count : at + (k + 1) * count, :] = values[:, k * 128 : (k + 1) * 128]
    if count > 16:
        rest = jnp.concatenate([values[: count // 2, 512:], values[count // 2 :, 512:]], axis=1)
        buffer[at + 4 * count : at + 4 * count + count // 2, :] = rest
    else:
        buffer[at + 4 * count : at + 5 * count, 0:64] = values[:, 512:]


def unpack(buffer, at, count):
    blocks = [buffer[at + k * count : at + (k + 1) * count, :] for k in range(4)]
    if count > 16:
        rest = buffer[at + 4 * count : at + 4 * count + count // 2, :]
        rest = jnp.concatenate([rest[:, :64], rest[:, 64:]], axis=0)
    else:
        rest = buffer[at + 4 * count : at + 5 * count, 0:64]
    return jnp.concatenate(blocks + [rest], axis=1)


def late_kernel(
    scalars, acts_ref, first_mine, second_mine, first_other, second_other, dq_ref, cos_ref, sin_ref, act_ref, weight_ref,
    key_ref, value_ref, gain_ref, ggain_ref, dact_ref, mine_ref, other_ref, late, gkv,
):
    block = pl.program_id(0)
    my_x, my_z, my_c = scalars[3], scalars[4], scalars[5]

    @pl.when(block == 0)
    def _():
        gkv[...] = jnp.zeros_like(gkv)

    total = None
    for kz in range(4):
        z = (my_z + kz) & 3
        mz = (3 - z - my_z) & 3
        for core, first_ref, second_ref in ((my_c, first_mine, second_other), (1 - my_c, first_other, second_mine)):
            unit = z * 2 + core
            first, second = first_ref[0, 0, kz], second_ref[0, mz, 0]
            table = acts_ref[unit, D:, :].astype(F32)
            table = table[0:HD] + table[HD:]
            turn = (table[0:HALF], table[HALF:])
            turned = []
            for g in range(KVH):
                rows = slice(g * CHUNK, (g + 1) * CHUNK)
                grads = jnp.concatenate([jnp.transpose(first[rows]), jnp.transpose(second[rows])], axis=1)
                turned.append(rotated(grads[0:HD].astype(F32), turn, -1.0).astype(BF))
                turned.append(grads[HD:])
            product = mm(acts_ref[unit, 0:D, :], jnp.concatenate(turned, axis=0), NT)
            total = product if total is None else total + product
    gkv[...] += total

    @pl.when(block == 3)
    def _():
        turn = (cos_ref[...], sin_ref[...])
        heads = [rotated(dq_ref[h * HD : (h + 1) * HD, :], turn, -1.0).astype(BF) for h in range(H)]
        low = jnp.concatenate(heads, axis=0)
        weight = weight_ref[...]
        gquery = mm(act_ref[...], low, NT)
        dact_ref[...] = mm(weight, low)
        at_q, at_kv, at_n, at_m = late_rows()
        late[at_n:, :] = jnp.zeros((32 * LATE_SHARD - at_n, 128), BF)
        pack(late, at_q, gquery.astype(BF))
        gain = row_sums(gquery * weight.astype(F32))
        for g in range(KVH):
            rows = slice(g * HD, (g + 1) * HD)
            grad = gkv[:, g * 128 : (g + 1) * 128]
            late[at_kv + g * D : at_kv + (g + 1) * D, :] = grad.astype(BF)
            columns = jnp.transpose(jnp.concatenate([key_ref[rows, :], value_ref[rows, :]], axis=0))
            gain = gain + row_sums(grad * columns.astype(F32))
        pack(late, at_n, (gain / gain_ref[...].reshape(1, D)).astype(BF))
        pack(late, at_m, ggain_ref[...].astype(BF))
        for x in range(4):
            for z in range(4):
                index = ((x - my_x) & 3, (z - my_z) & 3)
                for target, core in ((mine_ref, my_c), (other_ref, 1 - my_c)):
                    at = ((core * 4 + x) * 4 + z) * LATE_SHARD
                    target[index] = late[pl.ds(pl.multiple_of(at, LATE_SHARD), LATE_SHARD), :]


def late_gradients(scalars, acts, mine, other, *arrays):
    whole = lambda array: pl.BlockSpec(array.shape, lambda k, s: (0,) * len(array.shape))
    mirrored = lambda k, s: (3 - ((s[3] + k) & 3) - s[3]) & 3
    unit = (KVH * CHUNK, 128)
    first = pl.BlockSpec((1, 1, 4) + unit, lambda k, s: (0, k, 0, 0, 0))
    second = pl.BlockSpec((1, 4, 1) + unit, lambda k, s: (1, 0, mirrored(k, s), 0, 0))
    outs = (shape(D, TOK, dtype=F32),) + (shape(4, 4, LATE_SHARD, 128),) * 2
    return pl.pallas_call(
        late_kernel,
        grid_spec=pltpu.PrefetchScalarGridSpec(
            num_scalar_prefetch=1,
            grid=(4,),
            in_specs=[pl.BlockSpec((8, ACTR, TOK), lambda k, s: ((s[3] + k) & 3, 0, 0)), first, second, first, second]
            + [whole(array) for array in arrays],
            out_specs=tuple(whole(out) for out in outs),
            scratch_shapes=[pltpu.VMEM((32 * LATE_SHARD, 128), BF), pltpu.VMEM((D, 2 * KVW), F32)],
        ),
        out_shape=outs,
        compiler_params=pltpu.CompilerParams(vmem_limit_bytes=56 * 1024 * 1024),
        cost_estimate=pl.CostEstimate(flops=4 * 10**9, bytes_accessed=20 * 10**6, transcendentals=0),
        name="late_gradients",
    )(scalars, acts, mine, mine, other, other, *arrays)


def join_kernel(mine_ref, came_ref, late_mine, late_came, *outs):
    for k in range(4):
        for j in range(4):
            first, second = slice(0, LATE_SPLIT), slice(LATE_SPLIT, LATE_SHARD)
            outs[k][j, 0:KVR, :] = add(mine_ref[0, k, j], came_ref[0, k, j])
            outs[k][j, KVR:, :] = add(late_mine[k, j, first], late_came[k, j, first])
            outs[4 + k][j, 0:KVR, :] = add(mine_ref[1, k, j], came_ref[1, k, j])
            outs[4 + k][j, KVR:, :] = add(late_mine[j, k, second], late_came[j, k, second])


def late_finish_kernel(scalars, own_ref, came_ref, gquery_ref, gkey_ref, gvalue_ref, gnorm_ref, gmlp_ref, late):
    my_x, my_z, my_c = scalars[3], scalars[4], scalars[5]
    for source, core in ((own_ref, my_c), (came_ref, 1 - my_c)):
        for x in range(4):
            for z in range(4):
                at = ((core * 4 + ((my_x - x) & 3)) * 4 + ((my_z - z) & 3)) * LATE_SHARD
                late[pl.ds(pl.multiple_of(at, LATE_SHARD), LATE_SHARD), :] = source[x, z]
    at_q, at_kv, at_n, at_m = late_rows()
    gquery_ref[...] = unpack(late, at_q, D).astype(F32)
    for g in range(KVH):
        grad = jnp.transpose(late[at_kv + g * D : at_kv + (g + 1) * D, :].astype(F32))
        gkey_ref[g * HD : (g + 1) * HD, :] = grad[:HD]
        gvalue_ref[g * HD : (g + 1) * HD, :] = grad[HD:]
    gnorm_ref[...] = unpack(late, at_n, 16).astype(F32)[0]
    gmlp_ref[...] = unpack(late, at_m, 16).astype(F32)[0]


def tail_kernel(
    a0, a1, a2, a3, b0, b1, b2, b3, cos_ref, sin_ref, x_ref, gain_ref, key_ref, value_ref, dact_ref, dmid_ref, grad_ref
):
    turn = (cos_ref[...], sin_ref[...])
    summed = []
    for parts in ((a0, a1, a2, a3), (b0, b1, b2, b3)):
        total = parts[0][0 : KVR, :].astype(F32)
        for part in parts[1:]:
            total = total + part[0 : KVR, :].astype(F32)
        summed.append(total)
    keys, values = [], []
    for g in range(KVH):
        columns = [jnp.transpose(t[g * CHUNK : (g + 1) * CHUNK, :]) for t in summed]
        columns = jnp.concatenate(columns, axis=1)
        keys.append(rotated(columns[:HD], turn, -1.0).astype(BF))
        values.append(columns[HD:].astype(BF))
    keys, values = jnp.concatenate(keys, axis=0), jnp.concatenate(values, axis=0)
    grads = dact_ref[...] + mm(key_ref[...], keys, TN) + mm(value_ref[...], values, TN)
    x = x_ref[...].astype(F32)
    rms = inverse_rms(x)
    pulled = grads * column(gain_ref)
    inner = jnp.mean(pulled * x, axis=0, keepdims=True)
    grad_ref[...] = (dmid_ref[...] + (pulled * rms - x * (rms * rms * rms * inner))).astype(BF)


def shift(values, axis, by):
    return lax.ppermute(values, axis, [(i, (i + by) % 4) for i in range(4)])


def swap(values):
    return lax.ppermute(values, "core", [(0, 1), (1, 0)])


def mirror(values):
    return lax.ppermute(values, SEQ, [(i, UNITS - 1 - i) for i in range(UNITS)])


def zigzag(values):
    return jnp.concatenate([values[:, :CHUNK], mirror(values[:, CHUNK:])], axis=1)


def add(*parts):
    parts = [p.astype(F32) for p in parts]
    total = parts[0] + parts[1] if len(parts) == 2 else (parts[0] + parts[2]) + (parts[1] + parts[3])
    return total.astype(BF)


def spread(parts, axis):
    return [parts[0]] + [shift(parts[k], axis, k) for k in (1, 2, 3)]


def collect(values, axis):
    return [values] + [shift(values, axis, k) for k in (1, 2, 3)]


def turns(places):
    freqs = ROPE_BASE ** (-2.0 * jnp.arange(HALF).astype(F32) / HD)
    angles = freqs[:, None] * places.astype(F32)
    return jnp.cos(angles), jnp.sin(angles)


def body(
    tokens,
    segments,
    positions,
    norm_gain,
    query_weight,
    key_weight,
    value_weight,
    output_weight,
    mlp_gain,
    gate_weight,
    up_weight,
    down_weight,
    cotangent,
):
    axis = {name: lax.axis_index(name) for name in ALL}
    at = {name: index.reshape(1) for name, index in axis.items()}
    unit = (axis["x"] * 4 + axis["z"]) * 2 + axis["core"]
    x_own = tokens[0].T
    key_cols, value_cols, down_cols = key_weight.T, value_weight.T, down_weight.T

    packed, own_act = call(
        keys_kernel, "keys_values", (shape(PADROWS, 2 * KVW), shape(ACTR, TOK)), None,
        (x_own, norm_gain, *turns(positions), key_cols, value_cols, segments),
    )
    gathered = lax.all_gather(packed, SEQ, axis=0, tiled=False)
    acts = lax.all_gather(own_act, SEQ, axis=0, tiled=False)
    x_own, segments, positions, packed = lax.optimization_barrier((x_own, segments, positions, packed))

    third = TOK * unit + jnp.sum((segments < 2).astype(jnp.int32))
    marks = jnp.where(segments == 2, third, jnp.where(segments == 1, -64, 0))
    ints = jnp.concatenate([positions >> 6, positions & 63, marks >> 6, marks & 63], axis=0)
    ints = jnp.pad(ints, ((0, 12), (0, 0))).astype(BF)
    both = zigzag(jnp.concatenate([x_own, cotangent[0].T, ints], axis=0))
    x, out_grad = both[:D], both[D : 2 * D]
    ints = both[2 * D :].astype(jnp.int32)
    places = ints[0:1] * 64 + ints[1:2]
    marks = ints[2:3] * 64 + ints[3:4]
    marks = jnp.broadcast_to(marks.reshape(2, 1, CHUNK), (2, 8, CHUNK))
    chunk_a, chunk_b = 2 * unit, 2 * UNITS - 1 - 2 * unit
    scalars = jnp.stack([
        (chunk_a > chunk_b).astype(jnp.int32), jnp.minimum(chunk_a, chunk_b), jnp.maximum(chunk_a, chunk_b),
        axis["x"], axis["z"], axis["core"], axis["dp"],
    ])
    turn = turns(places)
    act, queries = call(
        queries_kernel, "queries", (shape(D, TOK), shape(D, TOK)), None, (x, norm_gain, *turn, query_weight)
    )

    attended, norm = attend(scalars, marks, queries, gathered)
    result, dmid, dattn, ggain, mine, other = feed_forward(
        scalars, x, out_grad, attended, mlp_gain, output_weight, gate_weight, up_weight, down_cols
    )

    early = add(mine, swap(other))
    early, dattn, result = lax.optimization_barrier((early, dattn, result))
    early = lax.all_to_all(early.reshape(64, 2, SHARD, 128), CHIPS, 0, 0, tiled=True)

    dq, mine, other = attend_back(scalars, marks, queries, dattn, attended, norm, gathered)
    early = jnp.sum(early.astype(F32), axis=0).astype(BF)
    result = zigzag(result)
    other, early, result = lax.optimization_barrier((other, early, result))
    early = lax.all_gather(early, ALL, axis=0, tiled=False)

    came = swap(other)
    dact, late_mine, late_other = late_gradients(
        scalars, acts, mine, other, dq, *turn, act, query_weight, key_cols, value_cols, norm_gain, ggain
    )
    halves = call(
        join_kernel, "join",
        (shape(4, KVR + LATE_SPLIT, 128),) * 4 + (shape(4, KVR + LATE_SHARD - LATE_SPLIT, 128),) * 4, None,
        (mine, came, late_mine, swap(late_other)),
    )
    first_came, second_came = spread(halves[:4], "x"), spread(halves[4:], "z")
    first = [add(*(c[k] for c in first_came)) for k in range(4)]
    second = [add(*(c[k] for c in second_came)) for k in range(4)]
    first, second = lax.optimization_barrier((first, second))
    first_came, second_came = spread(first, "z"), spread(second, "x")
    late = jnp.concatenate(
        [add(*(part[KVR:] for part in first_came)), add(*(part[KVR:] for part in second_came))], axis=0
    )
    late_came = collect(late, "dp")
    input_grad = call(
        tail_kernel, "tail", shape(D, TOK), None,
        (*first_came, *second_came, *turn, x, norm_gain, key_cols, value_cols, dact, dmid),
    )
    late = add(*late_came)
    late, input_grad = lax.optimization_barrier((late, input_grad))
    late = jnp.stack(collect(late, "z"))
    late_came = collect(late, "x")
    input_grad = zigzag(input_grad)
    early = early_finish(early.reshape(64, 2, 2, SHARD, 128))
    late_came, input_grad, early = lax.optimization_barrier((late_came, input_grad, early))
    late = jnp.stack(late_came)
    late = call(
        late_finish_kernel, "late_finish",
        (shape(D, D, dtype=F32), shape(KVW, D, dtype=F32), shape(KVW, D, dtype=F32)) + (shape(D, dtype=F32),) * 2,
        scalars, (late, swap(late)), (pltpu.VMEM((32 * LATE_SHARD, 128), BF),),
    )
    return (
        result.T[None],
        input_grad.T[None],
        late[3],
        late[0],
        late[1].T,
        late[2].T,
        early[3],
        late[4],
        early[0],
        early[1],
        early[2].T,
    )


def solution(mesh):
    inner = Mesh(mesh.devices.reshape(4, 4, 4, 2), ALL)
    row = P("dp", SEQ, None)
    flat = P("dp", SEQ)
    return jax.shard_map(
        body,
        mesh=inner,
        in_specs=(row, flat, flat) + (P(),) * 9 + (row,),
        out_specs=(row, row) + (P(),) * 9,
        check_vma=False,
    )
```

```python
from functools import partial

import jax
import jax.numpy as jnp
from jax import lax
from jax.experimental import pallas as pl
from jax.experimental.pallas import tpu as pltpu
from jax.sharding import Mesh
from jax.sharding import PartitionSpec as P

D = 576
H = 9
KVH = 3
GROUP = H // KVH
HD = 64
HALF = HD // 2
FF = 1536
KVW = KVH * HD
EPSILON = 1e-05
ROPE_BASE = 10000.0
LOG2E = 1.4426950408889634
MASKED = -1e30
SCALE = HD**-0.5

TOK = 256
CHUNK = TOK // 2
UNITS = 32
COLS = GROUP * CHUNK
PADROWS = TOK + 16
SHARD = 96
GROUPS = 32
LATE_SHARD = 144
LATE_SPLIT = 80
KVR = KVH * CHUNK
FF_BLOCK = 512

SEQ = ("x", "z", "core")
ALL = ("dp", "x", "z", "core")
CHIPS = ("dp", "x", "z")
BF = jnp.bfloat16
F32 = jnp.float32

NT = (((1,), (1,)), ((), ()))
NN = (((1,), (0,)), ((), ()))
TN = (((0,), (0,)), ((), ()))


def mm(left, right, dims=NN):
    return lax.dot_general(left, right, dims, preferred_element_type=F32)


def vmem(count):
    return [pl.BlockSpec(memory_space=pltpu.VMEM)] * count


def smem():
    return pl.BlockSpec(memory_space=pltpu.SMEM)


def call(kernel, name, out_shape, scalars, arrays, scratch=(), flops=10**8, moved=10**6, left=0, left_out=0):
    outs = out_shape if isinstance(out_shape, (tuple, list)) else (out_shape,)
    given = ([] if scalars is None else [scalars]) + list(arrays)
    stay = [pl.BlockSpec(memory_space=pl.ANY)]
    specs = ([] if scalars is None else [smem()]) + vmem(len(arrays) - left) + stay * left
    out_specs = vmem(len(outs) - left_out) + stay * left_out
    return pl.pallas_call(
        kernel,
        out_shape=out_shape,
        in_specs=specs,
        out_specs=tuple(out_specs) if isinstance(out_shape, (tuple, list)) else out_specs[0],
        scratch_shapes=list(scratch),
        compiler_params=pltpu.CompilerParams(vmem_limit_bytes=56 * 1024 * 1024),
        cost_estimate=pl.CostEstimate(flops=flops, bytes_accessed=moved, transcendentals=0),
        name=name,
    )(*given)


def shape(*dims, dtype=BF):
    return jax.ShapeDtypeStruct(dims, dtype)


def column_info(scalars, marks_ref, kv_ref):
    lo_idx = scalars[0]
    first_len = kv_ref[0, TOK : TOK + 16, 0:128].astype(F32)[0:1, :].astype(jnp.int32)
    first_len = jnp.concatenate([first_len] * (2 * GROUP), axis=1)
    hi, lo = marks_ref[1 - lo_idx, 0:1, :], marks_ref[lo_idx, 0:1, :]
    marks = jnp.concatenate([hi] * GROUP + [lo] * GROUP, axis=1)
    first_key = jnp.where(marks < 0, first_len, marks)
    lane = lax.broadcasted_iota(jnp.int32, (1, 2 * COLS), 1)
    start = jnp.where(lane < COLS, scalars[2], scalars[1]) * CHUNK
    return first_key, start + lax.rem(lane, CHUNK)


def full_mask(tile, first_key, place, rows, cols):
    keys = tile * TOK + lax.broadcasted_iota(jnp.int32, (rows, cols), 0)
    return (keys >= first_key[:, :cols]) & (keys <= place[:, :cols])


def tiles(scalars, step, most, upper):
    lo_diag = scalars[1] // 2
    hi_diag = scalars[2] // 2
    joint = jnp.maximum(lo_diag - 1, 0)
    single = hi_diag - lo_diag - 1

    @pl.loop(0, jnp.where(lo_diag > 0, 2, 1))
    def _(j):
        step(j * lo_diag, 1, 2 * COLS, True)

    @pl.loop(0, joint // 2)
    def _(j):
        step(1 + 2 * j, 2, 2 * COLS, False)

    @pl.when(joint % 2 == 1)
    def _():
        step(lo_diag - 1, 1, 2 * COLS, False)

    upper()

    @pl.loop(0, single // most)
    def _(j):
        step(lo_diag + 1 + most * j, most, COLS, False)

    if most == 4:

        @pl.when(single % 4 == 2)
        def _():
            step(hi_diag - 2, 2, COLS, False)

    step(hi_diag, 1, COLS, True)


def gather_columns(cat_ref, source_ref, scalars, first_row):
    cat_ref[...] = jnp.zeros_like(cat_ref)
    lo_idx = scalars[0]
    for part in range(2):
        index = (1 - lo_idx) if part == 0 else lo_idx
        lanes = pl.ds(pl.multiple_of(index * CHUNK, CHUNK), CHUNK)
        for head in range(H):
            at = part * COLS + (head % GROUP) * CHUNK
            block = source_ref[head * HD : (head + 1) * HD, lanes]
            cat_ref[head // GROUP, first_row : first_row + HD, at : at + CHUNK] = block


def scatter_columns(out_ref, values, group, scalars):
    lo_idx = scalars[0]
    for part in range(2):
        index = (1 - lo_idx) if part == 0 else lo_idx
        lanes = pl.ds(pl.multiple_of(index * CHUNK, CHUNK), CHUNK)
        for j in range(GROUP):
            head = group * GROUP + j
            at = part * COLS + j * CHUNK
            out_ref[head * HD : (head + 1) * HD, lanes] = values[:, at : at + CHUNK]


def fetch(source, target, sems):
    half = UNITS // 2
    copies = [
        pltpu.make_async_copy(source.at[pl.ds(i * half, half)], target.at[pl.ds(i * half, half)], sems.at[i])
        for i in range(2)
    ]
    for copy in copies:
        copy.start()
    return copies[0].wait, copies[1].wait


def forward_kernel(scalars, marks_ref, q_ref, kv_hbm, out_ref, lse_ref, qcat, acc, run_max, kv_ref, sems):
    lower, upper = fetch(kv_hbm, kv_ref, sems)
    gather_columns(qcat, q_ref, scalars, 0)
    lower()
    first_key, place = column_info(scalars, marks_ref, kv_ref)
    acc[...] = jnp.zeros_like(acc)
    run_max[...] = jnp.full_like(run_max, MASKED)

    def step(tile, count, cols, whole):
        rows = count * TOK
        if whole:
            allowed = full_mask(tile, first_key, place, rows, cols)
        else:
            seen = first_key[:, :cols] <= tile * TOK
        blocks = [kv_ref[pl.ds(tile, count), 0:TOK, g * 128 : (g + 1) * 128].reshape(rows, 128) for g in range(KVH)]
        all_scores = [mm(blocks[g], qcat[g, :, 0:cols]) * LOG2E for g in range(KVH)]
        all_values = [
            jnp.concatenate([jnp.ones((16, rows), BF), jnp.transpose(block)[HD:, :]], axis=0) for block in blocks
        ]
        factors, all_weights = [], []
        for g in range(KVH):
            scores = all_scores[g]
            old_max = run_max[g, 0:1, 0:cols]
            if whole:
                scores = jnp.where(allowed, scores, MASKED)
                new_max = jnp.maximum(old_max, jnp.max(scores, axis=0, keepdims=True))
                shift = new_max
            else:
                new_max = jnp.maximum(old_max, jnp.max(scores, axis=0, keepdims=True))
                new_max = jnp.where(seen, new_max, old_max)
                shift = jnp.where(seen, new_max, -MASKED)
            all_weights.append(jnp.exp2(scores - shift).astype(BF))
            factors.append(jnp.exp2(old_max - new_max))
            run_max[g, 0:1, 0:cols] = new_max
        for g in range(KVH):
            acc[g, :, 0:cols] = acc[g, :, 0:cols] * factors[g] + mm(all_values[g], all_weights[g])

    tiles(scalars, step, 4, upper)
    for g in range(KVH):
        total = acc[g, 0:1, :]
        scatter_columns(out_ref, acc[g, 16:, :] / total, g, scalars)
        lse_ref[g] = jnp.broadcast_to(run_max[g, 0:1, :] + jnp.log2(total), (8, 2 * COLS))


def backward_kernel(
    scalars, marks_ref, q_ref, do_ref, out_ref, lse_ref, kv_hbm, dq_ref, mine_ref, other_ref,
    qcat, docat, acc, delta, kv_ref, grads_ref, sems,
):
    lower, upper = fetch(kv_hbm, kv_ref, sems)
    gather_columns(qcat, q_ref, scalars, 0)
    gather_columns(docat, do_ref, scalars, HD)
    lower()
    first_key, place = column_info(scalars, marks_ref, kv_ref)
    lo_idx = scalars[0]
    hi_diag = scalars[2] // 2
    my_x, my_z, my_c = scalars[3], scalars[4], scalars[5]
    acc[...] = jnp.zeros_like(acc)
    for part in range(2):
        index = (1 - lo_idx) if part == 0 else lo_idx
        lanes = pl.ds(pl.multiple_of(index * CHUNK, CHUNK), CHUNK)
        for head in range(H):
            rows = slice(head * HD, (head + 1) * HD)
            at = part * COLS + (head % GROUP) * CHUNK
            terms = do_ref[rows, lanes].astype(F32) * out_ref[rows, lanes]
            delta[head // GROUP, 0:1, at : at + CHUNK] = jnp.sum(terms, axis=0, keepdims=True)

    def store(tile, grads):
        mirrored = UNITS - 1 - tile
        kx, kz = (tile // 8 - my_x) & 3, ((tile // 2) % 4 - my_z) & 3
        mx, mz = (mirrored // 8 - my_x) & 3, ((mirrored // 2) % 4 - my_z) & 3
        same = lax.rem(tile, 2) == my_c

        for half in range(2):
            for g, grad in enumerate(grads):
                rows = slice(g * CHUNK, (g + 1) * CHUNK)
                grads_ref[tile, half, rows, :] = grad[half * CHUNK : (half + 1) * CHUNK]

        def send(first_ref, second_ref):
            pltpu.make_async_copy(grads_ref.at[tile, 0], first_ref.at[0, kx, kz], sems.at[2]).start()
            pltpu.make_async_copy(grads_ref.at[tile, 1], second_ref.at[1, mz, mx], sems.at[2]).start()

        @pl.when(same)
        def _():
            send(mine_ref, other_ref)

        @pl.when(jnp.logical_not(same))
        def _():
            send(other_ref, mine_ref)

    def step(tile, count, cols, whole):
        rows = count * TOK
        if whole:
            allowed = full_mask(tile, first_key, place, rows, cols)
        else:
            seen = first_key[:, :cols] <= tile * TOK
        all_grads, all_probs, all_grad_scores = [], [], []
        blocks = [kv_ref[pl.ds(tile, count), 0:TOK, g * 128 : (g + 1) * 128].reshape(rows, 128) for g in range(KVH)]
        all_scores = [mm(blocks[g], qcat[g, :, 0:cols]) * LOG2E for g in range(KVH)]
        all_grad_probs = [mm(blocks[g], docat[g, :, 0:cols]) for g in range(KVH)]
        for g in range(KVH):
            scores = all_scores[g]
            shift = lse_ref[g, 0:1, 0:cols]
            if whole:
                scores = jnp.where(allowed, scores, MASKED)
            else:
                shift = jnp.where(seen, shift, -MASKED)
            probs = jnp.exp2(scores - shift)
            all_grad_scores.append((probs * (all_grad_probs[g] - delta[g, 0:1, 0:cols])).astype(BF))
            all_probs.append(probs.astype(BF))
        for g in range(KVH):
            all_grads.append(
                mm(all_grad_scores[g], qcat[g, :, 0:cols], NT) + mm(all_probs[g], docat[g, :, 0:cols], NT)
            )
            keys = jnp.transpose(blocks[g])[0:HD, :]
            acc[g, :, 0:cols] = acc[g, :, 0:cols] + mm(keys, all_grad_scores[g])
        for i in range(count):
            store(tile + i, [grad[i * TOK : (i + 1) * TOK].astype(BF) for grad in all_grads])

    tiles(scalars, step, 2, upper)

    @pl.loop(hi_diag + 1, UNITS)
    def _(t):
        store(t, [jnp.zeros((TOK, 128), BF)] * KVH)

    for g in range(KVH):
        scatter_columns(dq_ref, acc[g] * SCALE, g, scalars)
    pltpu.make_async_copy(grads_ref, grads_ref, sems.at[2]).wait()


def attend(scalars, marks, queries, keys_values):
    return call(
        forward_kernel,
        "attention_forward",
        (shape(D, TOK, dtype=F32), shape(KVH, 8, 2 * COLS, dtype=F32)),
        scalars,
        (marks, queries, keys_values),
        (
            pltpu.VMEM((KVH, 128, 2 * COLS), BF),
            pltpu.VMEM((KVH, 16 + HD, 2 * COLS), F32),
            pltpu.VMEM((KVH, 8, 2 * COLS), F32),
            pltpu.VMEM(keys_values.shape, BF),
            pltpu.SemaphoreType.DMA((2,)),
        ),
        flops=20 * 10**9,
        moved=7 * 10**6,
        left=1,
    )


def attend_back(scalars, marks, queries, grad_out, attended, norm, keys_values):
    blocks = shape(2, 4, 4, KVH * CHUNK, 128)
    return call(
        backward_kernel,
        "attention_backward",
        (shape(D, TOK, dtype=F32), blocks, blocks),
        scalars,
        (marks, queries, grad_out, attended, norm, keys_values),
        (
            pltpu.VMEM((KVH, 128, 2 * COLS), BF),
            pltpu.VMEM((KVH, 128, 2 * COLS), BF),
            pltpu.VMEM((KVH, HD, 2 * COLS), F32),
            pltpu.VMEM((KVH, 8, 2 * COLS), F32),
            pltpu.VMEM(keys_values.shape, BF),
            pltpu.VMEM((UNITS, 2, KVR, 128), BF),
            pltpu.SemaphoreType.DMA((3,)),
        ),
        left=1,
        left_out=2,
        flops=40 * 10**9,
        moved=24 * 10**6,
    )


def inverse_rms(values):
    return lax.rsqrt(jnp.mean(values * values, axis=0, keepdims=True) + EPSILON)


def rotated(values, turn, sign):
    cosine, sine = turn[0], turn[1] * sign
    first, second = values[:HALF], values[HALF:]
    return jnp.concatenate([first * cosine - second * sine, second * cosine + first * sine], axis=0)


def row_sums(values):
    ones = jnp.ones((16, values.shape[1]), BF)
    high = values.astype(BF)
    low = (values - high.astype(F32)).astype(BF)
    return mm(ones, high, NT) + mm(ones, low, NT)


def column(ref):
    row = ref[...].reshape(1, ref.shape[0])
    return jnp.transpose(jnp.broadcast_to(row, (8, ref.shape[0])))[:, 0:1]


def keys_kernel(x_ref, gain_ref, cos_ref, sin_ref, key_ref, value_ref, seg_ref, place_ref, out_ref, act_ref):
    x = x_ref[...].astype(F32)
    act = (x * inverse_rms(x) * column(gain_ref)).astype(BF)
    act_ref[...] = act
    keys = mm(key_ref[...], act)
    values = mm(value_ref[...], act)
    turn = (cos_ref[...], sin_ref[...])
    for g in range(KVH):
        rows = slice(g * HD, (g + 1) * HD)
        block = jnp.concatenate([rotated(keys[rows], turn, 1.0), values[rows]], axis=0)
        out_ref[0:TOK, g * 128 : (g + 1) * 128] = jnp.transpose(block).astype(BF)
    first_len = jnp.sum((seg_ref[...] == 0).astype(F32), axis=1, keepdims=True)
    row = lax.broadcasted_iota(jnp.int32, (16, TOK), 0)
    places = place_ref[...]
    places = jnp.where(row < 12, places >> 6, places & 63).astype(F32)
    out_ref[TOK:, 0:TOK] = jnp.where(row < 8, first_len, places).astype(BF)
    out_ref[TOK:, TOK:] = jnp.zeros((16, 2 * KVW - TOK), BF)


def queries_kernel(x_ref, gain_ref, cos_ref, sin_ref, weight_ref, act_ref, out_ref):
    x = x_ref[...].astype(F32)
    act = (x * inverse_rms(x) * column(gain_ref)).astype(BF)
    act_ref[...] = act
    queries = mm(weight_ref[...], act, TN)
    turn = (cos_ref[...], sin_ref[...])
    for head in range(H):
        rows = slice(head * HD, (head + 1) * HD)
        low = rotated(queries[rows], turn, 1.0).astype(BF)
        out_ref[rows, :] = low * jnp.asarray(SCALE, BF)


def mlp_kernel(
    scalars, x_ref, c_ref, attn_ref, gain_ref, out_weight, gate_ref, up_ref, down_ref,
    result_ref, dmid_ref, dattn_ref, ggain_ref, mine_ref, other_ref,
    mid, act, act_cols, c_cols, result, dact, shards, sems,
):
    block = pl.program_id(0)
    my_c = scalars[5]

    def put(group, values):
        for k in range(values.shape[1] // 128):
            for i in range(values.shape[0] // SHARD):
                j = k * (values.shape[0] // SHARD) + i
                piece = values[i * SHARD : (i + 1) * SHARD, k * 128 : (k + 1) * 128]
                shards[group + j // 8, j % 8] = piece

    def send(group):
        @pl.when(group // 16 == my_c)
        def _():
            pltpu.make_async_copy(shards.at[group], mine_ref.at[group % 16], sems.at[0]).start()

        @pl.when(group // 16 != my_c)
        def _():
            pltpu.make_async_copy(shards.at[group], other_ref.at[group % 16], sems.at[1]).start()

    @pl.when(block == 0)
    def _():
        low = attn_ref[...].astype(BF)
        middle = x_ref[...].astype(F32) + mm(out_weight[...], low, TN)
        mid[...] = middle
        normal = (middle * inverse_rms(middle) * column(gain_ref)).astype(BF)
        act_cols[...] = normal
        act[...] = jnp.transpose(normal)
        c_cols[...] = jnp.transpose(c_ref[...])
        result[...] = jnp.zeros_like(result)
        dact[...] = jnp.zeros_like(dact)

    gate = mm(act[...], gate_ref[...])
    up = mm(act[...], up_ref[...])
    sigmoid = 1.0 / (1.0 + jnp.exp(-gate))
    silu = gate * sigmoid
    hidden = (silu * up).astype(BF)
    dhidden = mm(c_cols[...], down_ref[...])
    dup = (dhidden * silu).astype(BF)
    dgate = (dhidden * up * (sigmoid * (1.0 + gate * (1.0 - sigmoid)))).astype(BF)
    result[...] += mm(down_ref[...], hidden, NT)
    put(block * 9, mm(act_cols[...], dgate).astype(BF))
    put(block * 9 + 3, mm(act_cols[...], dup).astype(BF))
    put(block * 9 + 6, mm(c_ref[...], hidden).astype(BF))
    for group in range(9):
        send(block * 9 + group)
    dact[...] += mm(gate_ref[...], dgate, NT) + mm(up_ref[...], dup, NT)

    @pl.when(block == FF // FF_BLOCK - 1)
    def _():
        middle = mid[...]
        gain = column(gain_ref)
        rms = inverse_rms(middle)
        grads = dact[...]
        result_ref[...] = (middle + result[...]).astype(BF)
        ggain_ref[...] = row_sums(grads * middle * rms)
        pulled = grads * gain
        inner = jnp.mean(pulled * middle, axis=0, keepdims=True)
        dmid = c_ref[...].astype(F32) + (pulled * rms - middle * (rms * rms * rms * inner))
        dmid_ref[...] = dmid
        low = dmid.astype(BF)
        dattn_ref[...] = mm(out_weight[...], low).astype(BF)
        gout = mm(attn_ref[...].astype(BF), low, NT).astype(BF)
        put(27, gout[:, :512])
        shards[30:32] = jnp.zeros((2, 8, SHARD, 128), BF)
        put(30, jnp.concatenate([gout[: D // 2, 512:], gout[D // 2 :, 512:]], axis=1))
        for group in range(27, 32):
            send(group)
        for i, ref in enumerate((mine_ref, other_ref)):
            pltpu.make_async_copy(ref, ref, sems.at[i]).wait()


def feed_forward(scalars, x, cotangent, attended, gain, out_weight, gate_weight, up_weight, down_weight):
    whole = lambda *dims: pl.BlockSpec(dims, lambda f: (0,) * len(dims))
    part = pl.BlockSpec((D, FF_BLOCK), lambda f: (0, f))
    return pl.pallas_call(
        mlp_kernel,
        grid=(FF // FF_BLOCK,),
        out_shape=(shape(D, TOK), shape(D, TOK, dtype=F32), shape(D, TOK), shape(16, D, dtype=F32))
        + (shape(GROUPS // 2, 8, SHARD, 128),) * 2,
        in_specs=[smem(), whole(D, TOK), whole(D, TOK), whole(D, TOK), whole(D), whole(D, D), part, part, part],
        out_specs=(whole(D, TOK), whole(D, TOK), whole(D, TOK), whole(16, D))
        + (pl.BlockSpec(memory_space=pl.ANY),) * 2,
        scratch_shapes=[
            pltpu.VMEM((D, TOK), F32), pltpu.VMEM((TOK, D), BF), pltpu.VMEM((D, TOK), BF),
            pltpu.VMEM((TOK, D), BF), pltpu.VMEM((D, TOK), F32), pltpu.VMEM((D, TOK), F32),
            pltpu.VMEM((GROUPS, 8, SHARD, 128), BF), pltpu.SemaphoreType.DMA((2,)),
        ],
        compiler_params=pltpu.CompilerParams(vmem_limit_bytes=56 * 1024 * 1024),
        cost_estimate=pl.CostEstimate(flops=5 * 10**9, bytes_accessed=14 * 10**6, transcendentals=10**6),
        name="feed_forward",
    )(scalars, x, cotangent, attended, gain, out_weight, gate_weight, up_weight, down_weight)


def early_finish_kernel(scalars, source, gate_ref, up_ref, down_ref, out_ref, shards, sems):
    block = pl.program_id(0)
    my_y = scalars[6]

    def part(core, y):
        return shards.at[core, pl.ds(y * 16, 16)]

    @pl.when(block == 0)
    def _():
        for core in range(2):
            for k in range(4):
                y = (my_y - k) & 3
                pltpu.make_async_copy(source.at[:, core, k], part(core, y), sems.at[core, y]).start()

    needed = (((0, 0), (0, 1), (0, 2)), ((0, 3), (1, 0)), ((1, 1), (1, 2), (1, 3)))
    for step, places in enumerate(needed):

        @pl.when(block == step)
        def _():
            for core, y in places:
                pltpu.make_async_copy(part(core, y), part(core, y), sems.at[core, y]).wait()

    def get(group, k, i):
        piece = group * 8 + D // SHARD * k + i
        half, piece = piece // (GROUPS * 4), piece % (GROUPS * 4)
        return shards[half, piece // 2, piece % 2].astype(F32)

    for kind, ref in enumerate((gate_ref, up_ref, down_ref)):
        for k in range(4):
            for i in range(D // SHARD):
                ref[i * SHARD : (i + 1) * SHARD, k * 128 : (k + 1) * 128] = get(block * 9 + kind * 3, k, i)

    @pl.when(block == FF // FF_BLOCK - 1)
    def _():
        for k in range(4):
            for i in range(D // SHARD):
                out_ref[i * SHARD : (i + 1) * SHARD, k * 128 : (k + 1) * 128] = get(27, k, i)
        rest = jnp.concatenate([get(30, 0, i) for i in range(3)], axis=0)
        out_ref[:, 512:] = jnp.concatenate([rest[:, :HD], rest[:, HD:]], axis=0)


def early_finish(scalars, source):
    part = pl.BlockSpec((D, FF_BLOCK), lambda f: (0, f))
    return pl.pallas_call(
        early_finish_kernel,
        grid=(FF // FF_BLOCK,),
        out_shape=(shape(D, FF, dtype=F32),) * 3 + (shape(D, D, dtype=F32),),
        in_specs=[smem(), pl.BlockSpec(memory_space=pl.ANY)],
        out_specs=(part, part, part, pl.BlockSpec((D, D), lambda f: (0, 0))),
        scratch_shapes=[pltpu.VMEM((2, 64, 2, SHARD, 128), BF), pltpu.SemaphoreType.DMA((2, 4))],
        compiler_params=pltpu.CompilerParams(vmem_limit_bytes=56 * 1024 * 1024),
        cost_estimate=pl.CostEstimate(flops=10**7, bytes_accessed=19 * 10**6, transcendentals=0),
        name="early_gradients",
    )(scalars, source)


def late_rows():
    return 0, 2592, 4320, 4400


def pack(buffer, at, values):
    count = values.shape[0]
    for k in range(4):
        buffer[at + k * count : at + (k + 1) * count, :] = values[:, k * 128 : (k + 1) * 128]
    if count > 16:
        rest = jnp.concatenate([values[: count // 2, 512:], values[count // 2 :, 512:]], axis=1)
        buffer[at + 4 * count : at + 4 * count + count // 2, :] = rest
    else:
        buffer[at + 4 * count : at + 5 * count, 0:64] = values[:, 512:]


def unpack(buffer, at, count):
    blocks = [buffer[at + k * count : at + (k + 1) * count, :] for k in range(4)]
    if count > 16:
        rest = buffer[at + 4 * count : at + 4 * count + count // 2, :]
        rest = jnp.concatenate([rest[:, :64], rest[:, 64:]], axis=0)
    else:
        rest = buffer[at + 4 * count : at + 5 * count, 0:64]
    return jnp.concatenate(blocks + [rest], axis=1)


def late_kernel(
    scalars, acts_ref, cos_all, sin_all, first_mine, second_mine, first_other, second_other, dq_ref, cos_ref, sin_ref, act_ref, weight_ref,
    key_ref, value_ref, gain_ref, ggain_ref, dact_ref, mine_ref, other_ref, late, gkv,
):
    block = pl.program_id(0)
    my_x, my_z, my_c = scalars[3], scalars[4], scalars[5]

    @pl.when(block == 0)
    def _():
        gkv[...] = jnp.zeros_like(gkv)

    total = None
    for kz in range(4):
        z = (my_z + kz) & 3
        mz = (3 - z - my_z) & 3
        for core, first_ref, second_ref in ((my_c, first_mine, second_other), (1 - my_c, first_other, second_mine)):
            unit = z * 2 + core
            first, second = first_ref[0, 0, kz], second_ref[0, mz, 0]
            lanes = pl.ds(pl.multiple_of(unit * TOK, TOK), TOK)
            turn = (cos_all[:, lanes], sin_all[:, lanes])
            turned = []
            for g in range(KVH):
                rows = slice(g * CHUNK, (g + 1) * CHUNK)
                grads = jnp.concatenate([jnp.transpose(first[rows]), jnp.transpose(second[rows])], axis=1)
                turned.append(rotated(grads[0:HD].astype(F32), turn, -1.0).astype(BF))
                turned.append(grads[HD:])
            product = mm(acts_ref[unit], jnp.concatenate(turned, axis=0), NT)
            total = product if total is None else total + product
    gkv[...] += total

    @pl.when(block == 3)
    def _():
        turn = (cos_ref[...], sin_ref[...])
        heads = [rotated(dq_ref[h * HD : (h + 1) * HD, :], turn, -1.0).astype(BF) for h in range(H)]
        low = jnp.concatenate(heads, axis=0)
        weight = weight_ref[...]
        gquery = mm(act_ref[...], low, NT)
        dact_ref[...] = mm(weight, low)
        at_q, at_kv, at_n, at_m = late_rows()
        late[at_n:, :] = jnp.zeros((32 * LATE_SHARD - at_n, 128), BF)
        pack(late, at_q, gquery.astype(BF))
        gain = row_sums(gquery * weight.astype(F32))
        for g in range(KVH):
            rows = slice(g * HD, (g + 1) * HD)
            grad = gkv[:, g * 128 : (g + 1) * 128]
            late[at_kv + g * D : at_kv + (g + 1) * D, :] = grad.astype(BF)
            columns = jnp.transpose(jnp.concatenate([key_ref[rows, :], value_ref[rows, :]], axis=0))
            gain = gain + row_sums(grad * columns.astype(F32))
        pack(late, at_n, (gain / gain_ref[...].reshape(1, D)).astype(BF))
        pack(late, at_m, ggain_ref[...].astype(BF))
        for x in range(4):
            for z in range(4):
                index = ((x - my_x) & 3, (z - my_z) & 3)
                for target, core in ((mine_ref, my_c), (other_ref, 1 - my_c)):
                    at = ((core * 4 + x) * 4 + z) * LATE_SHARD
                    target[index] = late[pl.ds(pl.multiple_of(at, LATE_SHARD), LATE_SHARD), :]


def late_gradients(scalars, acts, table, mine, other, *arrays):
    whole = lambda array: pl.BlockSpec(array.shape, lambda k, s: (0,) * len(array.shape))
    mirrored = lambda k, s: (3 - ((s[3] + k) & 3) - s[3]) & 3
    unit = (KVH * CHUNK, 128)
    first = pl.BlockSpec((1, 1, 4) + unit, lambda k, s: (0, k, 0, 0, 0))
    second = pl.BlockSpec((1, 4, 1) + unit, lambda k, s: (1, 0, mirrored(k, s), 0, 0))
    outs = (shape(D, TOK, dtype=F32),) + (shape(4, 4, LATE_SHARD, 128),) * 2
    return pl.pallas_call(
        late_kernel,
        grid_spec=pltpu.PrefetchScalarGridSpec(
            num_scalar_prefetch=1,
            grid=(4,),
            in_specs=[pl.BlockSpec((8, D, TOK), lambda k, s: ((s[3] + k) & 3, 0, 0))]
            + [pl.BlockSpec((HALF, 8 * TOK), lambda k, s: (0, (s[3] + k) & 3))] * 2
            + [first, second, first, second]
            + [whole(array) for array in arrays],
            out_specs=tuple(whole(out) for out in outs),
            scratch_shapes=[pltpu.VMEM((32 * LATE_SHARD, 128), BF), pltpu.VMEM((D, 2 * KVW), F32)],
        ),
        out_shape=outs,
        compiler_params=pltpu.CompilerParams(vmem_limit_bytes=56 * 1024 * 1024),
        cost_estimate=pl.CostEstimate(flops=4 * 10**9, bytes_accessed=20 * 10**6, transcendentals=0),
        name="late_gradients",
    )(scalars, acts, *table, mine, mine, other, other, *arrays)


def join_kernel(mine_ref, came_ref, late_mine, late_came, *outs):
    j = pl.program_id(0)
    first, second = slice(0, LATE_SPLIT), slice(LATE_SPLIT, LATE_SHARD)
    for k in range(4):
        outs[k][0, 0:KVR, :] = add(mine_ref[0, k, 0], came_ref[0, k, 0])
        outs[k][0, KVR:, :] = add(late_mine[k, j, first], late_came[k, j, first])
        outs[4 + k][0, 0:KVR, :] = add(mine_ref[1, k, 0], came_ref[1, k, 0])
        outs[4 + k][0, KVR:, :] = add(late_mine[j, k, second], late_came[j, k, second])


def join(mine, came, late_mine, late_came):
    part = pl.BlockSpec((2, 4, 1, KVR, 128), lambda j: (0, 0, j, 0, 0))
    late = pl.BlockSpec(late_mine.shape, lambda j: (0, 0, 0, 0))
    heights = (KVR + LATE_SPLIT,) * 4 + (KVR + LATE_SHARD - LATE_SPLIT,) * 4
    return pl.pallas_call(
        join_kernel,
        grid=(4,),
        out_shape=tuple(shape(4, rows, 128) for rows in heights),
        in_specs=[part, part, late, late],
        out_specs=tuple(pl.BlockSpec((1, rows, 128), lambda j: (j, 0, 0)) for rows in heights),
        compiler_params=pltpu.CompilerParams(vmem_limit_bytes=56 * 1024 * 1024),
        cost_estimate=pl.CostEstimate(flops=10**7, bytes_accessed=11 * 10**6, transcendentals=0),
        name="join",
    )(mine, came, late_mine, late_came)


def late_finish_kernel(scalars, own_ref, came_ref, gquery_ref, gkey_ref, gvalue_ref, gnorm_ref, gmlp_ref, late):
    my_x, my_z, my_c = scalars[3], scalars[4], scalars[5]
    for source, core in ((own_ref, my_c), (came_ref, 1 - my_c)):
        for x in range(4):
            for z in range(4):
                at = ((core * 4 + ((my_x - x) & 3)) * 4 + ((my_z - z) & 3)) * LATE_SHARD
                late[pl.ds(pl.multiple_of(at, LATE_SHARD), LATE_SHARD), :] = source[x, z]
    at_q, at_kv, at_n, at_m = late_rows()
    gquery_ref[...] = unpack(late, at_q, D).astype(F32)
    for g in range(KVH):
        grad = jnp.transpose(late[at_kv + g * D : at_kv + (g + 1) * D, :].astype(F32))
        gkey_ref[g * HD : (g + 1) * HD, :] = grad[:HD]
        gvalue_ref[g * HD : (g + 1) * HD, :] = grad[HD:]
    gnorm_ref[...] = unpack(late, at_n, 16).astype(F32)[0]
    gmlp_ref[...] = unpack(late, at_m, 16).astype(F32)[0]


def tail_kernel(
    a0, a1, a2, a3, b0, b1, b2, b3, cos_ref, sin_ref, x_ref, gain_ref, key_ref, value_ref, dact_ref, dmid_ref, grad_ref
):
    turn = (cos_ref[...], sin_ref[...])
    summed = []
    for parts in ((a0, a1, a2, a3), (b0, b1, b2, b3)):
        total = parts[0][0 : KVR, :].astype(F32)
        for part in parts[1:]:
            total = total + part[0 : KVR, :].astype(F32)
        summed.append(total)
    keys, values = [], []
    for g in range(KVH):
        columns = [jnp.transpose(t[g * CHUNK : (g + 1) * CHUNK, :]) for t in summed]
        columns = jnp.concatenate(columns, axis=1)
        keys.append(rotated(columns[:HD], turn, -1.0).astype(BF))
        values.append(columns[HD:].astype(BF))
    keys, values = jnp.concatenate(keys, axis=0), jnp.concatenate(values, axis=0)
    grads = dact_ref[...] + mm(key_ref[...], keys, TN) + mm(value_ref[...], values, TN)
    x = x_ref[...].astype(F32)
    rms = inverse_rms(x)
    pulled = grads * column(gain_ref)
    inner = jnp.mean(pulled * x, axis=0, keepdims=True)
    grad_ref[...] = (dmid_ref[...] + (pulled * rms - x * (rms * rms * rms * inner))).astype(BF)


def shift(values, axis, by):
    return lax.ppermute(values, axis, [(i, (i + by) % 4) for i in range(4)])


def swap(values):
    return lax.ppermute(values, "core", [(0, 1), (1, 0)])


def mirror(values):
    return lax.ppermute(values, SEQ, [(i, UNITS - 1 - i) for i in range(UNITS)])


def zigzag(values):
    return jnp.concatenate([values[:, :CHUNK], mirror(values[:, CHUNK:])], axis=1)


def add(*parts):
    parts = [p.astype(F32) for p in parts]
    total = parts[0] + parts[1] if len(parts) == 2 else (parts[0] + parts[2]) + (parts[1] + parts[3])
    return total.astype(BF)


def spread(parts, axis):
    return [parts[0]] + [shift(parts[k], axis, k) for k in (1, 2, 3)]


def collect(values, axis):
    return [values] + [shift(values, axis, k) for k in (1, 2, 3)]


def turns(places):
    freqs = ROPE_BASE ** (-2.0 * jnp.arange(HALF).astype(F32) / HD)
    angles = freqs[:, None] * places.astype(F32)
    return jnp.cos(angles), jnp.sin(angles)


def body(
    tokens,
    segments,
    positions,
    norm_gain,
    query_weight,
    key_weight,
    value_weight,
    output_weight,
    mlp_gain,
    gate_weight,
    up_weight,
    down_weight,
    cotangent,
):
    axis = {name: lax.axis_index(name) for name in ALL}
    at = {name: index.reshape(1) for name, index in axis.items()}
    unit = (axis["x"] * 4 + axis["z"]) * 2 + axis["core"]
    x_own = tokens[0].T
    key_cols, value_cols, down_cols = key_weight.T, value_weight.T, down_weight.T

    packed, own_act = call(
        keys_kernel, "keys_values", (shape(PADROWS, 2 * KVW), shape(D, TOK)), None,
        (x_own, norm_gain, *turns(positions), key_cols, value_cols, segments, positions),
    )
    gathered = lax.all_gather(packed, SEQ, axis=0, tiled=False)
    acts = lax.all_gather(own_act, SEQ, axis=0, tiled=False)
    x_own, segments, positions, packed = lax.optimization_barrier((x_own, segments, positions, packed))

    third = TOK * unit + jnp.sum((segments < 2).astype(jnp.int32))
    marks = jnp.where(segments == 2, third, jnp.where(segments == 1, -64, 0))
    ints = jnp.concatenate([positions >> 6, positions & 63, marks >> 6, marks & 63], axis=0)
    ints = jnp.pad(ints, ((0, 12), (0, 0))).astype(BF)
    both = zigzag(jnp.concatenate([x_own, cotangent[0].T, ints], axis=0))
    x, out_grad = both[:D], both[D : 2 * D]
    ints = both[2 * D :].astype(jnp.int32)
    places = ints[0:1] * 64 + ints[1:2]
    marks = ints[2:3] * 64 + ints[3:4]
    marks = jnp.broadcast_to(marks.reshape(2, 1, CHUNK), (2, 8, CHUNK))
    chunk_a, chunk_b = 2 * unit, 2 * UNITS - 1 - 2 * unit
    scalars = jnp.stack([
        (chunk_a > chunk_b).astype(jnp.int32), jnp.minimum(chunk_a, chunk_b), jnp.maximum(chunk_a, chunk_b),
        axis["x"], axis["z"], axis["core"], axis["dp"],
    ])
    turn = turns(places)
    act, queries = call(
        queries_kernel, "queries", (shape(D, TOK), shape(D, TOK)), None, (x, norm_gain, *turn, query_weight)
    )

    attended, norm = attend(scalars, marks, queries, gathered)
    result, dmid, dattn, ggain, mine, other = feed_forward(
        scalars, x, out_grad, attended, mlp_gain, output_weight, gate_weight, up_weight, down_cols
    )

    came = swap(other)
    row_places = gathered[:, TOK + 8, :TOK].astype(F32) * 64 + gathered[:, TOK + 12, :TOK].astype(F32)
    table = turns(row_places.reshape(1, UNITS * TOK))
    came, table = lax.optimization_barrier((came, table))
    early = add(mine, came)
    early, dattn = lax.optimization_barrier((early, dattn))
    early = lax.all_to_all(early.reshape(64, 2, SHARD, 128), CHIPS, 0, 0, tiled=True)

    dq, mine, other = attend_back(scalars, marks, queries, dattn, attended, norm, gathered)

    came = swap(other)
    dact, late_mine, late_other = late_gradients(
        scalars, acts, table, mine, other, dq, *turn, act, query_weight, key_cols, value_cols, norm_gain, ggain
    )
    early, late_mine, late_other = lax.optimization_barrier((early, late_mine, late_other))
    late_came = swap(late_other)
    early_came = collect(jnp.sum(early.astype(F32), axis=0).astype(BF), "dp")
    halves = join(mine, came, late_mine, late_came)
    halves, early_came = lax.optimization_barrier((halves, early_came))
    early = lax.all_gather(jnp.stack(early_came), SEQ, axis=0, tiled=False)
    first_came, second_came = spread(halves[:4], "x"), spread(halves[4:], "z")
    first = [add(*(c[k] for c in first_came)) for k in range(4)]
    second = [add(*(c[k] for c in second_came)) for k in range(4)]
    first, second = lax.optimization_barrier((first, second))
    first_came, second_came = spread(first, "z"), spread(second, "x")
    late = jnp.concatenate(
        [add(*(part[KVR:] for part in first_came)), add(*(part[KVR:] for part in second_came))], axis=0
    )
    late_came = collect(late, "dp")
    result = zigzag(result)
    input_grad = call(
        tail_kernel, "tail", shape(D, TOK), None,
        (*first_came, *second_came, *turn, x, norm_gain, key_cols, value_cols, dact, dmid),
    )
    late = add(*late_came)
    late, input_grad, result = lax.optimization_barrier((late, input_grad, result))
    late = jnp.stack(collect(late, "z"))
    late_came = collect(late, "x")
    input_grad = zigzag(input_grad)
    early = early_finish(scalars, early.reshape(16, 2, 4, 2, SHARD, 128))
    late_came, input_grad, early = lax.optimization_barrier((late_came, input_grad, early))
    late = jnp.stack(late_came)
    late = call(
        late_finish_kernel, "late_finish",
        (shape(D, D, dtype=F32), shape(KVW, D, dtype=F32), shape(KVW, D, dtype=F32)) + (shape(D, dtype=F32),) * 2,
        scalars, (late, swap(late)), (pltpu.VMEM((32 * LATE_SHARD, 128), BF),),
    )
    return (
        result.T[None],
        input_grad.T[None],
        late[3],
        late[0],
        late[1].T,
        late[2].T,
        early[3],
        late[4],
        early[0],
        early[1],
        early[2].T,
    )


def solution(mesh):
    inner = Mesh(mesh.devices.reshape(4, 4, 4, 2), ALL)
    row = P("dp", SEQ, None)
    flat = P("dp", SEQ)
    return jax.shard_map(
        body,
        mesh=inner,
        in_specs=(row, flat, flat) + (P(),) * 9 + (row,),
        out_specs=(row, row) + (P(),) * 9,
        check_vma=False,
    )
```

```python
from functools import partial

import jax
import jax.numpy as jnp
from jax import lax
from jax.experimental import pallas as pl
from jax.experimental.pallas import tpu as pltpu
from jax.sharding import Mesh
from jax.sharding import PartitionSpec as P

D = 576
H = 9
KVH = 3
GROUP = H // KVH
HD = 64
HALF = HD // 2
FF = 1536
KVW = KVH * HD
EPSILON = 1e-05
ROPE_BASE = 10000.0
LOG2E = 1.4426950408889634
MASKED = -1e30
SCALE = HD**-0.5

TOK = 256
CHUNK = TOK // 2
UNITS = 32
COLS = GROUP * CHUNK
PADROWS = TOK + 16
SHARD = 96
GROUPS = 32
LATE_SHARD = 144
LATE_SPLIT = 80
FORWARD = 224
KVR = KVH * CHUNK
FF_BLOCK = 512

SEQ = ("x", "z", "core")
ALL = ("dp", "x", "z", "core")
CHIPS = ("dp", "x", "z")
BF = jnp.bfloat16
F32 = jnp.float32

NT = (((1,), (1,)), ((), ()))
NN = (((1,), (0,)), ((), ()))
TN = (((0,), (0,)), ((), ()))


def mm(left, right, dims=NN):
    return lax.dot_general(left, right, dims, preferred_element_type=F32)


def vmem(count):
    return [pl.BlockSpec(memory_space=pltpu.VMEM)] * count


def smem():
    return pl.BlockSpec(memory_space=pltpu.SMEM)


def call(kernel, name, out_shape, scalars, arrays, scratch=(), flops=10**8, moved=10**6, left=0, left_out=0):
    outs = out_shape if isinstance(out_shape, (tuple, list)) else (out_shape,)
    given = ([] if scalars is None else [scalars]) + list(arrays)
    stay = [pl.BlockSpec(memory_space=pl.ANY)]
    specs = ([] if scalars is None else [smem()]) + vmem(len(arrays) - left) + stay * left
    out_specs = vmem(len(outs) - left_out) + stay * left_out
    return pl.pallas_call(
        kernel,
        out_shape=out_shape,
        in_specs=specs,
        out_specs=tuple(out_specs) if isinstance(out_shape, (tuple, list)) else out_specs[0],
        scratch_shapes=list(scratch),
        compiler_params=pltpu.CompilerParams(vmem_limit_bytes=56 * 1024 * 1024),
        cost_estimate=pl.CostEstimate(flops=flops, bytes_accessed=moved, transcendentals=0),
        name=name,
    )(*given)


def shape(*dims, dtype=BF):
    return jax.ShapeDtypeStruct(dims, dtype)


def column_info(scalars, marks_ref, kv_ref):
    lo_idx = scalars[0]
    first_len = kv_ref[0, TOK : TOK + 16, 0:128].astype(F32)[0:1, :].astype(jnp.int32)
    first_len = jnp.concatenate([first_len] * (2 * GROUP), axis=1)
    hi, lo = marks_ref[1 - lo_idx, 0:1, :], marks_ref[lo_idx, 0:1, :]
    marks = jnp.concatenate([hi] * GROUP + [lo] * GROUP, axis=1)
    first_key = jnp.where(marks < 0, first_len, marks)
    lane = lax.broadcasted_iota(jnp.int32, (1, 2 * COLS), 1)
    start = jnp.where(lane < COLS, scalars[2], scalars[1]) * CHUNK
    return first_key, start + lax.rem(lane, CHUNK)


def full_mask(tile, first_key, place, rows, cols):
    keys = tile * TOK + lax.broadcasted_iota(jnp.int32, (rows, cols), 0)
    return (keys >= first_key[:, :cols]) & (keys <= place[:, :cols])


def tiles(scalars, step, most, upper):
    lo_diag = scalars[1] // 2
    hi_diag = scalars[2] // 2
    joint = jnp.maximum(lo_diag - 1, 0)
    single = hi_diag - lo_diag - 1

    @pl.loop(0, jnp.where(lo_diag > 0, 2, 1))
    def _(j):
        step(j * lo_diag, 1, 2 * COLS, True)

    @pl.loop(0, joint // 2)
    def _(j):
        step(1 + 2 * j, 2, 2 * COLS, False)

    @pl.when(joint % 2 == 1)
    def _():
        step(lo_diag - 1, 1, 2 * COLS, False)

    upper()

    @pl.loop(0, single // most)
    def _(j):
        step(lo_diag + 1 + most * j, most, COLS, False)

    if most == 4:

        @pl.when(single % 4 == 2)
        def _():
            step(hi_diag - 2, 2, COLS, False)

    step(hi_diag, 1, COLS, True)


def gather_columns(cat_ref, source_ref, scalars, first_row):
    cat_ref[...] = jnp.zeros_like(cat_ref)
    lo_idx = scalars[0]
    for part in range(2):
        index = (1 - lo_idx) if part == 0 else lo_idx
        lanes = pl.ds(pl.multiple_of(index * CHUNK, CHUNK), CHUNK)
        for head in range(H):
            at = part * COLS + (head % GROUP) * CHUNK
            block = source_ref[head * HD : (head + 1) * HD, lanes]
            cat_ref[head // GROUP, first_row : first_row + HD, at : at + CHUNK] = block


def scatter_columns(out_ref, values, group, scalars):
    lo_idx = scalars[0]
    for part in range(2):
        index = (1 - lo_idx) if part == 0 else lo_idx
        lanes = pl.ds(pl.multiple_of(index * CHUNK, CHUNK), CHUNK)
        for j in range(GROUP):
            head = group * GROUP + j
            at = part * COLS + j * CHUNK
            out_ref[head * HD : (head + 1) * HD, lanes] = values[:, at : at + CHUNK]


def fetch(source, target, sems):
    half = UNITS // 2
    copies = [
        pltpu.make_async_copy(source.at[pl.ds(i * half, half)], target.at[pl.ds(i * half, half)], sems.at[i])
        for i in range(2)
    ]
    for copy in copies:
        copy.start()
    return copies[0].wait, copies[1].wait


def forward_kernel(scalars, marks_ref, q_ref, kv_hbm, out_ref, lse_ref, qcat, acc, run_max, kv_ref, sems):
    lower, upper = fetch(kv_hbm, kv_ref, sems)
    gather_columns(qcat, q_ref, scalars, 0)
    lower()
    first_key, place = column_info(scalars, marks_ref, kv_ref)
    acc[...] = jnp.zeros_like(acc)
    run_max[...] = jnp.full_like(run_max, MASKED)

    def step(tile, count, cols, whole):
        rows = count * TOK
        if whole:
            allowed = full_mask(tile, first_key, place, rows, cols)
        else:
            seen = first_key[:, :cols] <= tile * TOK
        blocks = [kv_ref[pl.ds(tile, count), 0:TOK, g * 128 : (g + 1) * 128].reshape(rows, 128) for g in range(KVH)]
        all_scores = [mm(blocks[g], qcat[g, :, 0:cols]) * LOG2E for g in range(KVH)]
        all_values = [
            jnp.concatenate([jnp.ones((16, rows), BF), jnp.transpose(block)[HD:, :]], axis=0) for block in blocks
        ]
        factors, all_weights = [], []
        for g in range(KVH):
            scores = all_scores[g]
            old_max = run_max[g, 0:1, 0:cols]
            if whole:
                scores = jnp.where(allowed, scores, MASKED)
                new_max = jnp.maximum(old_max, jnp.max(scores, axis=0, keepdims=True))
                shift = new_max
            else:
                new_max = jnp.maximum(old_max, jnp.max(scores, axis=0, keepdims=True))
                new_max = jnp.where(seen, new_max, old_max)
                shift = jnp.where(seen, new_max, -MASKED)
            all_weights.append(jnp.exp2(scores - shift).astype(BF))
            factors.append(jnp.exp2(old_max - new_max))
            run_max[g, 0:1, 0:cols] = new_max
        for g in range(KVH):
            acc[g, :, 0:cols] = acc[g, :, 0:cols] * factors[g] + mm(all_values[g], all_weights[g])

    tiles(scalars, step, 4, upper)
    for g in range(KVH):
        total = acc[g, 0:1, :]
        scatter_columns(out_ref, acc[g, 16:, :] / total, g, scalars)
        lse_ref[g] = jnp.broadcast_to(run_max[g, 0:1, :] + jnp.log2(total), (8, 2 * COLS))


def backward_kernel(
    scalars, marks_ref, q_ref, do_ref, out_ref, lse_ref, kv_hbm, dq_ref, mine_ref, other_ref,
    qcat, docat, acc, delta, kv_ref, grads_ref, sems,
):
    lower, upper = fetch(kv_hbm, kv_ref, sems)
    gather_columns(qcat, q_ref, scalars, 0)
    gather_columns(docat, do_ref, scalars, HD)
    lower()
    first_key, place = column_info(scalars, marks_ref, kv_ref)
    lo_idx = scalars[0]
    hi_diag = scalars[2] // 2
    my_x, my_z, my_c = scalars[3], scalars[4], scalars[5]
    acc[...] = jnp.zeros_like(acc)
    for part in range(2):
        index = (1 - lo_idx) if part == 0 else lo_idx
        lanes = pl.ds(pl.multiple_of(index * CHUNK, CHUNK), CHUNK)
        for head in range(H):
            rows = slice(head * HD, (head + 1) * HD)
            at = part * COLS + (head % GROUP) * CHUNK
            terms = do_ref[rows, lanes].astype(F32) * out_ref[rows, lanes]
            delta[head // GROUP, 0:1, at : at + CHUNK] = jnp.sum(terms, axis=0, keepdims=True)

    def store(tile, grads):
        mirrored = UNITS - 1 - tile
        kx, kz = (tile // 8 - my_x) & 3, ((tile // 2) % 4 - my_z) & 3
        mx, mz = (mirrored // 8 - my_x) & 3, ((mirrored // 2) % 4 - my_z) & 3
        same = lax.rem(tile, 2) == my_c

        for half in range(2):
            for g, grad in enumerate(grads):
                rows = slice(g * CHUNK, (g + 1) * CHUNK)
                grads_ref[tile, half, rows, :] = grad[half * CHUNK : (half + 1) * CHUNK]

        def send(first_ref, second_ref):
            pltpu.make_async_copy(grads_ref.at[tile, 0], first_ref.at[0, kx, kz], sems.at[2]).start()
            pltpu.make_async_copy(grads_ref.at[tile, 1], second_ref.at[1, mz, mx], sems.at[2]).start()

        @pl.when(same)
        def _():
            send(mine_ref, other_ref)

        @pl.when(jnp.logical_not(same))
        def _():
            send(other_ref, mine_ref)

    def step(tile, count, cols, whole):
        rows = count * TOK
        if whole:
            allowed = full_mask(tile, first_key, place, rows, cols)
        else:
            seen = first_key[:, :cols] <= tile * TOK
        all_grads, all_probs, all_grad_scores = [], [], []
        blocks = [kv_ref[pl.ds(tile, count), 0:TOK, g * 128 : (g + 1) * 128].reshape(rows, 128) for g in range(KVH)]
        all_scores = [mm(blocks[g], qcat[g, :, 0:cols]) * LOG2E for g in range(KVH)]
        all_grad_probs = [mm(blocks[g], docat[g, :, 0:cols]) for g in range(KVH)]
        for g in range(KVH):
            scores = all_scores[g]
            shift = lse_ref[g, 0:1, 0:cols]
            if whole:
                scores = jnp.where(allowed, scores, MASKED)
            else:
                shift = jnp.where(seen, shift, -MASKED)
            probs = jnp.exp2(scores - shift)
            all_grad_scores.append((probs * (all_grad_probs[g] - delta[g, 0:1, 0:cols])).astype(BF))
            all_probs.append(probs.astype(BF))
        for g in range(KVH):
            all_grads.append(
                mm(all_grad_scores[g], qcat[g, :, 0:cols], NT) + mm(all_probs[g], docat[g, :, 0:cols], NT)
            )
            keys = jnp.transpose(blocks[g])[0:HD, :]
            acc[g, :, 0:cols] = acc[g, :, 0:cols] + mm(keys, all_grad_scores[g])
        for i in range(count):
            store(tile + i, [grad[i * TOK : (i + 1) * TOK].astype(BF) for grad in all_grads])

    tiles(scalars, step, 2, upper)

    @pl.loop(hi_diag + 1, UNITS)
    def _(t):
        store(t, [jnp.zeros((TOK, 128), BF)] * KVH)

    for g in range(KVH):
        scatter_columns(dq_ref, acc[g] * SCALE, g, scalars)
    pltpu.make_async_copy(grads_ref, grads_ref, sems.at[2]).wait()


def attend(scalars, marks, queries, keys_values):
    return call(
        forward_kernel,
        "attention_forward",
        (shape(D, TOK, dtype=F32), shape(KVH, 8, 2 * COLS, dtype=F32)),
        scalars,
        (marks, queries, keys_values),
        (
            pltpu.VMEM((KVH, 128, 2 * COLS), BF),
            pltpu.VMEM((KVH, 16 + HD, 2 * COLS), F32),
            pltpu.VMEM((KVH, 8, 2 * COLS), F32),
            pltpu.VMEM(keys_values.shape, BF),
            pltpu.SemaphoreType.DMA((2,)),
        ),
        flops=20 * 10**9,
        moved=7 * 10**6,
        left=1,
    )


def attend_back(scalars, marks, queries, grad_out, attended, norm, keys_values):
    blocks = shape(2, 4, 4, KVH * CHUNK, 128)
    return call(
        backward_kernel,
        "attention_backward",
        (shape(D, TOK, dtype=F32), blocks, blocks),
        scalars,
        (marks, queries, grad_out, attended, norm, keys_values),
        (
            pltpu.VMEM((KVH, 128, 2 * COLS), BF),
            pltpu.VMEM((KVH, 128, 2 * COLS), BF),
            pltpu.VMEM((KVH, HD, 2 * COLS), F32),
            pltpu.VMEM((KVH, 8, 2 * COLS), F32),
            pltpu.VMEM(keys_values.shape, BF),
            pltpu.VMEM((UNITS, 2, KVR, 128), BF),
            pltpu.SemaphoreType.DMA((3,)),
        ),
        left=1,
        left_out=2,
        flops=40 * 10**9,
        moved=24 * 10**6,
    )


def inverse_rms(values):
    return lax.rsqrt(jnp.mean(values * values, axis=0, keepdims=True) + EPSILON)


def rotated(values, turn, sign):
    cosine, sine = turn[0], turn[1] * sign
    first, second = values[:HALF], values[HALF:]
    return jnp.concatenate([first * cosine - second * sine, second * cosine + first * sine], axis=0)


def row_sums(values):
    ones = jnp.ones((16, values.shape[1]), BF)
    high = values.astype(BF)
    low = (values - high.astype(F32)).astype(BF)
    return mm(ones, high, NT) + mm(ones, low, NT)


def column(ref):
    row = ref[...].reshape(1, ref.shape[0])
    return jnp.transpose(jnp.broadcast_to(row, (8, ref.shape[0])))[:, 0:1]


def keys_kernel(x_ref, gain_ref, cos_ref, sin_ref, key_ref, value_ref, seg_ref, place_ref, out_ref, act_ref):
    x = x_ref[...].astype(F32)
    act = (x * inverse_rms(x) * column(gain_ref)).astype(BF)
    act_ref[...] = act
    keys = mm(key_ref[...], act)
    values = mm(value_ref[...], act)
    turn = (cos_ref[...], sin_ref[...])
    for g in range(KVH):
        rows = slice(g * HD, (g + 1) * HD)
        block = jnp.concatenate([rotated(keys[rows], turn, 1.0), values[rows]], axis=0)
        out_ref[0:TOK, g * 128 : (g + 1) * 128] = jnp.transpose(block).astype(BF)
    first_len = jnp.sum((seg_ref[...] == 0).astype(F32), axis=1, keepdims=True)
    row = lax.broadcasted_iota(jnp.int32, (16, TOK), 0)
    places = place_ref[...]
    places = jnp.where(row < 12, places >> 6, places & 63).astype(F32)
    out_ref[TOK:, 0:TOK] = jnp.where(row < 8, first_len, places).astype(BF)
    out_ref[TOK:, TOK:] = jnp.zeros((16, 2 * KVW - TOK), BF)


def queries_kernel(x_ref, gain_ref, cos_ref, sin_ref, weight_ref, act_ref, out_ref):
    x = x_ref[...].astype(F32)
    act = (x * inverse_rms(x) * column(gain_ref)).astype(BF)
    act_ref[...] = act
    queries = mm(weight_ref[...], act, TN)
    turn = (cos_ref[...], sin_ref[...])
    for head in range(H):
        rows = slice(head * HD, (head + 1) * HD)
        low = rotated(queries[rows], turn, 1.0).astype(BF)
        out_ref[rows, :] = low * jnp.asarray(SCALE, BF)


def mlp_kernel(
    scalars, x_ref, c_ref, attn_ref, gain_ref, out_weight, gate_ref, up_ref, down_ref,
    result_ref, dmid_ref, dattn_ref, ggain_ref, mine_ref, other_ref,
    mid, act, act_cols, c_cols, result, dact, shards, sems,
):
    block = pl.program_id(0)
    my_c = scalars[5]

    def put(group, values):
        for k in range(values.shape[1] // 128):
            for i in range(values.shape[0] // SHARD):
                j = k * (values.shape[0] // SHARD) + i
                piece = values[i * SHARD : (i + 1) * SHARD, k * 128 : (k + 1) * 128]
                shards[group + j // 8, j % 8] = piece

    def send(group):
        @pl.when(group // 16 == my_c)
        def _():
            pltpu.make_async_copy(shards.at[group], mine_ref.at[group % 16], sems.at[0]).start()

        @pl.when(group // 16 != my_c)
        def _():
            pltpu.make_async_copy(shards.at[group], other_ref.at[group % 16], sems.at[1]).start()

    @pl.when(block == 0)
    def _():
        low = attn_ref[...].astype(BF)
        middle = x_ref[...].astype(F32) + mm(out_weight[...], low, TN)
        mid[...] = middle
        normal = (middle * inverse_rms(middle) * column(gain_ref)).astype(BF)
        act_cols[...] = normal
        act[...] = jnp.transpose(normal)
        c_cols[...] = jnp.transpose(c_ref[...])
        result[...] = jnp.zeros_like(result)
        dact[...] = jnp.zeros_like(dact)

    gate = mm(act[...], gate_ref[...])
    up = mm(act[...], up_ref[...])
    sigmoid = 1.0 / (1.0 + jnp.exp(-gate))
    silu = gate * sigmoid
    hidden = (silu * up).astype(BF)
    dhidden = mm(c_cols[...], down_ref[...])
    dup = (dhidden * silu).astype(BF)
    dgate = (dhidden * up * (sigmoid * (1.0 + gate * (1.0 - sigmoid)))).astype(BF)
    result[...] += mm(down_ref[...], hidden, NT)
    put(block * 9, mm(act_cols[...], dgate).astype(BF))
    put(block * 9 + 3, mm(act_cols[...], dup).astype(BF))
    put(block * 9 + 6, mm(c_ref[...], hidden).astype(BF))
    for group in range(9):
        send(block * 9 + group)
    dact[...] += mm(gate_ref[...], dgate, NT) + mm(up_ref[...], dup, NT)

    @pl.when(block == FF // FF_BLOCK - 1)
    def _():
        middle = mid[...]
        gain = column(gain_ref)
        rms = inverse_rms(middle)
        grads = dact[...]
        result_ref[...] = (middle + result[...]).astype(BF)
        ggain_ref[...] = row_sums(grads * middle * rms)
        pulled = grads * gain
        inner = jnp.mean(pulled * middle, axis=0, keepdims=True)
        dmid = c_ref[...].astype(F32) + (pulled * rms - middle * (rms * rms * rms * inner))
        dmid_ref[...] = dmid
        low = dmid.astype(BF)
        dattn_ref[...] = mm(out_weight[...], low).astype(BF)
        gout = mm(attn_ref[...].astype(BF), low, NT).astype(BF)
        put(27, gout[:, :512])
        shards[30:32] = jnp.zeros((2, 8, SHARD, 128), BF)
        put(30, jnp.concatenate([gout[: D // 2, 512:], gout[D // 2 :, 512:]], axis=1))
        for group in range(27, 32):
            send(group)
        for i, ref in enumerate((mine_ref, other_ref)):
            pltpu.make_async_copy(ref, ref, sems.at[i]).wait()


def feed_forward(scalars, x, cotangent, attended, gain, out_weight, gate_weight, up_weight, down_weight):
    whole = lambda *dims: pl.BlockSpec(dims, lambda f: (0,) * len(dims))
    part = pl.BlockSpec((D, FF_BLOCK), lambda f: (0, f))
    return pl.pallas_call(
        mlp_kernel,
        grid=(FF // FF_BLOCK,),
        out_shape=(shape(D, TOK), shape(D, TOK, dtype=F32), shape(D, TOK), shape(16, D, dtype=F32))
        + (shape(GROUPS // 2, 8, SHARD, 128),) * 2,
        in_specs=[smem(), whole(D, TOK), whole(D, TOK), whole(D, TOK), whole(D), whole(D, D), part, part, part],
        out_specs=(whole(D, TOK), whole(D, TOK), whole(D, TOK), whole(16, D))
        + (pl.BlockSpec(memory_space=pl.ANY),) * 2,
        scratch_shapes=[
            pltpu.VMEM((D, TOK), F32), pltpu.VMEM((TOK, D), BF), pltpu.VMEM((D, TOK), BF),
            pltpu.VMEM((TOK, D), BF), pltpu.VMEM((D, TOK), F32), pltpu.VMEM((D, TOK), F32),
            pltpu.VMEM((GROUPS, 8, SHARD, 128), BF), pltpu.SemaphoreType.DMA((2,)),
        ],
        compiler_params=pltpu.CompilerParams(vmem_limit_bytes=56 * 1024 * 1024),
        cost_estimate=pl.CostEstimate(flops=5 * 10**9, bytes_accessed=14 * 10**6, transcendentals=10**6),
        name="feed_forward",
    )(scalars, x, cotangent, attended, gain, out_weight, gate_weight, up_weight, down_weight)


def early_finish_kernel(scalars, source, gate_ref, up_ref, down_ref, out_ref, shards, sems):
    block = pl.program_id(0)
    my_y = scalars[6]

    def part(core, y):
        return shards.at[core, pl.ds(y * 16, 16)]

    @pl.when(block == 0)
    def _():
        for core in range(2):
            for k in range(4):
                y = (my_y - k) & 3
                pltpu.make_async_copy(source.at[:, core, k], part(core, y), sems.at[core, y]).start()

    needed = (((0, 0), (0, 1), (0, 2)), ((0, 3), (1, 0)), ((1, 1), (1, 2), (1, 3)))
    for step, places in enumerate(needed):

        @pl.when(block == step)
        def _():
            for core, y in places:
                pltpu.make_async_copy(part(core, y), part(core, y), sems.at[core, y]).wait()

    def get(group, k, i):
        piece = group * 8 + D // SHARD * k + i
        half, piece = piece // (GROUPS * 4), piece % (GROUPS * 4)
        return shards[half, piece // 2, piece % 2].astype(F32)

    for kind, ref in enumerate((gate_ref, up_ref, down_ref)):
        for k in range(4):
            for i in range(D // SHARD):
                ref[i * SHARD : (i + 1) * SHARD, k * 128 : (k + 1) * 128] = get(block * 9 + kind * 3, k, i)

    @pl.when(block == FF // FF_BLOCK - 1)
    def _():
        for k in range(4):
            for i in range(D // SHARD):
                out_ref[i * SHARD : (i + 1) * SHARD, k * 128 : (k + 1) * 128] = get(27, k, i)
        rest = jnp.concatenate([get(30, 0, i) for i in range(3)], axis=0)
        out_ref[:, 512:] = jnp.concatenate([rest[:, :HD], rest[:, HD:]], axis=0)


def early_finish(scalars, source):
    part = pl.BlockSpec((D, FF_BLOCK), lambda f: (0, f))
    return pl.pallas_call(
        early_finish_kernel,
        grid=(FF // FF_BLOCK,),
        out_shape=(shape(D, FF, dtype=F32),) * 3 + (shape(D, D, dtype=F32),),
        in_specs=[smem(), pl.BlockSpec(memory_space=pl.ANY)],
        out_specs=(part, part, part, pl.BlockSpec((D, D), lambda f: (0, 0))),
        scratch_shapes=[pltpu.VMEM((2, 64, 2, SHARD, 128), BF), pltpu.SemaphoreType.DMA((2, 4))],
        compiler_params=pltpu.CompilerParams(vmem_limit_bytes=56 * 1024 * 1024),
        cost_estimate=pl.CostEstimate(flops=10**7, bytes_accessed=19 * 10**6, transcendentals=0),
        name="early_gradients",
    )(scalars, source)


def late_rows():
    return 0, 2592, 4320, 4400


def pack(buffer, at, values):
    count = values.shape[0]
    for k in range(4):
        buffer[at + k * count : at + (k + 1) * count, :] = values[:, k * 128 : (k + 1) * 128]
    if count > 16:
        rest = jnp.concatenate([values[: count // 2, 512:], values[count // 2 :, 512:]], axis=1)
        buffer[at + 4 * count : at + 4 * count + count // 2, :] = rest
    else:
        buffer[at + 4 * count : at + 5 * count, 0:64] = values[:, 512:]


def unpack(buffer, at, count):
    blocks = [buffer[at + k * count : at + (k + 1) * count, :] for k in range(4)]
    if count > 16:
        rest = buffer[at + 4 * count : at + 4 * count + count // 2, :]
        rest = jnp.concatenate([rest[:, :64], rest[:, 64:]], axis=0)
    else:
        rest = buffer[at + 4 * count : at + 5 * count, 0:64]
    return jnp.concatenate(blocks + [rest], axis=1)


def late_kernel(
    scalars, acts_ref, cos_all, sin_all, first_mine, second_mine, first_other, second_other, dq_ref, cos_ref, sin_ref, act_ref, weight_ref,
    key_ref, value_ref, gain_ref, ggain_ref, dact_ref, mine_ref, other_ref, late, gkv,
):
    block = pl.program_id(0)
    my_x, my_z, my_c = scalars[3], scalars[4], scalars[5]

    @pl.when(block == 0)
    def _():
        gkv[...] = jnp.zeros_like(gkv)

    total = None
    for kz in range(4):
        z = (my_z + kz) & 3
        mz = (3 - z - my_z) & 3
        for core, first_ref, second_ref in ((my_c, first_mine, second_other), (1 - my_c, first_other, second_mine)):
            unit = z * 2 + core
            first, second = first_ref[0, 0, kz], second_ref[0, mz, 0]
            lanes = pl.ds(pl.multiple_of(unit * TOK, TOK), TOK)
            turn = (cos_all[:, lanes], sin_all[:, lanes])
            turned = []
            for g in range(KVH):
                rows = slice(g * CHUNK, (g + 1) * CHUNK)
                grads = jnp.concatenate([jnp.transpose(first[rows]), jnp.transpose(second[rows])], axis=1)
                turned.append(rotated(grads[0:HD].astype(F32), turn, -1.0).astype(BF))
                turned.append(grads[HD:])
            product = mm(acts_ref[unit], jnp.concatenate(turned, axis=0), NT)
            total = product if total is None else total + product
    gkv[...] += total

    @pl.when(block == 3)
    def _():
        turn = (cos_ref[...], sin_ref[...])
        heads = [rotated(dq_ref[h * HD : (h + 1) * HD, :], turn, -1.0).astype(BF) for h in range(H)]
        low = jnp.concatenate(heads, axis=0)
        weight = weight_ref[...]
        gquery = mm(act_ref[...], low, NT)
        dact_ref[...] = mm(weight, low)
        at_q, at_kv, at_n, at_m = late_rows()
        late[at_n:, :] = jnp.zeros((32 * LATE_SHARD - at_n, 128), BF)
        pack(late, at_q, gquery.astype(BF))
        gain = row_sums(gquery * weight.astype(F32))
        for g in range(KVH):
            rows = slice(g * HD, (g + 1) * HD)
            grad = gkv[:, g * 128 : (g + 1) * 128]
            late[at_kv + g * D : at_kv + (g + 1) * D, :] = grad.astype(BF)
            columns = jnp.transpose(jnp.concatenate([key_ref[rows, :], value_ref[rows, :]], axis=0))
            gain = gain + row_sums(grad * columns.astype(F32))
        pack(late, at_n, (gain / gain_ref[...].reshape(1, D)).astype(BF))
        pack(late, at_m, ggain_ref[...].astype(BF))
        for x in range(4):
            for z in range(4):
                index = ((x - my_x) & 3, (z - my_z) & 3)
                for target, core in ((mine_ref, my_c), (other_ref, 1 - my_c)):
                    at = ((core * 4 + x) * 4 + z) * LATE_SHARD
                    target[index] = late[pl.ds(pl.multiple_of(at, LATE_SHARD), LATE_SHARD), :]


def late_gradients(scalars, acts, table, mine, other, *arrays):
    whole = lambda array: pl.BlockSpec(array.shape, lambda k, s: (0,) * len(array.shape))
    mirrored = lambda k, s: (3 - ((s[3] + k) & 3) - s[3]) & 3
    unit = (KVH * CHUNK, 128)
    first = pl.BlockSpec((1, 1, 4) + unit, lambda k, s: (0, k, 0, 0, 0))
    second = pl.BlockSpec((1, 4, 1) + unit, lambda k, s: (1, 0, mirrored(k, s), 0, 0))
    outs = (shape(D, TOK, dtype=F32),) + (shape(4, 4, LATE_SHARD, 128),) * 2
    return pl.pallas_call(
        late_kernel,
        grid_spec=pltpu.PrefetchScalarGridSpec(
            num_scalar_prefetch=1,
            grid=(4,),
            in_specs=[pl.BlockSpec((8, D, TOK), lambda k, s: ((s[3] + k) & 3, 0, 0))]
            + [pl.BlockSpec((HALF, 8 * TOK), lambda k, s: (0, (s[3] + k) & 3))] * 2
            + [first, second, first, second]
            + [whole(array) for array in arrays],
            out_specs=tuple(whole(out) for out in outs),
            scratch_shapes=[pltpu.VMEM((32 * LATE_SHARD, 128), BF), pltpu.VMEM((D, 2 * KVW), F32)],
        ),
        out_shape=outs,
        compiler_params=pltpu.CompilerParams(vmem_limit_bytes=56 * 1024 * 1024),
        cost_estimate=pl.CostEstimate(flops=4 * 10**9, bytes_accessed=20 * 10**6, transcendentals=0),
        name="late_gradients",
    )(scalars, acts, *table, mine, mine, other, other, *arrays)


def join_kernel(mine_ref, came_ref, late_mine, late_came, *outs):
    j = pl.program_id(0)
    first, second = slice(0, LATE_SPLIT), slice(LATE_SPLIT, LATE_SHARD)
    for k in range(4):
        outs[k][0, 0:KVR, :] = add(mine_ref[0, k, 0], came_ref[0, k, 0])
        outs[k][0, KVR:, :] = add(late_mine[k, j, first], late_came[k, j, first])
        outs[4 + k][0, 0:KVR, :] = add(mine_ref[1, k, 0], came_ref[1, k, 0])
        outs[4 + k][0, KVR:, :] = add(late_mine[j, k, second], late_came[j, k, second])


def join(mine, came, late_mine, late_came):
    part = pl.BlockSpec((2, 4, 1, KVR, 128), lambda j: (0, 0, j, 0, 0))
    late = pl.BlockSpec(late_mine.shape, lambda j: (0, 0, 0, 0))
    heights = (KVR + LATE_SPLIT,) * 4 + (KVR + LATE_SHARD - LATE_SPLIT,) * 4
    return pl.pallas_call(
        join_kernel,
        grid=(4,),
        out_shape=tuple(shape(4, rows, 128) for rows in heights),
        in_specs=[part, part, late, late],
        out_specs=tuple(pl.BlockSpec((1, rows, 128), lambda j: (j, 0, 0)) for rows in heights),
        compiler_params=pltpu.CompilerParams(vmem_limit_bytes=56 * 1024 * 1024),
        cost_estimate=pl.CostEstimate(flops=10**7, bytes_accessed=11 * 10**6, transcendentals=0),
        name="join",
    )(mine, came, late_mine, late_came)


def late_finish_kernel(scalars, own_ref, came_ref, gquery_ref, gkey_ref, gvalue_ref, gnorm_ref, gmlp_ref, late):
    my_x, my_z, my_c = scalars[3], scalars[4], scalars[5]
    for source, core in ((own_ref, my_c), (came_ref, 1 - my_c)):
        for x in range(4):
            for z in range(4):
                at = ((core * 4 + ((my_x - x) & 3)) * 4 + ((my_z - z) & 3)) * LATE_SHARD
                late[pl.ds(pl.multiple_of(at, LATE_SHARD), LATE_SHARD), :] = source[x, z]
    at_q, at_kv, at_n, at_m = late_rows()
    gquery_ref[...] = unpack(late, at_q, D).astype(F32)
    for g in range(KVH):
        grad = jnp.transpose(late[at_kv + g * D : at_kv + (g + 1) * D, :].astype(F32))
        gkey_ref[g * HD : (g + 1) * HD, :] = grad[:HD]
        gvalue_ref[g * HD : (g + 1) * HD, :] = grad[HD:]
    gnorm_ref[...] = unpack(late, at_n, 16).astype(F32)[0]
    gmlp_ref[...] = unpack(late, at_m, 16).astype(F32)[0]


def tail_kernel(
    a0, a1, a2, a3, b0, b1, b2, b3, cos_ref, sin_ref, x_ref, gain_ref, key_ref, value_ref, dact_ref, dmid_ref, grad_ref
):
    turn = (cos_ref[...], sin_ref[...])
    summed = []
    for parts in ((a0, a1, a2, a3), (b0, b1, b2, b3)):
        total = parts[0][0 : KVR, :].astype(F32)
        for part in parts[1:]:
            total = total + part[0 : KVR, :].astype(F32)
        summed.append(total)
    keys, values = [], []
    for g in range(KVH):
        columns = [jnp.transpose(t[g * CHUNK : (g + 1) * CHUNK, :]) for t in summed]
        columns = jnp.concatenate(columns, axis=1)
        keys.append(rotated(columns[:HD], turn, -1.0).astype(BF))
        values.append(columns[HD:].astype(BF))
    keys, values = jnp.concatenate(keys, axis=0), jnp.concatenate(values, axis=0)
    grads = dact_ref[...] + mm(key_ref[...], keys, TN) + mm(value_ref[...], values, TN)
    x = x_ref[...].astype(F32)
    rms = inverse_rms(x)
    pulled = grads * column(gain_ref)
    inner = jnp.mean(pulled * x, axis=0, keepdims=True)
    grad_ref[...] = (dmid_ref[...] + (pulled * rms - x * (rms * rms * rms * inner))).astype(BF)


def shift(values, axis, by):
    return lax.ppermute(values, axis, [(i, (i + by) % 4) for i in range(4)])


def swap(values):
    return lax.ppermute(values, "core", [(0, 1), (1, 0)])


def mirror(values):
    return lax.ppermute(values, SEQ, [(i, UNITS - 1 - i) for i in range(UNITS)])


def zigzag(values):
    return jnp.concatenate([values[:, :CHUNK], mirror(values[:, CHUNK:])], axis=1)


def add(*parts):
    parts = [p.astype(F32) for p in parts]
    total = parts[0] + parts[1] if len(parts) == 2 else (parts[0] + parts[2]) + (parts[1] + parts[3])
    return total.astype(BF)


def spread(parts, axis):
    return [parts[0]] + [shift(parts[k], axis, k) for k in (1, 2, 3)]


def pass_on(parts, axis):
    near, far, back = parts[1], parts[2], parts[3]
    forward, backward = shift(far[:, :FORWARD], axis, 1), shift(far[:, FORWARD:], axis, 3)

    def rest():
        ahead = jnp.concatenate([add(near[:, :FORWARD], forward), near[:, FORWARD:]], axis=1)
        behind = jnp.concatenate([back[:, :FORWARD], add(back[:, FORWARD:], backward)], axis=1)
        return parts[0], shift(ahead, axis, 1), shift(behind, axis, 3)

    return rest


def add_three(*parts):
    return (parts[0].astype(F32) + (parts[1].astype(F32) + parts[2].astype(F32))).astype(BF)


def collect(values, axis):
    return [values] + [shift(values, axis, k) for k in (1, 2, 3)]


def turns(places):
    freqs = ROPE_BASE ** (-2.0 * jnp.arange(HALF).astype(F32) / HD)
    angles = freqs[:, None] * places.astype(F32)
    return jnp.cos(angles), jnp.sin(angles)


def body(
    tokens,
    segments,
    positions,
    norm_gain,
    query_weight,
    key_weight,
    value_weight,
    output_weight,
    mlp_gain,
    gate_weight,
    up_weight,
    down_weight,
    cotangent,
):
    axis = {name: lax.axis_index(name) for name in ALL}
    at = {name: index.reshape(1) for name, index in axis.items()}
    unit = (axis["x"] * 4 + axis["z"]) * 2 + axis["core"]
    x_own = tokens[0].T
    key_cols, value_cols, down_cols = key_weight.T, value_weight.T, down_weight.T

    packed, own_act = call(
        keys_kernel, "keys_values", (shape(PADROWS, 2 * KVW), shape(D, TOK)), None,
        (x_own, norm_gain, *turns(positions), key_cols, value_cols, segments, positions),
    )
    gathered = lax.all_gather(packed, SEQ, axis=0, tiled=False)
    acts = lax.all_gather(own_act, SEQ, axis=0, tiled=False)
    x_own, segments, positions, packed = lax.optimization_barrier((x_own, segments, positions, packed))

    third = TOK * unit + jnp.sum((segments < 2).astype(jnp.int32))
    marks = jnp.where(segments == 2, third, jnp.where(segments == 1, -64, 0))
    ints = jnp.concatenate([positions >> 6, positions & 63, marks >> 6, marks & 63], axis=0)
    ints = jnp.pad(ints, ((0, 12), (0, 0))).astype(BF)
    both = zigzag(jnp.concatenate([x_own, cotangent[0].T, ints], axis=0))
    x, out_grad = both[:D], both[D : 2 * D]
    ints = both[2 * D :].astype(jnp.int32)
    places = ints[0:1] * 64 + ints[1:2]
    marks = ints[2:3] * 64 + ints[3:4]
    marks = jnp.broadcast_to(marks.reshape(2, 1, CHUNK), (2, 8, CHUNK))
    chunk_a, chunk_b = 2 * unit, 2 * UNITS - 1 - 2 * unit
    scalars = jnp.stack([
        (chunk_a > chunk_b).astype(jnp.int32), jnp.minimum(chunk_a, chunk_b), jnp.maximum(chunk_a, chunk_b),
        axis["x"], axis["z"], axis["core"], axis["dp"],
    ])
    turn = turns(places)
    act, queries = call(
        queries_kernel, "queries", (shape(D, TOK), shape(D, TOK)), None, (x, norm_gain, *turn, query_weight)
    )

    attended, norm = attend(scalars, marks, queries, gathered)
    result, dmid, dattn, ggain, mine, other = feed_forward(
        scalars, x, out_grad, attended, mlp_gain, output_weight, gate_weight, up_weight, down_cols
    )

    came = swap(other)
    row_places = gathered[:, TOK + 8, :TOK].astype(F32) * 64 + gathered[:, TOK + 12, :TOK].astype(F32)
    table = turns(row_places.reshape(1, UNITS * TOK))
    came, table = lax.optimization_barrier((came, table))
    early = add(mine, came)
    early, dattn = lax.optimization_barrier((early, dattn))
    early = lax.all_to_all(early.reshape(64, 2, SHARD, 128), CHIPS, 0, 0, tiled=True)

    dq, mine, other = attend_back(scalars, marks, queries, dattn, attended, norm, gathered)

    came = swap(other)
    dact, late_mine, late_other = late_gradients(
        scalars, acts, table, mine, other, dq, *turn, act, query_weight, key_cols, value_cols, norm_gain, ggain
    )
    early, late_mine, late_other = lax.optimization_barrier((early, late_mine, late_other))
    late_came = swap(late_other)
    early_came = collect(jnp.sum(early.astype(F32), axis=0).astype(BF), "dp")
    halves = join(mine, came, late_mine, late_came)
    halves, early_came = lax.optimization_barrier((halves, early_came))
    early = lax.all_gather(jnp.stack(early_came), SEQ, axis=0, tiled=False)
    first_rest, second_rest = pass_on(halves[:4], "x"), pass_on(halves[4:], "z")
    first_came, second_came = first_rest(), second_rest()
    first = [add_three(*(c[k] for c in first_came)) for k in range(4)]
    second = [add_three(*(c[k] for c in second_came)) for k in range(4)]
    first, second = lax.optimization_barrier((first, second))
    first_came, second_came = spread(first, "z"), spread(second, "x")
    late = jnp.concatenate(
        [add(*(part[KVR:] for part in first_came)), add(*(part[KVR:] for part in second_came))], axis=0
    )
    late_came = collect(late, "dp")
    input_grad = call(
        tail_kernel, "tail", shape(D, TOK), None,
        (*first_came, *second_came, *turn, x, norm_gain, key_cols, value_cols, dact, dmid),
    )
    late = add(*late_came)
    late, input_grad = lax.optimization_barrier((late, input_grad))
    late = jnp.stack(collect(late, "z"))
    late_came = collect(late, "x")
    input_grad, result = zigzag(input_grad), zigzag(result)
    early = early_finish(scalars, early.reshape(16, 2, 4, 2, SHARD, 128))
    late_came, input_grad, result, early = lax.optimization_barrier((late_came, input_grad, result, early))
    late = jnp.stack(late_came)
    late = call(
        late_finish_kernel, "late_finish",
        (shape(D, D, dtype=F32), shape(KVW, D, dtype=F32), shape(KVW, D, dtype=F32)) + (shape(D, dtype=F32),) * 2,
        scalars, (late, swap(late)), (pltpu.VMEM((32 * LATE_SHARD, 128), BF),),
    )
    return (
        result.T[None],
        input_grad.T[None],
        late[3],
        late[0],
        late[1].T,
        late[2].T,
        early[3],
        late[4],
        early[0],
        early[1],
        early[2].T,
    )


def solution(mesh):
    inner = Mesh(mesh.devices.reshape(4, 4, 4, 2), ALL)
    row = P("dp", SEQ, None)
    flat = P("dp", SEQ)
    return jax.shard_map(
        body,
        mesh=inner,
        in_specs=(row, flat, flat) + (P(),) * 9 + (row,),
        out_specs=(row, row) + (P(),) * 9,
        check_vma=False,
    )
```

```python
from functools import partial

import jax
import jax.numpy as jnp
from jax import lax
from jax.experimental import pallas as pl
from jax.experimental.pallas import tpu as pltpu
from jax.sharding import Mesh
from jax.sharding import PartitionSpec as P

D = 576
H = 9
KVH = 3
GROUP = H // KVH
HD = 64
HALF = HD // 2
FF = 1536
KVW = KVH * HD
EPSILON = 1e-05
ROPE_BASE = 10000.0
LOG2E = 1.4426950408889634
MASKED = -1e30
SCALE = HD**-0.5

TOK = 256
CHUNK = TOK // 2
UNITS = 32
COLS = GROUP * CHUNK
PADROWS = TOK + 16
SHARD = 96
GROUPS = 32
LATE_SHARD = 144
LATE_SPLIT = 80
FORWARD = 224
KVR = KVH * CHUNK
FF_BLOCK = 512

SEQ = ("x", "z", "core")
ALL = ("dp", "x", "z", "core")
CHIPS = ("dp", "x", "z")
BF = jnp.bfloat16
F32 = jnp.float32

NT = (((1,), (1,)), ((), ()))
NN = (((1,), (0,)), ((), ()))
TN = (((0,), (0,)), ((), ()))


def mm(left, right, dims=NN):
    return lax.dot_general(left, right, dims, preferred_element_type=F32)


def vmem(count):
    return [pl.BlockSpec(memory_space=pltpu.VMEM)] * count


def smem():
    return pl.BlockSpec(memory_space=pltpu.SMEM)


def call(kernel, name, out_shape, scalars, arrays, scratch=(), flops=10**8, moved=10**6, left=0, left_out=0):
    outs = out_shape if isinstance(out_shape, (tuple, list)) else (out_shape,)
    given = ([] if scalars is None else [scalars]) + list(arrays)
    stay = [pl.BlockSpec(memory_space=pl.ANY)]
    specs = ([] if scalars is None else [smem()]) + vmem(len(arrays) - left) + stay * left
    out_specs = vmem(len(outs) - left_out) + stay * left_out
    return pl.pallas_call(
        kernel,
        out_shape=out_shape,
        in_specs=specs,
        out_specs=tuple(out_specs) if isinstance(out_shape, (tuple, list)) else out_specs[0],
        scratch_shapes=list(scratch),
        compiler_params=pltpu.CompilerParams(vmem_limit_bytes=56 * 1024 * 1024),
        cost_estimate=pl.CostEstimate(flops=flops, bytes_accessed=moved, transcendentals=0),
        name=name,
    )(*given)


def shape(*dims, dtype=BF):
    return jax.ShapeDtypeStruct(dims, dtype)


def column_info(scalars, marks_ref, kv_ref):
    lo_idx = scalars[0]
    first_len = kv_ref[0, TOK : TOK + 16, 0:128].astype(F32)[0:1, :].astype(jnp.int32)
    first_len = jnp.concatenate([first_len] * (2 * GROUP), axis=1)
    hi, lo = marks_ref[1 - lo_idx, 0:1, :], marks_ref[lo_idx, 0:1, :]
    marks = jnp.concatenate([hi] * GROUP + [lo] * GROUP, axis=1)
    first_key = jnp.where(marks < 0, first_len, marks)
    lane = lax.broadcasted_iota(jnp.int32, (1, 2 * COLS), 1)
    start = jnp.where(lane < COLS, scalars[2], scalars[1]) * CHUNK
    return first_key, start + lax.rem(lane, CHUNK)


def full_mask(tile, first_key, place, rows, cols):
    keys = tile * TOK + lax.broadcasted_iota(jnp.int32, (rows, cols), 0)
    return (keys >= first_key[:, :cols]) & (keys <= place[:, :cols])


def tiles(scalars, step, most, upper):
    lo_diag = scalars[1] // 2
    hi_diag = scalars[2] // 2
    joint = jnp.maximum(lo_diag - 1, 0)
    single = hi_diag - lo_diag - 1

    @pl.loop(0, jnp.where(lo_diag > 0, 2, 1))
    def _(j):
        step(j * lo_diag, 1, 2 * COLS, True)

    @pl.loop(0, joint // 2)
    def _(j):
        step(1 + 2 * j, 2, 2 * COLS, False)

    @pl.when(joint % 2 == 1)
    def _():
        step(lo_diag - 1, 1, 2 * COLS, False)

    upper()

    @pl.loop(0, single // most)
    def _(j):
        step(lo_diag + 1 + most * j, most, COLS, False)

    if most == 4:

        @pl.when(single % 4 == 2)
        def _():
            step(hi_diag - 2, 2, COLS, False)

    step(hi_diag, 1, COLS, True)


def gather_columns(cat_ref, source_ref, scalars, first_row):
    cat_ref[...] = jnp.zeros_like(cat_ref)
    lo_idx = scalars[0]
    for part in range(2):
        index = (1 - lo_idx) if part == 0 else lo_idx
        lanes = pl.ds(pl.multiple_of(index * CHUNK, CHUNK), CHUNK)
        for head in range(H):
            at = part * COLS + (head % GROUP) * CHUNK
            block = source_ref[head * HD : (head + 1) * HD, lanes]
            cat_ref[head // GROUP, first_row : first_row + HD, at : at + CHUNK] = block


def scatter_columns(out_ref, values, group, scalars):
    lo_idx = scalars[0]
    for part in range(2):
        index = (1 - lo_idx) if part == 0 else lo_idx
        lanes = pl.ds(pl.multiple_of(index * CHUNK, CHUNK), CHUNK)
        for j in range(GROUP):
            head = group * GROUP + j
            at = part * COLS + j * CHUNK
            out_ref[head * HD : (head + 1) * HD, lanes] = values[:, at : at + CHUNK]


def fetch(source, target, sems):
    half = UNITS // 2
    copies = [
        pltpu.make_async_copy(source.at[pl.ds(i * half, half)], target.at[pl.ds(i * half, half)], sems.at[i])
        for i in range(2)
    ]
    for copy in copies:
        copy.start()
    return copies[0].wait, copies[1].wait


def forward_kernel(scalars, marks_ref, q_ref, kv_hbm, out_ref, lse_ref, qcat, acc, run_max, kv_ref, sems):
    lower, upper = fetch(kv_hbm, kv_ref, sems)
    gather_columns(qcat, q_ref, scalars, 0)
    lower()
    first_key, place = column_info(scalars, marks_ref, kv_ref)
    acc[...] = jnp.zeros_like(acc)
    run_max[...] = jnp.full_like(run_max, MASKED)

    def step(tile, count, cols, whole):
        rows = count * TOK
        if whole:
            allowed = full_mask(tile, first_key, place, rows, cols)
        else:
            seen = first_key[:, :cols] <= tile * TOK
        blocks = [kv_ref[pl.ds(tile, count), 0:TOK, g * 128 : (g + 1) * 128].reshape(rows, 128) for g in range(KVH)]
        all_scores = [mm(blocks[g], qcat[g, :, 0:cols]) * LOG2E for g in range(KVH)]
        all_values = [
            jnp.concatenate([jnp.ones((16, rows), BF), jnp.transpose(block)[HD:, :]], axis=0) for block in blocks
        ]
        factors, all_weights = [], []
        for g in range(KVH):
            scores = all_scores[g]
            old_max = run_max[g, 0:1, 0:cols]
            if whole:
                scores = jnp.where(allowed, scores, MASKED)
                new_max = jnp.maximum(old_max, jnp.max(scores, axis=0, keepdims=True))
                shift = new_max
            else:
                new_max = jnp.maximum(old_max, jnp.max(scores, axis=0, keepdims=True))
                new_max = jnp.where(seen, new_max, old_max)
                shift = jnp.where(seen, new_max, -MASKED)
            all_weights.append(jnp.exp2(scores - shift).astype(BF))
            factors.append(jnp.exp2(old_max - new_max))
            run_max[g, 0:1, 0:cols] = new_max
        for g in range(KVH):
            acc[g, :, 0:cols] = acc[g, :, 0:cols] * factors[g] + mm(all_values[g], all_weights[g])

    tiles(scalars, step, 4, upper)
    for g in range(KVH):
        total = acc[g, 0:1, :]
        scatter_columns(out_ref, acc[g, 16:, :] / total, g, scalars)
        lse_ref[g] = jnp.broadcast_to(run_max[g, 0:1, :] + jnp.log2(total), (8, 2 * COLS))


def backward_kernel(
    scalars, marks_ref, q_ref, do_ref, out_ref, lse_ref, kv_hbm, dq_ref, mine_ref, other_ref,
    qcat, docat, acc, delta, kv_ref, grads_ref, sems,
):
    lower, upper = fetch(kv_hbm, kv_ref, sems)
    gather_columns(qcat, q_ref, scalars, 0)
    gather_columns(docat, do_ref, scalars, HD)
    lower()
    first_key, place = column_info(scalars, marks_ref, kv_ref)
    lo_idx = scalars[0]
    hi_diag = scalars[2] // 2
    my_x, my_z, my_c = scalars[3], scalars[4], scalars[5]
    acc[...] = jnp.zeros_like(acc)
    for part in range(2):
        index = (1 - lo_idx) if part == 0 else lo_idx
        lanes = pl.ds(pl.multiple_of(index * CHUNK, CHUNK), CHUNK)
        for head in range(H):
            rows = slice(head * HD, (head + 1) * HD)
            at = part * COLS + (head % GROUP) * CHUNK
            terms = do_ref[rows, lanes].astype(F32) * out_ref[rows, lanes]
            delta[head // GROUP, 0:1, at : at + CHUNK] = jnp.sum(terms, axis=0, keepdims=True)

    def store(tile, grads):
        mirrored = UNITS - 1 - tile
        kx, kz = (tile // 8 - my_x) & 3, ((tile // 2) % 4 - my_z) & 3
        mx, mz = (mirrored // 8 - my_x) & 3, ((mirrored // 2) % 4 - my_z) & 3
        same = lax.rem(tile, 2) == my_c

        for half in range(2):
            for g, grad in enumerate(grads):
                rows = slice(g * CHUNK, (g + 1) * CHUNK)
                grads_ref[tile, half, rows, :] = grad[half * CHUNK : (half + 1) * CHUNK]

        def send(first_ref, second_ref):
            pltpu.make_async_copy(grads_ref.at[tile, 0], first_ref.at[0, kx, kz], sems.at[2]).start()
            pltpu.make_async_copy(grads_ref.at[tile, 1], second_ref.at[1, mz, mx], sems.at[2]).start()

        @pl.when(same)
        def _():
            send(mine_ref, other_ref)

        @pl.when(jnp.logical_not(same))
        def _():
            send(other_ref, mine_ref)

    def step(tile, count, cols, whole):
        rows = count * TOK
        if whole:
            allowed = full_mask(tile, first_key, place, rows, cols)
        else:
            seen = first_key[:, :cols] <= tile * TOK
        all_grads, all_probs, all_grad_scores = [], [], []
        blocks = [kv_ref[pl.ds(tile, count), 0:TOK, g * 128 : (g + 1) * 128].reshape(rows, 128) for g in range(KVH)]
        all_scores = [mm(blocks[g], qcat[g, :, 0:cols]) * LOG2E for g in range(KVH)]
        all_grad_probs = [mm(blocks[g], docat[g, :, 0:cols]) for g in range(KVH)]
        for g in range(KVH):
            scores = all_scores[g]
            shift = lse_ref[g, 0:1, 0:cols]
            if whole:
                scores = jnp.where(allowed, scores, MASKED)
            else:
                shift = jnp.where(seen, shift, -MASKED)
            probs = jnp.exp2(scores - shift)
            all_grad_scores.append((probs * (all_grad_probs[g] - delta[g, 0:1, 0:cols])).astype(BF))
            all_probs.append(probs.astype(BF))
        for g in range(KVH):
            all_grads.append(
                mm(all_grad_scores[g], qcat[g, :, 0:cols], NT) + mm(all_probs[g], docat[g, :, 0:cols], NT)
            )
            keys = jnp.transpose(blocks[g])[0:HD, :]
            acc[g, :, 0:cols] = acc[g, :, 0:cols] + mm(keys, all_grad_scores[g])
        for i in range(count):
            store(tile + i, [grad[i * TOK : (i + 1) * TOK].astype(BF) for grad in all_grads])

    tiles(scalars, step, 2, upper)

    @pl.loop(hi_diag + 1, UNITS)
    def _(t):
        store(t, [jnp.zeros((TOK, 128), BF)] * KVH)

    for g in range(KVH):
        scatter_columns(dq_ref, acc[g] * SCALE, g, scalars)
    pltpu.make_async_copy(grads_ref, grads_ref, sems.at[2]).wait()


def attend(scalars, marks, queries, keys_values):
    return call(
        forward_kernel,
        "attention_forward",
        (shape(D, TOK, dtype=F32), shape(KVH, 8, 2 * COLS, dtype=F32)),
        scalars,
        (marks, queries, keys_values),
        (
            pltpu.VMEM((KVH, 128, 2 * COLS), BF),
            pltpu.VMEM((KVH, 16 + HD, 2 * COLS), F32),
            pltpu.VMEM((KVH, 8, 2 * COLS), F32),
            pltpu.VMEM(keys_values.shape, BF),
            pltpu.SemaphoreType.DMA((2,)),
        ),
        flops=20 * 10**9,
        moved=7 * 10**6,
        left=1,
    )


def attend_back(scalars, marks, queries, grad_out, attended, norm, keys_values):
    blocks = shape(2, 4, 4, KVH * CHUNK, 128)
    return call(
        backward_kernel,
        "attention_backward",
        (shape(D, TOK, dtype=F32), blocks, blocks),
        scalars,
        (marks, queries, grad_out, attended, norm, keys_values),
        (
            pltpu.VMEM((KVH, 128, 2 * COLS), BF),
            pltpu.VMEM((KVH, 128, 2 * COLS), BF),
            pltpu.VMEM((KVH, HD, 2 * COLS), F32),
            pltpu.VMEM((KVH, 8, 2 * COLS), F32),
            pltpu.VMEM(keys_values.shape, BF),
            pltpu.VMEM((UNITS, 2, KVR, 128), BF),
            pltpu.SemaphoreType.DMA((3,)),
        ),
        left=1,
        left_out=2,
        flops=40 * 10**9,
        moved=24 * 10**6,
    )


def inverse_rms(values):
    return lax.rsqrt(jnp.mean(values * values, axis=0, keepdims=True) + EPSILON)


def rotated(values, turn, sign):
    cosine, sine = turn[0], turn[1] * sign
    first, second = values[:HALF], values[HALF:]
    return jnp.concatenate([first * cosine - second * sine, second * cosine + first * sine], axis=0)


def row_sums(values):
    ones = jnp.ones((16, values.shape[1]), BF)
    high = values.astype(BF)
    low = (values - high.astype(F32)).astype(BF)
    return mm(ones, high, NT) + mm(ones, low, NT)


def column(ref):
    row = ref[...].reshape(1, ref.shape[0])
    return jnp.transpose(jnp.broadcast_to(row, (8, ref.shape[0])))[:, 0:1]


def keys_kernel(x_ref, gain_ref, cos_ref, sin_ref, key_ref, value_ref, seg_ref, place_ref, out_ref, act_ref):
    x = x_ref[...].astype(F32)
    act = (x * inverse_rms(x) * column(gain_ref)).astype(BF)
    act_ref[...] = act
    keys = mm(key_ref[...], act)
    values = mm(value_ref[...], act)
    turn = (cos_ref[...], sin_ref[...])
    for g in range(KVH):
        rows = slice(g * HD, (g + 1) * HD)
        block = jnp.concatenate([rotated(keys[rows], turn, 1.0), values[rows]], axis=0)
        out_ref[0:TOK, g * 128 : (g + 1) * 128] = jnp.transpose(block).astype(BF)
    first_len = jnp.sum((seg_ref[...] == 0).astype(F32), axis=1, keepdims=True)
    row = lax.broadcasted_iota(jnp.int32, (16, TOK), 0)
    places = place_ref[...]
    places = jnp.where(row < 12, places >> 6, places & 63).astype(F32)
    out_ref[TOK:, 0:TOK] = jnp.where(row < 8, first_len, places).astype(BF)
    out_ref[TOK:, TOK:] = jnp.zeros((16, 2 * KVW - TOK), BF)


def queries_kernel(x_ref, gain_ref, cos_ref, sin_ref, weight_ref, act_ref, out_ref):
    x = x_ref[...].astype(F32)
    act = (x * inverse_rms(x) * column(gain_ref)).astype(BF)
    act_ref[...] = act
    queries = mm(weight_ref[...], act, TN)
    turn = (cos_ref[...], sin_ref[...])
    for head in range(H):
        rows = slice(head * HD, (head + 1) * HD)
        low = rotated(queries[rows], turn, 1.0).astype(BF)
        out_ref[rows, :] = low * jnp.asarray(SCALE, BF)


def mlp_kernel(
    scalars, x_ref, c_ref, attn_ref, gain_ref, out_weight, gate_ref, up_ref, down_ref,
    result_ref, dmid_ref, dattn_ref, ggain_ref, mine_ref, other_ref,
    mid, act, act_cols, c_cols, result, dact, shards, sems,
):
    block = pl.program_id(0)
    my_c = scalars[5]

    def put(group, values):
        for k in range(values.shape[1] // 128):
            for i in range(values.shape[0] // SHARD):
                j = k * (values.shape[0] // SHARD) + i
                piece = values[i * SHARD : (i + 1) * SHARD, k * 128 : (k + 1) * 128]
                shards[group + j // 8, j % 8] = piece

    def send(group):
        @pl.when(group // 16 == my_c)
        def _():
            pltpu.make_async_copy(shards.at[group], mine_ref.at[group % 16], sems.at[0]).start()

        @pl.when(group // 16 != my_c)
        def _():
            pltpu.make_async_copy(shards.at[group], other_ref.at[group % 16], sems.at[1]).start()

    @pl.when(block == 0)
    def _():
        low = attn_ref[...].astype(BF)
        middle = x_ref[...].astype(F32) + mm(out_weight[...], low, TN)
        mid[...] = middle
        normal = (middle * inverse_rms(middle) * column(gain_ref)).astype(BF)
        act_cols[...] = normal
        act[...] = jnp.transpose(normal)
        c_cols[...] = jnp.transpose(c_ref[...])
        result[...] = jnp.zeros_like(result)
        dact[...] = jnp.zeros_like(dact)

    gate = mm(act[...], gate_ref[...])
    up = mm(act[...], up_ref[...])
    sigmoid = 1.0 / (1.0 + jnp.exp(-gate))
    silu = gate * sigmoid
    hidden = (silu * up).astype(BF)
    dhidden = mm(c_cols[...], down_ref[...])
    dup = (dhidden * silu).astype(BF)
    dgate = (dhidden * up * (sigmoid * (1.0 + gate * (1.0 - sigmoid)))).astype(BF)
    result[...] += mm(down_ref[...], hidden, NT)
    put(block * 9, mm(act_cols[...], dgate).astype(BF))
    put(block * 9 + 3, mm(act_cols[...], dup).astype(BF))
    put(block * 9 + 6, mm(c_ref[...], hidden).astype(BF))
    for group in range(9):
        send(block * 9 + group)
    dact[...] += mm(gate_ref[...], dgate, NT) + mm(up_ref[...], dup, NT)

    @pl.when(block == FF // FF_BLOCK - 1)
    def _():
        middle = mid[...]
        gain = column(gain_ref)
        rms = inverse_rms(middle)
        grads = dact[...]
        result_ref[...] = (middle + result[...]).astype(BF)
        ggain_ref[...] = row_sums(grads * middle * rms)
        pulled = grads * gain
        inner = jnp.mean(pulled * middle, axis=0, keepdims=True)
        dmid = c_ref[...].astype(F32) + (pulled * rms - middle * (rms * rms * rms * inner))
        dmid_ref[...] = dmid
        low = dmid.astype(BF)
        dattn_ref[...] = mm(out_weight[...], low).astype(BF)
        gout = mm(attn_ref[...].astype(BF), low, NT).astype(BF)
        put(27, gout[:, :512])
        shards[30:32] = jnp.zeros((2, 8, SHARD, 128), BF)
        put(30, jnp.concatenate([gout[: D // 2, 512:], gout[D // 2 :, 512:]], axis=1))
        for group in range(27, 32):
            send(group)
        for i, ref in enumerate((mine_ref, other_ref)):
            pltpu.make_async_copy(ref, ref, sems.at[i]).wait()


def feed_forward(scalars, x, cotangent, attended, gain, out_weight, gate_weight, up_weight, down_weight):
    whole = lambda *dims: pl.BlockSpec(dims, lambda f: (0,) * len(dims))
    part = pl.BlockSpec((D, FF_BLOCK), lambda f: (0, f))
    return pl.pallas_call(
        mlp_kernel,
        grid=(FF // FF_BLOCK,),
        out_shape=(shape(D, TOK), shape(D, TOK, dtype=F32), shape(D, TOK), shape(16, D, dtype=F32))
        + (shape(GROUPS // 2, 8, SHARD, 128),) * 2,
        in_specs=[smem(), whole(D, TOK), whole(D, TOK), whole(D, TOK), whole(D), whole(D, D), part, part, part],
        out_specs=(whole(D, TOK), whole(D, TOK), whole(D, TOK), whole(16, D))
        + (pl.BlockSpec(memory_space=pl.ANY),) * 2,
        scratch_shapes=[
            pltpu.VMEM((D, TOK), F32), pltpu.VMEM((TOK, D), BF), pltpu.VMEM((D, TOK), BF),
            pltpu.VMEM((TOK, D), BF), pltpu.VMEM((D, TOK), F32), pltpu.VMEM((D, TOK), F32),
            pltpu.VMEM((GROUPS, 8, SHARD, 128), BF), pltpu.SemaphoreType.DMA((2,)),
        ],
        compiler_params=pltpu.CompilerParams(vmem_limit_bytes=56 * 1024 * 1024),
        cost_estimate=pl.CostEstimate(flops=5 * 10**9, bytes_accessed=14 * 10**6, transcendentals=10**6),
        name="feed_forward",
    )(scalars, x, cotangent, attended, gain, out_weight, gate_weight, up_weight, down_weight)


def early_finish_kernel(scalars, source, gate_ref, up_ref, down_ref, out_ref, shards, sems):
    block = pl.program_id(0)
    my_y = scalars[6]

    def part(core, y):
        return shards.at[core, pl.ds(y * 16, 16)]

    @pl.when(block == 0)
    def _():
        for core in range(2):
            for k in range(4):
                y = (my_y - k) & 3
                pltpu.make_async_copy(source.at[:, core, k], part(core, y), sems.at[core, y]).start()

    needed = (((0, 0), (0, 1), (0, 2)), ((0, 3), (1, 0)), ((1, 1), (1, 2), (1, 3)))
    for step, places in enumerate(needed):

        @pl.when(block == step)
        def _():
            for core, y in places:
                pltpu.make_async_copy(part(core, y), part(core, y), sems.at[core, y]).wait()

    def get(group, k, i):
        piece = group * 8 + D // SHARD * k + i
        half, piece = piece // (GROUPS * 4), piece % (GROUPS * 4)
        return shards[half, piece // 2, piece % 2].astype(F32)

    for kind, ref in enumerate((gate_ref, up_ref, down_ref)):
        for k in range(4):
            for i in range(D // SHARD):
                ref[i * SHARD : (i + 1) * SHARD, k * 128 : (k + 1) * 128] = get(block * 9 + kind * 3, k, i)

    @pl.when(block == FF // FF_BLOCK - 1)
    def _():
        for k in range(4):
            for i in range(D // SHARD):
                out_ref[i * SHARD : (i + 1) * SHARD, k * 128 : (k + 1) * 128] = get(27, k, i)
        rest = jnp.concatenate([get(30, 0, i) for i in range(3)], axis=0)
        out_ref[:, 512:] = jnp.concatenate([rest[:, :HD], rest[:, HD:]], axis=0)


def early_finish(scalars, source):
    part = pl.BlockSpec((D, FF_BLOCK), lambda f: (0, f))
    return pl.pallas_call(
        early_finish_kernel,
        grid=(FF // FF_BLOCK,),
        out_shape=(shape(D, FF, dtype=F32),) * 3 + (shape(D, D, dtype=F32),),
        in_specs=[smem(), pl.BlockSpec(memory_space=pl.ANY)],
        out_specs=(part, part, part, pl.BlockSpec((D, D), lambda f: (0, 0))),
        scratch_shapes=[pltpu.VMEM((2, 64, 2, SHARD, 128), BF), pltpu.SemaphoreType.DMA((2, 4))],
        compiler_params=pltpu.CompilerParams(vmem_limit_bytes=56 * 1024 * 1024),
        cost_estimate=pl.CostEstimate(flops=10**7, bytes_accessed=19 * 10**6, transcendentals=0),
        name="early_gradients",
    )(scalars, source)


def late_rows():
    return 0, 2592, 4320, 4400


def pack(buffer, at, values):
    count = values.shape[0]
    for k in range(4):
        buffer[at + k * count : at + (k + 1) * count, :] = values[:, k * 128 : (k + 1) * 128]
    if count > 16:
        rest = jnp.concatenate([values[: count // 2, 512:], values[count // 2 :, 512:]], axis=1)
        buffer[at + 4 * count : at + 4 * count + count // 2, :] = rest
    else:
        buffer[at + 4 * count : at + 5 * count, 0:64] = values[:, 512:]


def unpack(buffer, at, count):
    blocks = [buffer[at + k * count : at + (k + 1) * count, :] for k in range(4)]
    if count > 16:
        rest = buffer[at + 4 * count : at + 4 * count + count // 2, :]
        rest = jnp.concatenate([rest[:, :64], rest[:, 64:]], axis=0)
    else:
        rest = buffer[at + 4 * count : at + 5 * count, 0:64]
    return jnp.concatenate(blocks + [rest], axis=1)


def late_kernel(
    scalars, acts_ref, cos_all, sin_all, first_mine, second_mine, first_other, second_other, dq_ref, cos_ref, sin_ref, act_ref, weight_ref,
    key_ref, value_ref, gain_ref, ggain_ref, dact_ref, mine_ref, other_ref, late, gkv,
):
    block = pl.program_id(0)
    my_x, my_z, my_c = scalars[3], scalars[4], scalars[5]

    @pl.when(block == 0)
    def _():
        gkv[...] = jnp.zeros_like(gkv)

    total = None
    for kz in range(4):
        z = (my_z + kz) & 3
        mz = (3 - z - my_z) & 3
        for core, first_ref, second_ref in ((my_c, first_mine, second_other), (1 - my_c, first_other, second_mine)):
            unit = z * 2 + core
            first, second = first_ref[0, 0, kz], second_ref[0, mz, 0]
            lanes = pl.ds(pl.multiple_of(unit * TOK, TOK), TOK)
            turn = (cos_all[:, lanes], sin_all[:, lanes])
            turned = []
            for g in range(KVH):
                rows = slice(g * CHUNK, (g + 1) * CHUNK)
                grads = jnp.concatenate([jnp.transpose(first[rows]), jnp.transpose(second[rows])], axis=1)
                turned.append(rotated(grads[0:HD].astype(F32), turn, -1.0).astype(BF))
                turned.append(grads[HD:])
            product = mm(acts_ref[unit], jnp.concatenate(turned, axis=0), NT)
            total = product if total is None else total + product
    gkv[...] += total

    @pl.when(block == 3)
    def _():
        turn = (cos_ref[...], sin_ref[...])
        heads = [rotated(dq_ref[h * HD : (h + 1) * HD, :], turn, -1.0).astype(BF) for h in range(H)]
        low = jnp.concatenate(heads, axis=0)
        weight = weight_ref[...]
        gquery = mm(act_ref[...], low, NT)
        dact_ref[...] = mm(weight, low)
        at_q, at_kv, at_n, at_m = late_rows()
        late[at_n:, :] = jnp.zeros((32 * LATE_SHARD - at_n, 128), BF)
        pack(late, at_q, gquery.astype(BF))
        gain = row_sums(gquery * weight.astype(F32))
        for g in range(KVH):
            rows = slice(g * HD, (g + 1) * HD)
            grad = gkv[:, g * 128 : (g + 1) * 128]
            late[at_kv + g * D : at_kv + (g + 1) * D, :] = grad.astype(BF)
            columns = jnp.transpose(jnp.concatenate([key_ref[rows, :], value_ref[rows, :]], axis=0))
            gain = gain + row_sums(grad * columns.astype(F32))
        pack(late, at_n, (gain / gain_ref[...].reshape(1, D)).astype(BF))
        pack(late, at_m, ggain_ref[...].astype(BF))
        for x in range(4):
            for z in range(4):
                index = ((x - my_x) & 3, (z - my_z) & 3)
                for target, core in ((mine_ref, my_c), (other_ref, 1 - my_c)):
                    at = ((core * 4 + x) * 4 + z) * LATE_SHARD
                    target[index] = late[pl.ds(pl.multiple_of(at, LATE_SHARD), LATE_SHARD), :]


def late_gradients(scalars, acts, table, mine, other, *arrays):
    whole = lambda array: pl.BlockSpec(array.shape, lambda k, s: (0,) * len(array.shape))
    mirrored = lambda k, s: (3 - ((s[3] + k) & 3) - s[3]) & 3
    unit = (KVH * CHUNK, 128)
    first = pl.BlockSpec((1, 1, 4) + unit, lambda k, s: (0, k, 0, 0, 0))
    second = pl.BlockSpec((1, 4, 1) + unit, lambda k, s: (1, 0, mirrored(k, s), 0, 0))
    outs = (shape(D, TOK, dtype=F32),) + (shape(4, 4, LATE_SHARD, 128),) * 2
    return pl.pallas_call(
        late_kernel,
        grid_spec=pltpu.PrefetchScalarGridSpec(
            num_scalar_prefetch=1,
            grid=(4,),
            in_specs=[pl.BlockSpec((8, D, TOK), lambda k, s: ((s[3] + k) & 3, 0, 0))]
            + [pl.BlockSpec((HALF, 8 * TOK), lambda k, s: (0, (s[3] + k) & 3))] * 2
            + [first, second, first, second]
            + [whole(array) for array in arrays],
            out_specs=tuple(whole(out) for out in outs),
            scratch_shapes=[pltpu.VMEM((32 * LATE_SHARD, 128), BF), pltpu.VMEM((D, 2 * KVW), F32)],
        ),
        out_shape=outs,
        compiler_params=pltpu.CompilerParams(vmem_limit_bytes=56 * 1024 * 1024),
        cost_estimate=pl.CostEstimate(flops=4 * 10**9, bytes_accessed=20 * 10**6, transcendentals=0),
        name="late_gradients",
    )(scalars, acts, *table, mine, mine, other, other, *arrays)


def join_kernel(mine_ref, came_ref, late_mine, late_came, *outs):
    j = pl.program_id(0)
    first, second = slice(0, LATE_SPLIT), slice(LATE_SPLIT, LATE_SHARD)
    for k, at in ((0, 0), (1, 1), (3, 4)):
        outs[at][0, 0:KVR, :] = add(mine_ref[0, k, 0], came_ref[0, k, 0])
        outs[at][0, KVR:, :] = add(late_mine[k, j, first], late_came[k, j, first])
        outs[5 + at][0, 0:KVR, :] = add(mine_ref[1, k, 0], came_ref[1, k, 0])
        outs[5 + at][0, KVR:, :] = add(late_mine[j, k, second], late_came[j, k, second])
    lower, upper = slice(0, FORWARD), slice(FORWARD, KVR)
    for half, at, late_at, span in ((0, 2, (2, j), first), (1, 7, (j, 2), second)):
        outs[at][0] = add(mine_ref[half, 2, 0, lower], came_ref[half, 2, 0, lower])
        outs[at + 1][0, 0 : KVR - FORWARD, :] = add(mine_ref[half, 2, 0, upper], came_ref[half, 2, 0, upper])
        outs[at + 1][0, KVR - FORWARD :, :] = add(late_mine[late_at + (span,)], late_came[late_at + (span,)])


def join(mine, came, late_mine, late_came):
    part = pl.BlockSpec((2, 4, 1, KVR, 128), lambda j: (0, 0, j, 0, 0))
    late = pl.BlockSpec(late_mine.shape, lambda j: (0, 0, 0, 0))
    heights = ()
    for rows in (KVR + LATE_SPLIT, KVR + LATE_SHARD - LATE_SPLIT):
        heights += (rows, rows, FORWARD, rows - FORWARD, rows)
    return pl.pallas_call(
        join_kernel,
        grid=(4,),
        out_shape=tuple(shape(4, rows, 128) for rows in heights),
        in_specs=[part, part, late, late],
        out_specs=tuple(pl.BlockSpec((1, rows, 128), lambda j: (j, 0, 0)) for rows in heights),
        compiler_params=pltpu.CompilerParams(vmem_limit_bytes=56 * 1024 * 1024),
        cost_estimate=pl.CostEstimate(flops=10**7, bytes_accessed=11 * 10**6, transcendentals=0),
        name="join",
    )(mine, came, late_mine, late_came)


def late_finish_kernel(scalars, own_ref, came_ref, gquery_ref, gkey_ref, gvalue_ref, gnorm_ref, gmlp_ref, late):
    my_x, my_z, my_c = scalars[3], scalars[4], scalars[5]
    for source, core in ((own_ref, my_c), (came_ref, 1 - my_c)):
        for x in range(4):
            for z in range(4):
                at = ((core * 4 + ((my_x - x) & 3)) * 4 + ((my_z - z) & 3)) * LATE_SHARD
                late[pl.ds(pl.multiple_of(at, LATE_SHARD), LATE_SHARD), :] = source[x, z]
    at_q, at_kv, at_n, at_m = late_rows()
    gquery_ref[...] = unpack(late, at_q, D).astype(F32)
    for g in range(KVH):
        grad = jnp.transpose(late[at_kv + g * D : at_kv + (g + 1) * D, :].astype(F32))
        gkey_ref[g * HD : (g + 1) * HD, :] = grad[:HD]
        gvalue_ref[g * HD : (g + 1) * HD, :] = grad[HD:]
    gnorm_ref[...] = unpack(late, at_n, 16).astype(F32)[0]
    gmlp_ref[...] = unpack(late, at_m, 16).astype(F32)[0]


def tail_kernel(
    a0, a1, a2, a3, b0, b1, b2, b3, cos_ref, sin_ref, x_ref, gain_ref, key_ref, value_ref, dact_ref, dmid_ref, grad_ref
):
    turn = (cos_ref[...], sin_ref[...])
    summed = []
    for parts in ((a0, a1, a2, a3), (b0, b1, b2, b3)):
        total = parts[0][0 : KVR, :].astype(F32)
        for part in parts[1:]:
            total = total + part[0 : KVR, :].astype(F32)
        summed.append(total)
    keys, values = [], []
    for g in range(KVH):
        columns = [jnp.transpose(t[g * CHUNK : (g + 1) * CHUNK, :]) for t in summed]
        columns = jnp.concatenate(columns, axis=1)
        keys.append(rotated(columns[:HD], turn, -1.0).astype(BF))
        values.append(columns[HD:].astype(BF))
    keys, values = jnp.concatenate(keys, axis=0), jnp.concatenate(values, axis=0)
    grads = dact_ref[...] + mm(key_ref[...], keys, TN) + mm(value_ref[...], values, TN)
    x = x_ref[...].astype(F32)
    rms = inverse_rms(x)
    pulled = grads * column(gain_ref)
    inner = jnp.mean(pulled * x, axis=0, keepdims=True)
    grad_ref[...] = (dmid_ref[...] + (pulled * rms - x * (rms * rms * rms * inner))).astype(BF)


def shift(values, axis, by):
    return lax.ppermute(values, axis, [(i, (i + by) % 4) for i in range(4)])


def swap(values):
    return lax.ppermute(values, "core", [(0, 1), (1, 0)])


def mirror(values):
    return lax.ppermute(values, SEQ, [(i, UNITS - 1 - i) for i in range(UNITS)])


def zigzag(values):
    return jnp.concatenate([values[:, :CHUNK], mirror(values[:, CHUNK:])], axis=1)


def add(*parts):
    parts = [p.astype(F32) for p in parts]
    total = parts[0] + parts[1] if len(parts) == 2 else (parts[0] + parts[2]) + (parts[1] + parts[3])
    return total.astype(BF)


def spread(parts, axis):
    return [parts[0]] + [shift(parts[k], axis, k) for k in (1, 2, 3)]


def pass_on(parts, axis):
    own, near, far_lower, far_upper, back = parts
    forward, backward = shift(far_lower, axis, 1), shift(far_upper, axis, 3)

    def rest():
        ahead = jnp.concatenate([add(near[:, :FORWARD], forward), near[:, FORWARD:]], axis=1)
        behind = jnp.concatenate([back[:, :FORWARD], add(back[:, FORWARD:], backward)], axis=1)
        return own, shift(ahead, axis, 1), shift(behind, axis, 3)

    return rest


def add_three(*parts):
    return (parts[0].astype(F32) + (parts[1].astype(F32) + parts[2].astype(F32))).astype(BF)


def collect(values, axis):
    return [values] + [shift(values, axis, k) for k in (1, 2, 3)]


def turns(places):
    freqs = ROPE_BASE ** (-2.0 * jnp.arange(HALF).astype(F32) / HD)
    angles = freqs[:, None] * places.astype(F32)
    return jnp.cos(angles), jnp.sin(angles)


def body(
    tokens,
    segments,
    positions,
    norm_gain,
    query_weight,
    key_weight,
    value_weight,
    output_weight,
    mlp_gain,
    gate_weight,
    up_weight,
    down_weight,
    cotangent,
):
    axis = {name: lax.axis_index(name) for name in ALL}
    at = {name: index.reshape(1) for name, index in axis.items()}
    unit = (axis["x"] * 4 + axis["z"]) * 2 + axis["core"]
    x_own = tokens[0].T
    key_cols, value_cols, down_cols = key_weight.T, value_weight.T, down_weight.T

    packed, own_act = call(
        keys_kernel, "keys_values", (shape(PADROWS, 2 * KVW), shape(D, TOK)), None,
        (x_own, norm_gain, *turns(positions), key_cols, value_cols, segments, positions),
    )
    gathered = lax.all_gather(packed, SEQ, axis=0, tiled=False)
    acts = lax.all_gather(own_act, SEQ, axis=0, tiled=False)
    x_own, segments, positions, packed = lax.optimization_barrier((x_own, segments, positions, packed))

    third = TOK * unit + jnp.sum((segments < 2).astype(jnp.int32))
    marks = jnp.where(segments == 2, third, jnp.where(segments == 1, -64, 0))
    ints = jnp.concatenate([positions >> 6, positions & 63, marks >> 6, marks & 63], axis=0)
    ints = jnp.pad(ints, ((0, 12), (0, 0))).astype(BF)
    both = zigzag(jnp.concatenate([x_own, cotangent[0].T, ints], axis=0))
    x, out_grad = both[:D], both[D : 2 * D]
    ints = both[2 * D :].astype(jnp.int32)
    places = ints[0:1] * 64 + ints[1:2]
    marks = ints[2:3] * 64 + ints[3:4]
    marks = jnp.broadcast_to(marks.reshape(2, 1, CHUNK), (2, 8, CHUNK))
    chunk_a, chunk_b = 2 * unit, 2 * UNITS - 1 - 2 * unit
    scalars = jnp.stack([
        (chunk_a > chunk_b).astype(jnp.int32), jnp.minimum(chunk_a, chunk_b), jnp.maximum(chunk_a, chunk_b),
        axis["x"], axis["z"], axis["core"], axis["dp"],
    ])
    turn = turns(places)
    act, queries = call(
        queries_kernel, "queries", (shape(D, TOK), shape(D, TOK)), None, (x, norm_gain, *turn, query_weight)
    )

    attended, norm = attend(scalars, marks, queries, gathered)
    result, dmid, dattn, ggain, mine, other = feed_forward(
        scalars, x, out_grad, attended, mlp_gain, output_weight, gate_weight, up_weight, down_cols
    )

    came = swap(other)
    row_places = gathered[:, TOK + 8, :TOK].astype(F32) * 64 + gathered[:, TOK + 12, :TOK].astype(F32)
    table = turns(row_places.reshape(1, UNITS * TOK))
    came, table = lax.optimization_barrier((came, table))
    early = add(mine, came)
    early, dattn = lax.optimization_barrier((early, dattn))
    early = lax.all_to_all(early.reshape(64, 2, SHARD, 128), CHIPS, 0, 0, tiled=True)

    dq, mine, other = attend_back(scalars, marks, queries, dattn, attended, norm, gathered)

    came = swap(other)
    dact, late_mine, late_other = late_gradients(
        scalars, acts, table, mine, other, dq, *turn, act, query_weight, key_cols, value_cols, norm_gain, ggain
    )
    early, late_mine, late_other = lax.optimization_barrier((early, late_mine, late_other))
    late_came = swap(late_other)
    early_came = collect(jnp.sum(early.astype(F32), axis=0).astype(BF), "dp")
    halves = join(mine, came, late_mine, late_came)
    halves, early_came = lax.optimization_barrier((halves, early_came))
    early = lax.all_gather(jnp.stack(early_came), SEQ, axis=0, tiled=False)
    first_rest, second_rest = pass_on(halves[:5], "x"), pass_on(halves[5:], "z")
    first_came, second_came = first_rest(), second_rest()
    first = [add_three(*(c[k] for c in first_came)) for k in range(4)]
    second = [add_three(*(c[k] for c in second_came)) for k in range(4)]
    first, second = lax.optimization_barrier((first, second))
    first_came, second_came = spread(first, "z"), spread(second, "x")
    late = jnp.concatenate(
        [add(*(part[KVR:] for part in first_came)), add(*(part[KVR:] for part in second_came))], axis=0
    )
    late_came = collect(late, "dp")
    input_grad = call(
        tail_kernel, "tail", shape(D, TOK), None,
        (*first_came, *second_came, *turn, x, norm_gain, key_cols, value_cols, dact, dmid),
    )
    late = add(*late_came)
    late, input_grad = lax.optimization_barrier((late, input_grad))
    late = jnp.stack(collect(late, "z"))
    late_came = collect(late, "x")
    input_grad, result = zigzag(input_grad), zigzag(result)
    early = early_finish(scalars, early.reshape(16, 2, 4, 2, SHARD, 128))
    late_came, input_grad, result, early = lax.optimization_barrier((late_came, input_grad, result, early))
    late = jnp.stack(late_came)
    late = call(
        late_finish_kernel, "late_finish",
        (shape(D, D, dtype=F32), shape(KVW, D, dtype=F32), shape(KVW, D, dtype=F32)) + (shape(D, dtype=F32),) * 2,
        scalars, (late, swap(late)), (pltpu.VMEM((32 * LATE_SHARD, 128), BF),),
    )
    return (
        result.T[None],
        input_grad.T[None],
        late[3],
        late[0],
        late[1].T,
        late[2].T,
        early[3],
        late[4],
        early[0],
        early[1],
        early[2].T,
    )


def solution(mesh):
    inner = Mesh(mesh.devices.reshape(4, 4, 4, 2), ALL)
    row = P("dp", SEQ, None)
    flat = P("dp", SEQ)
    return jax.shard_map(
        body,
        mesh=inner,
        in_specs=(row, flat, flat) + (P(),) * 9 + (row,),
        out_specs=(row, row) + (P(),) * 9,
        check_vma=False,
    )
```
